32 devices in a mesh: seq: 16 (over z, y, x), tp: 2 (over core).
Axes of the slice: x: 2, y: 2, z: 4, core: 2. Of those that a mesh axis runs over, the one named last changes fastest.
Arguments:
- tokens: bfloat16 [16384, 1024], P(('seq', 'tp')), may hold values from -6 to 6
- norm_gain: float32 [1024], replicated, may hold values from 0.5 to 1.5
- query_weight: bfloat16 [1024, 1024], P(None, 'tp'), may hold values from -0.1875 to 0.1875
- key_weight: bfloat16 [1024, 1024], P(None, 'tp'), may hold values from -0.1875 to 0.1875
- value_weight: bfloat16 [1024, 1024], P(None, 'tp'), may hold values from -0.1875 to 0.1875
- forget_weight: bfloat16 [1024, 256], P(None, 'tp'), may hold values from -0.09375 to 0.09375
- forget_bias: float32 [256], P('tp'), may hold values from 1 to 10
- head_gain: float32 [1024], P('tp'), may hold values from 0.5 to 1.5
- out_weight: bfloat16 [1024, 1024], P('tp'), may hold values from -0.1875 to 0.1875
- feed_gain: float32 [1024], replicated, may hold values from 0.5 to 1.5
- gate_weight: bfloat16 [1024, 2816], P(None, 'tp'), may hold values from -0.1875 to 0.1875
- up_weight: bfloat16 [1024, 2816], P(None, 'tp'), may hold values from -0.1875 to 0.1875
- down_weight: bfloat16 [2816, 1024], P('tp'), may hold values from -0.109375 to 0.109375
- lengths: int32 [4], replicated, may hold values from 1 to 15424, as said below
- cotangent: bfloat16 [16384, 1024], P(('seq', 'tp')), may hold values from -6 to 6
Outputs:
- block_out: bfloat16 [16384, 1024], P(('seq', 'tp'))
- tokens_grad: bfloat16 [16384, 1024], P(('seq', 'tp'))
- norm_gain_grad: float32 [1024], replicated
- query_weight_grad: float32 [1024, 1024], P(None, 'tp')
- key_weight_grad: float32 [1024, 1024], P(None, 'tp')
- value_weight_grad: float32 [1024, 1024], P(None, 'tp')
- forget_weight_grad: float32 [1024, 256], P(None, 'tp')
- forget_bias_grad: float32 [256], P('tp')
- head_gain_grad: float32 [1024], P('tp')
- out_weight_grad: float32 [1024, 1024], P('tp')
- feed_gain_grad: float32 [1024], replicated
- gate_weight_grad: float32 [1024, 2816], P(None, 'tp')
- up_weight_grad: float32 [1024, 2816], P(None, 'tp')
- down_weight_grad: float32 [2816, 1024], P('tp')
The draws below stay inside these ranges and needn't reach their ends.
Inputs may be any that keep to these rules, and one draw needn't show every extreme that they name: `lengths`: every length lies between 64 * (k - 1) + 1 and 64 * k for its bucket count k; the buckets of all 4 sequences fill all 16384 positions exactly; exactly one length is 15424, the others take 1024 - 64 positions of buckets together.
All inputs are finite; a program needn't handle non-finite values.
Results may differ from the reference program's by a relative error of at most 0.023.
Values may be sent and summed in bfloat16 or wider, within the bound.
A program may use at most 192 MiB of HBM per device.

```python
import jax
import jax.numpy as jnp
from jax import lax

D = 1024
HEADS = 4
DH = 256
SLOTS = 64
FF = 2816
TOK_DEV = 1024
BLK = 64
BUCKET = 64
TOKENS = 16384
NSEQ = 4


def draw_lengths(key, part):
    key = jax.random.fold_in(key, 17)
    pick_key, pad_key, move_key = jax.random.split(key, 3)
    others = NSEQ - 1
    other_buckets = TOK_DEV // BUCKET - 1
    longest_buckets = TOKENS // BUCKET - other_buckets
    spare = other_buckets - others
    order = jnp.arange(others, dtype=jnp.int32)
    extra = (spare // others + (order < spare % others).astype(jnp.int32)).astype(jnp.int32)

    def move(step, extra_now):
        step_key = jax.random.fold_in(move_key, step)
        donor_key, taker_key, amount_key = jax.random.split(step_key, 3)
        donor = jax.random.randint(donor_key, (), 0, others)
        taker = jax.random.randint(taker_key, (), 0, others)
        amount = jax.random.randint(amount_key, (), 0, extra_now[donor] + 1)
        amount = jnp.where(donor == taker, 0, amount).astype(jnp.int32)
        return extra_now.at[donor].add(-amount).at[taker].add(amount)
    extra = lax.fori_loop(0, 4 * NSEQ, move, extra)
    longest = jax.random.randint(pick_key, (), 0, NSEQ)
    place = jnp.arange(NSEQ, dtype=jnp.int32)
    source = jnp.clip(place - (place > longest).astype(jnp.int32), 0, others - 1)
    counts = jnp.where(place == longest, longest_buckets, 1 + extra[source])
    pads = jax.random.randint(pad_key, (NSEQ,), 0, BUCKET)
    pads = jnp.where(place == longest, 0, pads)
    return (counts * BUCKET - pads).astype(jnp.int32)


def steps_of(rng, dims, shards, smallest, largest):
    factor_of, own = 1.0, jax.random.fold_in(rng, 6)
    for dim, blocks in shards:
        draws = jnp.exp(jax.random.uniform(jax.random.fold_in(own, dim), (blocks,), jnp.float32, smallest / len(shards), largest / len(shards)))
        factor_of = factor_of * jnp.repeat(draws, dims[dim] // blocks).reshape([-1 if axis == dim else 1 for axis in range(len(dims))])
    return factor_of


def scatter_about(stream_key, shape, scale, reach, shards=(), kind=jnp.bfloat16):
    drawn = scale * jax.random.normal(stream_key, shape, jnp.float32)
    if shards:
        drawn = drawn * steps_of(stream_key, shape, shards, -0.22, 0.18)
    return jnp.clip(drawn, -reach, reach).astype(kind)


def setup_inputs(seed: int = 0) -> dict:
    key_of = jax.random.split(jax.random.key(seed), 16)
    tokens = scatter_about(key_of[0], (TOKENS, D), 1.0, 6.0, ((0, 32),))
    norm_gain = jnp.clip(1.0 + 0.1 * jax.random.normal(key_of[1], (D,), jnp.float32), 0.5, 1.5)
    query_weight = scatter_about(key_of[2], (D, D), D ** -0.5, 0.1875, ((1, 2),))
    key_weight = scatter_about(key_of[3], (D, D), D ** -0.5, 0.1875, ((1, 2),))
    value_weight = scatter_about(key_of[4], (D, D), D ** -0.5, 0.1875, ((1, 2),))
    forget_weight = scatter_about(key_of[5], (D, HEADS * SLOTS), (4 * D) ** -0.5, 0.09375, ((1, 2),))
    forget_bias = jnp.clip(1.0 + 9.0 * jax.random.uniform(key_of[6], (HEADS * SLOTS,), jnp.float32) ** steps_of(key_of[6], (HEADS * SLOTS,), ((0, 2),), -0.2, 0.2), 1.0, 10.0)
    head_gain = jnp.clip(1.0 + 0.1 * jax.random.normal(key_of[7], (D,), jnp.float32), 0.5, 1.5)
    out_weight = scatter_about(key_of[8], (D, D), D ** -0.5, 0.1875, ((0, 2),))
    feed_gain = jnp.clip(1.0 + 0.1 * jax.random.normal(key_of[9], (D,), jnp.float32), 0.5, 1.5)
    gate_weight = scatter_about(key_of[10], (D, FF), D ** -0.5, 0.1875, ((1, 2),))
    up_weight = scatter_about(key_of[11], (D, FF), D ** -0.5, 0.1875, ((1, 2),))
    down_weight = scatter_about(key_of[12], (FF, D), FF ** -0.5, 0.109375, ((0, 2),))
    lengths = draw_lengths(jax.random.fold_in(key_of[15], 71), 0)
    cotangent = scatter_about(key_of[14], (TOKENS, D), 1.0, 6.0, ((0, 32),))
    return {"tokens": tokens, "norm_gain": norm_gain, "query_weight": query_weight, "key_weight": key_weight, "value_weight": value_weight, "forget_weight": forget_weight, "forget_bias": forget_bias, "head_gain": head_gain, "out_weight": out_weight, "feed_gain": feed_gain, "gate_weight": gate_weight, "up_weight": up_weight, "down_weight": down_weight, "lengths": lengths, "cotangent": cotangent}


EPS = 1e-06
NORMALIZER = 8.0
HIGH_PRECISION = lax.Precision.HIGHEST

@jax.custom_vjp
def low(v):
    return lax.optimization_barrier(v.astype(jnp.bfloat16)).astype(jnp.float32)

@jax.custom_vjp
def low_back(v):
    return v

def low_keep(v):
    return (low(v), None)

def low_pass(kept, grad):
    return (grad,)

def back_keep(v):
    return (v, None)

def back_low(kept, grad):
    return (low(grad),)
low.defvjp(low_keep, low_pass)
low_back.defvjp(back_keep, back_low)

def rms_norm(value, gain):
    return value * lax.rsqrt(lax.optimization_barrier(jnp.mean(value * value, axis=-1, keepdims=True)) + EPS) * gain

def token_marks(lengths, positions):
    buckets = (lengths + BUCKET - 1) // BUCKET
    spans = (buckets * BUCKET).astype(jnp.int32)
    starts = (jnp.cumsum(spans) - spans).astype(jnp.int32)
    member = (positions[:, None] >= starts[None, :]).astype(jnp.int32)
    segment = (lax.optimization_barrier(jnp.sum(member, axis=1)) - 1).astype(jnp.int32)
    picked = (segment[:, None] == jnp.arange(lengths.shape[0], dtype=jnp.int32)[None, :]).astype(jnp.int32)
    begin = lax.optimization_barrier(jnp.sum(picked * starts[None, :], axis=1)).astype(jnp.int32)
    length = lax.optimization_barrier(jnp.sum(picked * lengths[None, :], axis=1)).astype(jnp.int32)
    offset = positions - begin
    return (segment, offset < length, offset == 0)

def slot_weights(gate_log, keep, reset):
    return jnp.where(reset[:, None, None], 1.0, 1.0 - jnp.exp(gate_log)) * keep[:, None, None]

def mixer_block(carry, block):
    key_slot_state, value_slot_state, last_seg = carry
    query_rows, key_rows, value_rows, gate_log, weight, segment = block
    width = query_rows.shape[-1]
    cum = jnp.cumsum(gate_log, axis=0)
    order = jnp.arange(segment.shape[0], dtype=jnp.int32)
    same = (segment[:, None] == segment[None, :]) & (order[:, None] >= order[None, :])
    mask = same[:, :, None, None]
    decay = jnp.where(mask, jnp.exp(jnp.where(mask, cum[:, None] - cum[None, :], 0.0)), 0.0)
    mixed = decay * weight[None]
    decay_factor = jnp.where((segment == last_seg)[:, None, None], jnp.exp(cum), 0.0)
    scores = jnp.einsum('thd,jhd->htj', query_rows, key_rows, precision=HIGH_PRECISION)
    inner = jnp.einsum('htj,tjhm->thm', scores, mixed, precision=HIGH_PRECISION)
    outer_product = decay_factor * jnp.einsum('zuw,ulw->zul', query_rows, key_slot_state, precision=HIGH_PRECISION)
    slot_probabilities = jax.nn.softmax((inner + outer_product) * width ** (-0.5), axis=-1)
    reading = jnp.einsum('thm,tjhm->htj', slot_probabilities, mixed, precision=HIGH_PRECISION)
    output_rows = jnp.einsum('isr,srw->isw', slot_probabilities * decay_factor, value_slot_state, precision=HIGH_PRECISION)
    output_rows = output_rows + jnp.einsum('htj,jhd->thd', reading, value_rows, precision=HIGH_PRECISION)
    trailing_part = mixed[-1]
    key_following = decay_factor[-1][:, :, None] * key_slot_state + jnp.einsum('lqo,lqi->qoi', trailing_part, key_rows, precision=HIGH_PRECISION)
    value_following = decay_factor[-1][:, :, None] * value_slot_state + jnp.einsum('lqo,lqi->qoi', trailing_part, value_rows, precision=HIGH_PRECISION)
    return ((key_following, value_following, segment[-1]), output_rows)

def run_mixer(query_rows, key_rows, value_rows, gate_log, key_init, value_init, segment, keep, reset, last_seg):
    weight = slot_weights(gate_log, keep, reset)
    count = query_rows.shape[0] // BLK

    def split(array):
        return array.reshape((count, BLK) + array.shape[1:])
    carry = (key_init, value_init, last_seg)
    blocks = (split(query_rows), split(key_rows), split(value_rows), split(gate_log), split(weight), split(segment))
    _, output_rows = lax.scan(jax.checkpoint(mixer_block), carry, blocks)
    return output_rows.reshape(query_rows.shape)

def reference(tokens, norm_gain, query_weight, key_weight, value_weight, forget_weight, forget_bias, head_gain, out_weight, feed_gain, gate_weight, up_weight, down_weight, lengths, cotangent):
    count = tokens.shape[0]
    positions = jnp.arange(count, dtype=jnp.int32)
    segment, valid, reset = token_marks(lengths, positions)
    keep = valid.astype(jnp.float32)

    def forward(inputs, gain_one, weight_q, weight_k, weight_v, weight_f, bias_f, gain_head, weight_o, gain_two, weight_g, weight_u, weight_d):
        normed_in = low(rms_norm(inputs, gain_one))
        q_raw = low_back(jnp.dot(normed_in, weight_q, precision=HIGH_PRECISION))
        k_raw = low_back(jnp.dot(normed_in, weight_k, precision=HIGH_PRECISION))
        v_raw = low_back(jnp.dot(normed_in, weight_v, precision=HIGH_PRECISION))
        z_raw = low_back(jnp.dot(normed_in, weight_f, precision=HIGH_PRECISION) + bias_f)
        query_rows = low(jax.nn.silu(q_raw)).reshape(count, HEADS, DH)
        key_rows = low(jax.nn.silu(k_raw)).reshape(count, HEADS, DH)
        value_rows = low(v_raw).reshape(count, HEADS, DH)
        gate_log = jnp.where(valid[:, None], jax.nn.log_sigmoid(z_raw) / NORMALIZER, 0.0).reshape(count, HEADS, SLOTS)
        zeros = jnp.zeros((HEADS, SLOTS, DH), jnp.float32)
        mixed = run_mixer(query_rows, key_rows, value_rows, gate_log, zeros, zeros, segment, keep, reset, jnp.int32(-1))
        normed = (rms_norm(mixed, gain_head.reshape(HEADS, DH)) * keep[:, None, None]).reshape(count, HEADS * DH)
        attn = low_back(jnp.dot(low(normed), weight_o, precision=HIGH_PRECISION))
        resid = inputs + attn
        hidden_in = low(rms_norm(resid, gain_two))
        gate = low_back(jnp.dot(hidden_in, weight_g, precision=HIGH_PRECISION))
        upper = low_back(jnp.dot(hidden_in, weight_u, precision=HIGH_PRECISION))
        act = low(jax.nn.silu(gate) * upper)
        return resid + low_back(jnp.dot(act, weight_d, precision=HIGH_PRECISION))
    result, backward = jax.vjp(forward, tokens.astype(jnp.float32), norm_gain.astype(jnp.float32), query_weight.astype(jnp.float32), key_weight.astype(jnp.float32), value_weight.astype(jnp.float32), forget_weight.astype(jnp.float32), forget_bias.astype(jnp.float32), head_gain.astype(jnp.float32), out_weight.astype(jnp.float32), feed_gain.astype(jnp.float32), gate_weight.astype(jnp.float32), up_weight.astype(jnp.float32), down_weight.astype(jnp.float32))
    grads = backward(cotangent.astype(jnp.float32))
    return (result.astype(jnp.bfloat16), grads[0].astype(jnp.bfloat16), grads[1], grads[2], grads[3], grads[4], grads[5], grads[6], grads[7], grads[8], grads[9], grads[10], grads[11], grads[12])
```

```python
import functools

import jax
import jax.numpy as jnp
import numpy as np
from jax import lax
from jax.experimental import pallas as pl
from jax.experimental.pallas import tpu as pltpu
from jax.sharding import PartitionSpec as P

DH = 256
SLOTS = 64
BUCKET = 64
CH = 128
BASE = 8
HALVES = (64, 32, 16, 8)
RESET_LOG = -16384.0
LIFT = 2.0**20
SCALE = DH**-0.5

EPS = 1e-06
NORMALIZER = 8.0

BF = jnp.bfloat16
F32 = jnp.float32
VMEM_LIMIT = 56 * 1024 * 1024


def dot(a, b):
    return lax.dot_general(a, b, (((1,), (0,)), ((), ())), preferred_element_type=F32)


def nt(a, b):
    return lax.dot_general(a, b, (((1,), (1,)), ((), ())), preferred_element_type=F32)


def tn(a, b):
    return lax.dot_general(a, b, (((0,), (0,)), ((), ())), preferred_element_type=F32)


def tables():
    t, u = np.arange(CH)[:, None], np.arange(CH)[None, :]
    sums, pairs = [u <= t, u > t], []
    for half in HALVES:
        mid = t // (2 * half) * (2 * half) + half
        sums.append(np.where(t >= mid, (u >= mid) & (u <= t), (u > t) & (u < mid)))
        pairs.append(
            (t // (2 * half) == u // (2 * half)) & (t % (2 * half) >= half) & (u % (2 * half) < half)
        )
    ref = t // BASE * BASE + BASE // 2 - 1
    sums.append(((u > ref) & (u <= t)).astype(int) - ((u > t) & (u <= ref)).astype(int))
    pairs.append((t // BASE == u // BASE) & (u <= t))
    stacked = np.concatenate([s.astype(np.float32) for s in sums], 0)
    back = np.concatenate([(u >= t), (u >= t) & ((t >= BUCKET) | (u < BUCKET))], 0).astype(np.float32)
    return (
        np.concatenate([stacked] * 3, 1),
        np.stack(pairs).astype(np.float32),
        np.stack([p.T for p in pairs]).astype(np.float32),
        np.concatenate([back] * 3, 1),
    )


def split3(x):
    high = x.astype(BF)
    rest = x - high.astype(F32)
    middle = rest.astype(BF)
    low = (rest - middle.astype(F32)).astype(BF)
    return jnp.concatenate([high, middle, low], 0)


def decays(gate, weight, sums_ref):
    sums = dot(sums_ref[...], split3(gate))
    part = [sums[i * CH : (i + 1) * CH] for i in range(3 + len(HALVES))]
    first, last = jnp.exp(part[0]), jnp.exp(part[1])
    rows = [jnp.exp(p) for p in part[2:-1]]
    cols = [r * weight for r in rows]
    slopes = list(rows)
    rows.append(jnp.exp(part[-1]) * LIFT)
    slopes.append(jnp.exp(-part[-1]) * (1 / LIFT))
    cols.append(slopes[-1] * weight)
    return first, last, rows, cols, slopes


def halves(x):
    left = lax.broadcasted_iota(jnp.int32, x.shape, 1) < SLOTS
    zero = jnp.zeros_like(x)
    return jnp.where(left, x, zero), jnp.where(left, zero, x)


def head(x, h):
    return x[:, h * DH : (h + 1) * DH]


def slots(x, h):
    return x[:, h * SLOTS : (h + 1) * SLOTS]


def state(x, h):
    return x[h * SLOTS : (h + 1) * SLOTS]


def through(pairwise, rows, cols, pairs_ref):
    total = None
    for i in range(len(rows)):
        keep = pairs_ref[i] != 0
        left = jnp.concatenate([jnp.where(keep, p, 0.0).astype(BF) for p in pairwise], 1)
        right = jnp.concatenate(halves(cols[i].astype(BF)), 0)
        term = rows[i] * dot(left, right)
        total = term if total is None else total + term
    return total


def back_through(values, rows, cols, pairs_ref):
    totals = None
    for i in range(len(rows)):
        keep = pairs_ref[i] != 0
        stack = [part for v in values for part in halves((v * rows[i]).astype(BF))]
        out = nt(jnp.concatenate(stack, 0), cols[i].astype(BF))
        terms = [jnp.where(keep, out[n * CH : (n + 1) * CH], 0.0) for n in range(len(stack))]
        totals = terms if totals is None else [a + b for a, b in zip(totals, terms)]
    return totals


def softmax2(logits):
    out = []
    for h in range(2):
        x = slots(logits, h) * SCALE
        e = jnp.exp(x - jnp.max(x, axis=-1, keepdims=True))
        out.append(e / jnp.sum(e, axis=-1, keepdims=True))
    return jnp.concatenate(out, 1)


def fade_of(gate):
    return jnp.exp(jnp.sum(gate.T, axis=1, keepdims=True))


def run_part(trail, keys, values):
    return jnp.concatenate(
        [
            jnp.concatenate([tn(slots(trail, h), head(keys, h)), tn(slots(trail, h), head(values, h))], 1)
            for h in range(2)
        ],
        0,
    )


def project_kernel(
    tp_ref, own_ref, other_ref, gain_ref, wq_ref, wk_ref, wv_ref, wf_ref, bias_ref, code_ref, sums_ref,
    xn_ref, q_ref, k_ref, v_ref, dsq_ref, dsk_ref, gate_ref, weight_ref, dz_ref, kv_ref, fade_ref,
):
    step = pl.program_id(0)
    mine = step // (pl.num_programs(0) // 2) == tp_ref[0]
    x = jnp.where(mine, own_ref[...], other_ref[...]).astype(F32)
    mean = jnp.mean(x * x, axis=-1, keepdims=True)
    xn = (x * lax.rsqrt(mean + EPS) * gain_ref[...]).astype(BF)
    xn_ref[...] = xn

    def silu(raw):
        s = 1.0 / (1.0 + jnp.exp(-raw))
        return (raw * s).astype(BF), (s * (1.0 + raw * (1.0 - s))).astype(BF)

    q, dsq = silu(dot(xn, wq_ref[...]))
    q_ref[...], dsq_ref[...] = q, dsq
    k, dsk = silu(dot(xn, wk_ref[...]))
    k_ref[...], dsk_ref[...] = k, dsk
    v = dot(xn, wv_ref[...]).astype(BF)
    v_ref[...] = v
    z = dot(xn, wf_ref[...]) + bias_ref[...]
    code = code_ref[...]
    valid, reset = code > 0.5, code > 1.5
    soft = jnp.log(1.0 + jnp.exp(-jnp.abs(z)))
    log_sig = jnp.minimum(z, 0.0) - soft
    gate = jnp.where(valid, log_sig * (1.0 / NORMALIZER), 0.0)
    weight = jnp.where(reset, 1.0, 1.0 - jnp.exp(gate))
    gate = jnp.where(reset, RESET_LOG, gate)
    down = jnp.exp(-jnp.abs(z))
    sig_neg = jnp.where(z > 0, down, 1.0) / (1.0 + down)
    gate_ref[...] = gate
    weight_ref[...] = weight
    dz_ref[...] = jnp.where(valid & (code < 1.5), sig_neg * (1.0 / NORMALIZER), 0.0)
    last = jnp.exp(dot(sums_ref[CH : 2 * CH], split3(gate)))
    part = run_part((last * weight).astype(BF), k, v)
    fade = fade_of(gate)

    @pl.when(step == 0)
    def _():
        kv_ref[...] = part
        fade_ref[...] = jnp.broadcast_to(fade, fade_ref.shape)

    @pl.when(step > 0)
    def _():
        kv_ref[...] = fade * kv_ref[...] + part
        fade_ref[...] = fade_ref[...] * fade


def mix_kernel(
    tp_ref, q_ref, k_ref, v_ref, gate_ref, weight_ref, code_ref, start_ref, sums_ref, pairs_ref, gain_ref, wo_ref,
    logit_ref, kvs_ref, mixed_ref, normed_ref, own_ref, other_ref, kv_ref,
):
    step = pl.program_id(0)

    @pl.when(step == 0)
    def _():
        kv_ref[...] = start_ref[...]

    q, k, v = q_ref[...], k_ref[...], v_ref[...]
    gate, weight = gate_ref[...], weight_ref[...]
    first, last, rows, cols, _ = decays(gate, weight, sums_ref)
    kv = kv_ref[...]
    kvs_ref[0] = kv
    low = kv.astype(BF)
    scores = [nt(head(q, h), head(k, h)) for h in range(2)]
    outer = jnp.concatenate([nt(head(q, h), state(low, h)[:, :DH]) for h in range(2)], 1)
    logits = first * outer + through(scores, rows, cols, pairs_ref)
    logit_ref[...] = logits
    probs = softmax2(logits)
    reading = back_through([probs], rows, cols, pairs_ref)
    spread = (probs * first).astype(BF)
    kv_ref[...] = fade_of(gate) * kv + run_part((last * weight).astype(BF), k, v)
    code = code_ref[:, :1]
    normed = []
    for h in range(2):
        mixed = dot(slots(spread, h), state(low, h)[:, DH:]) + dot(reading[h].astype(BF), head(v, h))
        mixed_ref[:, h * DH : (h + 1) * DH] = mixed
        r = lax.rsqrt(jnp.mean(mixed * mixed, axis=-1, keepdims=True) + EPS)
        r = jnp.where(code > 0.5, r, 0.0)
        normed.append((mixed * r * gain_ref[:, h * DH : (h + 1) * DH]).astype(BF))
    normed = jnp.concatenate(normed, 1)
    normed_ref[...] = normed
    attn = dot(normed, wo_ref[...]).astype(BF)
    mine = step // (pl.num_programs(0) // 2) == tp_ref[0]

    @pl.when(mine)
    def _():
        own_ref[...] = attn

    @pl.when(jnp.logical_not(mine))
    def _():
        other_ref[...] = attn


def score_kernel(
    tp_ref, da_own_ref, da_other_ref, wo_ref, mixed_ref, code_ref, gain_ref, q_ref, k_ref, v_ref, gate_ref, weight_ref,
    logit_ref, kvs_ref, sums_ref, pairs_ref,
    da_ref, dmix_ref, dl_ref, y_ref, gain_grad_ref, dkv_ref, reach_ref,
):
    step = pl.program_id(0)
    mine = step // (pl.num_programs(0) // 2) == tp_ref[0]
    da = jnp.where(mine, da_own_ref[...], da_other_ref[...])
    da_ref[...] = da
    dnormed = nt(da, wo_ref[...])
    dnormed = jnp.where(code_ref[:, :1] > 0.5, dnormed, 0.0)
    dmix, gain_grad = [], []
    for h in range(2):
        mixed = mixed_ref[:, h * DH : (h + 1) * DH]
        r = lax.rsqrt(jnp.mean(mixed * mixed, axis=-1, keepdims=True) + EPS)
        n = mixed * r
        d = head(dnormed, h)
        u = d * gain_ref[:, h * DH : (h + 1) * DH]
        gain_grad.append(jnp.sum(d * n, axis=0, keepdims=True))
        dmix.append((r * (u - n * jnp.mean(u * n, axis=-1, keepdims=True))).astype(BF))
    gain_grad = jnp.concatenate(gain_grad, 1)
    dmix = jnp.concatenate(dmix, 1)
    dmix_ref[...] = dmix
    q, k, v = q_ref[...], k_ref[...], v_ref[...]
    gate, weight = gate_ref[...], weight_ref[...]
    first, _, rows, cols, _ = decays(gate, weight, sums_ref)
    logits = logit_ref[...]
    probs = softmax2(logits)
    low = kvs_ref[0].astype(BF)
    reads = [nt(head(dmix, h), head(v, h)) for h in range(2)]
    outer = jnp.concatenate([nt(head(dmix, h), state(low, h)[:, DH:]) for h in range(2)], 1)
    dprobs = first * outer + through(reads, rows, cols, pairs_ref)
    weighted = probs * dprobs
    sums = [
        jnp.broadcast_to(jnp.sum(slots(weighted, h), axis=-1, keepdims=True), (CH, SLOTS)) for h in range(2)
    ]
    dl = (weighted - probs * jnp.concatenate(sums, 1)) * SCALE
    dl_ref[...] = dl
    y_ref[...] = dl * logits + weighted
    part = state_grads(dl, probs, first, q, dmix)
    fade = fade_of(gate)

    @pl.when(step == 0)
    def _():
        gain_grad_ref[...] = gain_grad
        dkv_ref[...] = part
        reach_ref[...] = jnp.broadcast_to(fade, reach_ref.shape)

    @pl.when(step > 0)
    def _():
        gain_grad_ref[...] += gain_grad
        reach = reach_ref[...]
        dkv_ref[...] += jnp.concatenate([reach] * (dkv_ref.shape[1] // reach.shape[1]), 1) * part
        reach_ref[...] = reach * fade


def state_grads(dl, probs, first, q, dmix):
    a, b = (dl * first).astype(BF), (probs * first).astype(BF)
    return jnp.concatenate(
        [jnp.concatenate([tn(slots(a, h), head(q, h)), tn(slots(b, h), head(dmix, h))], 1) for h in range(2)], 0
    )


def grad_kernel(
    tp_ref, q_ref, k_ref, v_ref, dsq_ref, dsk_ref, gate_ref, weight_ref, dz_ref, logit_ref, kvs_ref, dmix_ref, dl_ref, y_ref,
    end_ref, flow_ref, sums_ref, pairs_ref, flipped_ref, back_ref, wq_ref, wk_ref, wv_ref, wf_ref,
    dq_ref, dk_ref, dv_ref, df_ref, bias_ref, own_ref, other_ref, dkv_ref, carry_ref,
):
    step = pl.program_id(0)

    @pl.when(step == 0)
    def _():
        dkv_ref[...] = end_ref[...]
        carry_ref[...] = flow_ref[...]

    q, k, v, dmix = q_ref[...], k_ref[...], v_ref[...], dmix_ref[...]
    gate, weight = gate_ref[...], weight_ref[...]
    dl = dl_ref[...]
    first, last, rows, cols, slopes = decays(gate, weight, sums_ref)
    probs = softmax2(logit_ref[...])
    kv, dkv = kvs_ref[0], dkv_ref[...]
    low, dlow = kv.astype(BF), dkv.astype(BF)
    r0, r1, s0, s1 = back_through([probs, dl], rows, cols, pairs_ref)
    turned = [
        nt(head(a, h), head(b, h)) for h in range(2) for a, b in ((k, q), (v, dmix))
    ]
    dw = last * jnp.concatenate(
        [nt(jnp.concatenate([head(k, h), head(v, h)], 1), state(dlow, h)) for h in range(2)], 1
    )
    for i in range(len(rows)):
        keep = flipped_ref[i] != 0
        left = jnp.concatenate([jnp.where(keep, x, 0.0).astype(BF) for x in turned], 1)
        a, b = halves((dl * rows[i]).astype(BF)), halves((probs * rows[i]).astype(BF))
        dw = dw + slopes[i] * dot(left, jnp.concatenate([a[0], b[0], a[1], b[1]], 0))
    trail = (last * weight).astype(BF)
    spread = (dl * first).astype(BF)
    reading, dscore = [r0.astype(BF), r1.astype(BF)], [s0.astype(BF), s1.astype(BF)]
    dq, dk, dv = [], [], []
    for h in range(2):
        dq.append(dot(dscore[h], head(k, h)) + dot(slots(spread, h), state(low, h)[:, :DH]))
        dk.append(tn(dscore[h], head(q, h)) + dot(slots(trail, h), state(dlow, h)[:, :DH]))
        dv.append(tn(reading[h], head(dmix, h)) + dot(slots(trail, h), state(dlow, h)[:, DH:]))
    dq = (jnp.concatenate(dq, 1) * dsq_ref[...].astype(F32)).astype(BF)
    dk = (jnp.concatenate(dk, 1) * dsk_ref[...].astype(F32)).astype(BF)
    dv = jnp.concatenate(dv, 1).astype(BF)
    both = dot(back_ref[...], split3(y_ref[...] - weight * dw))
    cut = gate[BUCKET : BUCKET + 1] < 0.5 * RESET_LOG
    late = lax.broadcasted_iota(jnp.int32, gate.shape, 0) >= BUCKET
    flow = jnp.where(cut, both[CH:], both[:CH]) + jnp.where(cut & jnp.logical_not(late), 0.0, carry_ref[...])
    df = ((flow - jnp.exp(gate) * dw) * dz_ref[...]).astype(BF)
    dq_ref[...], dk_ref[...], dv_ref[...], df_ref[...] = dq, dk, dv, df
    bias_part = jnp.sum(df.astype(F32), axis=0, keepdims=True)
    new = fade_of(gate) * dkv + state_grads(dl, probs, first, q, dmix)
    dkv_ref[...] = new
    carry_ref[...] = jnp.sum((kv * new).T, axis=0, keepdims=True)
    dx = (nt(dq, wq_ref[...]) + nt(dk, wk_ref[...]) + nt(dv, wv_ref[...]) + nt(df, wf_ref[...])).astype(BF)
    n = pl.num_programs(0)
    mine = (n - 1 - step) // (n // 2) == tp_ref[0]

    @pl.when(mine)
    def _():
        own_ref[...] = dx

    @pl.when(jnp.logical_not(mine))
    def _():
        other_ref[...] = dx

    @pl.when(step == 0)
    def _():
        bias_ref[...] = bias_part

    @pl.when(step > 0)
    def _():
        bias_ref[...] += bias_part


def call(kernel, count, ins, outs, scratch=(), tp=None, flops=0, moved=0, name=None):
    grid_spec = pltpu.PrefetchScalarGridSpec(
        num_scalar_prefetch=1,
        grid=(count,),
        in_specs=[pl.BlockSpec(block, index) for _, block, index in ins],
        out_specs=[pl.BlockSpec(block, index) for _, _, block, index in outs],
        scratch_shapes=list(scratch),
    )
    return pl.pallas_call(
        kernel,
        grid_spec=grid_spec,
        out_shape=[jax.ShapeDtypeStruct(shape, dtype) for shape, dtype, _, _ in outs],
        compiler_params=pltpu.CompilerParams(
            dimension_semantics=("arbitrary",), vmem_limit_bytes=VMEM_LIMIT
        ),
        cost_estimate=pl.CostEstimate(flops=flops, bytes_accessed=moved, transcendentals=0),
        name=name,
    )(tp, *[a for a, _, _ in ins])


def whole(array):
    return (array, array.shape, lambda i, tp: (0,) * array.ndim)


def rows_of(array):
    return (array, (CH, array.shape[1]), lambda i, tp: (i, 0))


def swap(x):
    return lax.ppermute(x, "tp", [(0, 1), (1, 0)])


def scan_states(total, fade, earlier):
    count = lax.axis_size("seq")
    index = lax.axis_index("seq")
    entering, entering_fade = jnp.zeros_like(total), jnp.ones_like(fade)
    for bit in range(count.bit_length() - 1):
        high = fade.astype(BF)
        sent = jnp.concatenate([total.astype(BF), high, (fade - high.astype(F32)).astype(BF)], 1)
        got = lax.ppermute(sent, "seq", [(i, i ^ (1 << bit)) for i in range(count)])
        width = total.shape[1]
        part = got[:, :width].astype(F32)
        part_fade = got[:, width : width + CH].astype(F32) + got[:, width + CH :].astype(F32)
        behind = ((index >> bit) & 1) == (1 if earlier else 0)
        entering = jnp.where(behind, entering_fade[:, :1] * part + entering, entering)
        entering_fade = jnp.where(behind, entering_fade * part_fade, entering_fade)
        total = jnp.where(behind, fade[:, :1] * part + total, part_fade[:, :1] * total + part)
        fade = fade * part_fade
    return entering


def token_code(lengths, positions):
    buckets = (lengths + BUCKET - 1) // BUCKET
    spans = buckets * BUCKET
    starts = jnp.cumsum(spans) - spans
    segment = jnp.sum((positions[:, None] >= starts[None, :]).astype(jnp.int32), axis=1) - 1
    picked = segment[:, None] == jnp.arange(lengths.shape[0], dtype=jnp.int32)[None, :]
    begin = jnp.sum(jnp.where(picked, starts[None, :], 0), axis=1)
    length = jnp.sum(jnp.where(picked, lengths[None, :], 0), axis=1)
    offset = positions - begin
    return jnp.where(offset == 0, 2.0, jnp.where(offset < length, 1.0, 0.0)).astype(F32)


def row_norm(x, gain):
    r = lax.rsqrt(jnp.mean(x * x, axis=-1, keepdims=True) + EPS)
    return x * r * gain


def row_norm_back(x, gain, grad):
    r = lax.rsqrt(jnp.mean(x * x, axis=-1, keepdims=True) + EPS)
    n = x * r
    u = grad * gain
    return r * (u - n * jnp.mean(u * n, axis=-1, keepdims=True)), jnp.sum(grad * n, axis=0)


def per_device(
    tokens, norm_gain, query_weight, key_weight, value_weight, forget_weight, forget_bias, head_gain,
    out_weight, feed_gain, gate_weight, up_weight, down_weight, lengths, cotangent,
):
    half, width = tokens.shape
    span = 2 * half
    count = span // CH
    cols = query_weight.shape[1]
    lanes = forget_weight.shape[1]
    tp = lax.axis_index("tp").astype(jnp.int32)[None]
    sums, pairs, flipped, back = tables()
    sums, back = jnp.asarray(sums, BF), jnp.asarray(back, BF)
    pairs, flipped = jnp.asarray(pairs), jnp.asarray(flipped)

    tokens_other, cot_other = swap(tokens), swap(cotangent)
    positions = lax.axis_index("seq") * span + jnp.arange(span, dtype=jnp.int32)
    code = jnp.broadcast_to(token_code(lengths, positions)[:, None], (span, lanes))
    half_map = lambda i, tp: (i % (count // 2), 0)
    own_map = lambda i, tp: (jnp.clip(i - tp[0] * (count // 2), 0, count // 2 - 1), 0)
    other_map = lambda i, tp: (jnp.clip(i - (1 - tp[0]) * (count // 2), 0, count // 2 - 1), 0)
    block = (CH, width)
    row = lambda n, d: ((span, n), d, (CH, n), lambda i, tp: (i, 0))
    fixed = lambda shape: (shape, F32, shape, lambda i, tp: (0,) * len(shape))

    xn, q, k, v, dsq, dsk, gate, weight, dzf, kv_run, fade_run = call(
        project_kernel, count,
        [(tokens, block, half_map), (tokens_other, block, half_map), whole(norm_gain[None]), whole(query_weight),
         whole(key_weight), whole(value_weight), whole(forget_weight), whole(forget_bias[None]), rows_of(code), whole(sums)],
        [row(width, BF)] + [row(cols, BF)] * 5 + [row(lanes, F32)] * 3 + [fixed((lanes, 2 * DH)), fixed((lanes, CH))],
        tp=tp, flops=2 * span * width * (3 * cols + lanes), moved=16 << 20, name="project",
    )

    kv_start = scan_states(kv_run, fade_run, True)

    logits, kvs, mixed, normed, attn_own, attn_other = call(
        mix_kernel, count,
        [rows_of(q), rows_of(k), rows_of(v), rows_of(gate), rows_of(weight), rows_of(code), whole(kv_start), whole(sums),
         whole(pairs), whole(head_gain[None]), whole(out_weight)],
        [row(lanes, F32), ((count, lanes, 2 * DH), F32, (1, lanes, 2 * DH), lambda i, tp: (i, 0, 0)), row(cols, F32),
         row(cols, BF), ((half, width), BF, block, own_map), ((half, width), BF, block, other_map)],
        scratch=[pltpu.VMEM((lanes, 2 * DH), F32)],
        tp=tp, flops=4 * span * width * cols, moved=16 << 20, name="mix",
    )

    own = tokens.astype(F32)
    resid = own + (attn_own.astype(F32) + swap(attn_other).astype(F32))
    hidden_own = row_norm(resid, feed_gain).astype(BF)
    hidden = jnp.concatenate([hidden_own, swap(hidden_own)], 0)
    cot = jnp.concatenate([cotangent, cot_other], 0)
    ff_gate = dot(hidden, gate_weight)
    ff_up = dot(hidden, up_weight)
    dact = nt(cot, down_weight)
    sig = jax.nn.sigmoid(ff_gate)
    act = (ff_gate * sig * ff_up).astype(BF)
    dgate = (dact * ff_up * sig * (1.0 + ff_gate * (1.0 - sig))).astype(BF)
    dup = (dact * ff_gate * sig).astype(BF)
    feed = dot(act, down_weight).astype(BF)
    dhidden = (nt(dgate, gate_weight) + nt(dup, up_weight)).astype(BF)
    down_grad = tn(act, cot).astype(BF)
    gate_grad = tn(hidden, dgate).astype(BF)
    up_grad = tn(hidden, dup).astype(BF)
    ff_grads = lax.psum((gate_grad, up_grad, down_grad), "seq")

    dhidden_own = dhidden[:half].astype(F32) + swap(dhidden[half:]).astype(F32)
    block_out = (resid + (feed[:half].astype(F32) + swap(feed[half:]).astype(F32))).astype(BF)
    dresid_norm, feed_gain_part = row_norm_back(resid, feed_gain, dhidden_own)
    dresid = cotangent.astype(F32) + dresid_norm
    da_own = dresid.astype(BF)
    da_other = swap(da_own)

    da, dmix, dl, y, head_gain_grad, dkv_run, reach = call(
        score_kernel, count,
        [(da_own, block, half_map), (da_other, block, half_map), whole(out_weight), rows_of(mixed), rows_of(code),
         whole(head_gain[None]), rows_of(q), rows_of(k), rows_of(v), rows_of(gate), rows_of(weight), rows_of(logits),
         (kvs, (1, lanes, 2 * DH), lambda i, tp: (i, 0, 0)), whole(sums), whole(pairs)],
        [row(width, BF), row(cols, BF), row(lanes, F32), row(lanes, F32), fixed((1, cols)), fixed((lanes, 2 * DH)),
         fixed((lanes, CH))],
        tp=tp, flops=4 * span * width * cols, moved=16 << 20, name="score",
    )

    dkv_end = scan_states(dkv_run, reach, False)
    out_grad = tn(normed, da).astype(BF)
    kv_end = fade_run[:, :1] * kv_start + kv_run
    flow = jnp.sum(kv_end * dkv_end, axis=1)[None]

    turn = lambda i: count - 1 - i
    rows_back = lambda a: (a, (CH, a.shape[1]), lambda i, tp: (turn(i), 0))
    row_back = lambda n, d: ((span, n), d, (CH, n), lambda i, tp: (turn(i), 0))
    dq, dk, dv, df, bias_grad, dx_own, dx_other = call(
        grad_kernel, count,
        [rows_back(a) for a in (q, k, v, dsq, dsk, gate, weight, dzf, logits)]
        + [(kvs, (1, lanes, 2 * DH), lambda i, tp: (turn(i), 0, 0)), rows_back(dmix), rows_back(dl), rows_back(y),
           whole(dkv_end), whole(flow), whole(sums), whole(pairs), whole(flipped), whole(back),
           whole(query_weight), whole(key_weight), whole(value_weight), whole(forget_weight)],
        [row_back(cols, BF)] * 3 + [row_back(lanes, BF), fixed((1, lanes)),
         ((half, width), BF, block, lambda i, tp: own_map(turn(i), tp)),
         ((half, width), BF, block, lambda i, tp: other_map(turn(i), tp))],
        scratch=[pltpu.VMEM((lanes, 2 * DH), F32), pltpu.VMEM((1, lanes), F32)],
        tp=tp, flops=2 * span * width * (3 * cols + lanes), moved=24 << 20, name="grad",
    )

    grads = [tn(xn, d).astype(BF) for d in (dq, dk, dv, df)]
    mixer_grads = lax.psum((*grads, out_grad), "seq")
    dx = dx_own.astype(F32) + swap(dx_other).astype(F32)
    own_grad, norm_gain_part = row_norm_back(own, norm_gain, dx)
    tokens_grad = (dresid + own_grad).astype(BF)
    norm_gain_grad, feed_gain_grad = lax.psum((norm_gain_part, feed_gain_part), ("seq", "tp"))
    bias_sum, head_sum = lax.psum((bias_grad[0], head_gain_grad[0]), "seq")
    wide = [g.astype(F32) for g in (*mixer_grads, *ff_grads)]
    return (
        block_out, tokens_grad, norm_gain_grad, wide[0], wide[1], wide[2], wide[3], bias_sum, head_sum, wide[4],
        feed_gain_grad, wide[5], wide[6], wide[7],
    )


def solution(mesh):
    rows, by_col, by_row = P(("seq", "tp"), None), P(None, "tp"), P("tp", None)
    return jax.shard_map(
        per_device,
        mesh=mesh,
        in_specs=(
            rows, P(), by_col, by_col, by_col, by_col, P("tp"), P("tp"), by_row, P(), by_col, by_col, by_row, P(), rows,
        ),
        out_specs=(
            rows, rows, P(), by_col, by_col, by_col, by_col, P("tp"), P("tp"), by_row, P(), by_col, by_col, by_row,
        ),
        check_vma=False,
    )
```

```python
import functools

import jax
import jax.numpy as jnp
import numpy as np
from jax import lax
from jax.experimental import pallas as pl
from jax.experimental.pallas import tpu as pltpu
from jax.sharding import PartitionSpec as P

DH = 256
SLOTS = 64
BUCKET = 64
CH = 128
BASE = 8
HALVES = (64, 32, 16, 8)
RESET_LOG = -16384.0
LIFT = 2.0**20
SCALE = DH**-0.5

EPS = 1e-06
NORMALIZER = 8.0

BF = jnp.bfloat16
F32 = jnp.float32
VMEM_LIMIT = 56 * 1024 * 1024
UNIT = 1024
MESH = pl.DeviceIdType.MESH


def dot(a, b):
    return lax.dot_general(a, b, (((1,), (0,)), ((), ())), preferred_element_type=F32)


def nt(a, b):
    return lax.dot_general(a, b, (((1,), (1,)), ((), ())), preferred_element_type=F32)


def tn(a, b):
    return lax.dot_general(a, b, (((0,), (0,)), ((), ())), preferred_element_type=F32)


def tables():
    t, u = np.arange(CH)[:, None], np.arange(CH)[None, :]
    sums, pairs = [u <= t, u > t], []
    for half in HALVES:
        mid = t // (2 * half) * (2 * half) + half
        sums.append(np.where(t >= mid, (u >= mid) & (u <= t), (u > t) & (u < mid)))
        pairs.append(
            (t // (2 * half) == u // (2 * half)) & (t % (2 * half) >= half) & (u % (2 * half) < half)
        )
    ref = t // BASE * BASE + BASE // 2 - 1
    sums.append(((u > ref) & (u <= t)).astype(int) - ((u > t) & (u <= ref)).astype(int))
    pairs.append((t // BASE == u // BASE) & (u <= t))
    stacked = np.concatenate([s.astype(np.float32) for s in sums], 0)
    back = np.concatenate([(u >= t), (u >= t) & ((t >= BUCKET) | (u < BUCKET))], 0).astype(np.float32)
    return (
        np.concatenate([stacked] * 3, 1),
        np.stack(pairs).astype(np.float32),
        np.stack([p.T for p in pairs]).astype(np.float32),
        np.concatenate([back] * 3, 1),
    )


def split3(x):
    high = x.astype(BF)
    rest = x - high.astype(F32)
    middle = rest.astype(BF)
    low = (rest - middle.astype(F32)).astype(BF)
    return jnp.concatenate([high, middle, low], 0)


def decays(gate, weight, sums_ref):
    sums = dot(sums_ref[...], split3(gate))
    part = [sums[i * CH : (i + 1) * CH] for i in range(3 + len(HALVES))]
    first, last = jnp.exp(part[0]), jnp.exp(part[1])
    rows = [jnp.exp(p) for p in part[2:-1]]
    cols = [r * weight for r in rows]
    slopes = list(rows)
    rows.append(jnp.exp(part[-1]) * LIFT)
    slopes.append(jnp.exp(-part[-1]) * (1 / LIFT))
    cols.append(slopes[-1] * weight)
    return first, last, rows, cols, slopes


def halves(x):
    left = lax.broadcasted_iota(jnp.int32, x.shape, 1) < SLOTS
    zero = jnp.zeros_like(x)
    return jnp.where(left, x, zero), jnp.where(left, zero, x)


def head(x, h):
    return x[:, h * DH : (h + 1) * DH]


def slots(x, h):
    return x[:, h * SLOTS : (h + 1) * SLOTS]


def state(x, h):
    return x[h * SLOTS : (h + 1) * SLOTS]


def through(pairwise, rows, cols, pairs_ref):
    total = None
    for i in range(len(rows)):
        keep = pairs_ref[i] != 0
        left = jnp.concatenate([jnp.where(keep, p, 0.0).astype(BF) for p in pairwise], 1)
        right = jnp.concatenate(halves(cols[i].astype(BF)), 0)
        term = rows[i] * dot(left, right)
        total = term if total is None else total + term
    return total


def back_through(values, rows, cols, pairs_ref):
    totals = None
    for i in range(len(rows)):
        keep = pairs_ref[i] != 0
        stack = [part for v in values for part in halves((v * rows[i]).astype(BF))]
        out = nt(jnp.concatenate(stack, 0), cols[i].astype(BF))
        terms = [jnp.where(keep, out[n * CH : (n + 1) * CH], 0.0) for n in range(len(stack))]
        totals = terms if totals is None else [a + b for a, b in zip(totals, terms)]
    return totals


def softmax2(logits):
    out = []
    for h in range(2):
        x = slots(logits, h) * SCALE
        e = jnp.exp(x - jnp.max(x, axis=-1, keepdims=True))
        out.append(e / jnp.sum(e, axis=-1, keepdims=True))
    return jnp.concatenate(out, 1)


def fade_of(gate):
    return jnp.exp(jnp.sum(gate.T, axis=1, keepdims=True))


def run_part(trail, keys, values):
    return jnp.concatenate(
        [
            jnp.concatenate([tn(slots(trail, h), head(keys, h)), tn(slots(trail, h), head(values, h))], 1)
            for h in range(2)
        ],
        0,
    )


def project_kernel(
    tp_ref, own_ref, other_ref, gain_ref, wq_ref, wk_ref, wv_ref, wf_ref, bias_ref, code_ref, sums_ref,
    xn_ref, q_ref, k_ref, v_ref, dsq_ref, dsk_ref, gate_ref, weight_ref, dz_ref, kv_ref, fade_ref,
):
    step = pl.program_id(0)
    mine = step // (pl.num_programs(0) // 2) == tp_ref[0]
    x = jnp.where(mine, own_ref[...], other_ref[...]).astype(F32)
    mean = jnp.mean(x * x, axis=-1, keepdims=True)
    xn = (x * lax.rsqrt(mean + EPS) * gain_ref[...]).astype(BF)
    xn_ref[...] = xn

    def silu(raw):
        s = 1.0 / (1.0 + jnp.exp(-raw))
        return (raw * s).astype(BF), (s * (1.0 + raw * (1.0 - s))).astype(BF)

    q, dsq = silu(dot(xn, wq_ref[...]))
    q_ref[...], dsq_ref[...] = q, dsq
    k, dsk = silu(dot(xn, wk_ref[...]))
    k_ref[...], dsk_ref[...] = k, dsk
    v = dot(xn, wv_ref[...]).astype(BF)
    v_ref[...] = v
    z = dot(xn, wf_ref[...]) + bias_ref[...]
    code = code_ref[...]
    valid, reset = code > 0.5, code > 1.5
    soft = jnp.log(1.0 + jnp.exp(-jnp.abs(z)))
    log_sig = jnp.minimum(z, 0.0) - soft
    gate = jnp.where(valid, log_sig * (1.0 / NORMALIZER), 0.0)
    weight = jnp.where(reset, 1.0, 1.0 - jnp.exp(gate))
    gate = jnp.where(reset, RESET_LOG, gate)
    down = jnp.exp(-jnp.abs(z))
    sig_neg = jnp.where(z > 0, down, 1.0) / (1.0 + down)
    gate_ref[...] = gate
    weight_ref[...] = weight
    dz_ref[...] = jnp.where(valid & (code < 1.5), sig_neg * (1.0 / NORMALIZER), 0.0)
    last = jnp.exp(dot(sums_ref[CH : 2 * CH], split3(gate)))
    part = run_part((last * weight).astype(BF), k, v)
    fade = fade_of(gate)

    @pl.when(step == 0)
    def _():
        kv_ref[...] = part
        fade_ref[...] = jnp.broadcast_to(fade, fade_ref.shape)

    @pl.when(step > 0)
    def _():
        kv_ref[...] = fade * kv_ref[...] + part
        fade_ref[...] = fade_ref[...] * fade


def mix_kernel(
    tp_ref, q_ref, k_ref, v_ref, gate_ref, weight_ref, code_ref, start_ref, sums_ref, pairs_ref, gain_ref, wo_ref,
    logit_ref, kvs_ref, mixed_ref, normed_ref, own_ref, other_ref, kv_ref,
):
    step = pl.program_id(0)

    @pl.when(step == 0)
    def _():
        kv_ref[...] = start_ref[...]

    q, k, v = q_ref[...], k_ref[...], v_ref[...]
    gate, weight = gate_ref[...], weight_ref[...]
    first, last, rows, cols, _ = decays(gate, weight, sums_ref)
    kv = kv_ref[...]
    kvs_ref[0] = kv
    low = kv.astype(BF)
    scores = [nt(head(q, h), head(k, h)) for h in range(2)]
    outer = jnp.concatenate([nt(head(q, h), state(low, h)[:, :DH]) for h in range(2)], 1)
    logits = first * outer + through(scores, rows, cols, pairs_ref)
    logit_ref[...] = logits
    probs = softmax2(logits)
    reading = back_through([probs], rows, cols, pairs_ref)
    spread = (probs * first).astype(BF)
    kv_ref[...] = fade_of(gate) * kv + run_part((last * weight).astype(BF), k, v)
    code = code_ref[:, :1]
    normed = []
    for h in range(2):
        mixed = dot(slots(spread, h), state(low, h)[:, DH:]) + dot(reading[h].astype(BF), head(v, h))
        mixed_ref[:, h * DH : (h + 1) * DH] = mixed
        r = lax.rsqrt(jnp.mean(mixed * mixed, axis=-1, keepdims=True) + EPS)
        r = jnp.where(code > 0.5, r, 0.0)
        normed.append((mixed * r * gain_ref[:, h * DH : (h + 1) * DH]).astype(BF))
    normed = jnp.concatenate(normed, 1)
    normed_ref[...] = normed
    attn = dot(normed, wo_ref[...]).astype(BF)
    mine = step // (pl.num_programs(0) // 2) == tp_ref[0]

    @pl.when(mine)
    def _():
        own_ref[...] = attn

    @pl.when(jnp.logical_not(mine))
    def _():
        other_ref[...] = attn


def score_kernel(
    tp_ref, da_own_ref, da_other_ref, wo_ref, mixed_ref, code_ref, gain_ref, q_ref, k_ref, v_ref, gate_ref, weight_ref,
    logit_ref, kvs_ref, sums_ref, pairs_ref,
    da_ref, dmix_ref, dl_ref, y_ref, gain_grad_ref, dkv_ref, reach_ref,
):
    step = pl.program_id(0)
    mine = step // (pl.num_programs(0) // 2) == tp_ref[0]
    da = jnp.where(mine, da_own_ref[...], da_other_ref[...])
    da_ref[...] = da
    dnormed = nt(da, wo_ref[...])
    dnormed = jnp.where(code_ref[:, :1] > 0.5, dnormed, 0.0)
    dmix, gain_grad = [], []
    for h in range(2):
        mixed = mixed_ref[:, h * DH : (h + 1) * DH]
        r = lax.rsqrt(jnp.mean(mixed * mixed, axis=-1, keepdims=True) + EPS)
        n = mixed * r
        d = head(dnormed, h)
        u = d * gain_ref[:, h * DH : (h + 1) * DH]
        gain_grad.append(jnp.sum(d * n, axis=0, keepdims=True))
        dmix.append((r * (u - n * jnp.mean(u * n, axis=-1, keepdims=True))).astype(BF))
    gain_grad = jnp.concatenate(gain_grad, 1)
    dmix = jnp.concatenate(dmix, 1)
    dmix_ref[...] = dmix
    q, k, v = q_ref[...], k_ref[...], v_ref[...]
    gate, weight = gate_ref[...], weight_ref[...]
    first, _, rows, cols, _ = decays(gate, weight, sums_ref)
    logits = logit_ref[...]
    probs = softmax2(logits)
    low = kvs_ref[0].astype(BF)
    reads = [nt(head(dmix, h), head(v, h)) for h in range(2)]
    outer = jnp.concatenate([nt(head(dmix, h), state(low, h)[:, DH:]) for h in range(2)], 1)
    dprobs = first * outer + through(reads, rows, cols, pairs_ref)
    weighted = probs * dprobs
    sums = [
        jnp.broadcast_to(jnp.sum(slots(weighted, h), axis=-1, keepdims=True), (CH, SLOTS)) for h in range(2)
    ]
    dl = (weighted - probs * jnp.concatenate(sums, 1)) * SCALE
    dl_ref[...] = dl
    y_ref[...] = dl * logits + weighted
    part = state_grads(dl, probs, first, q, dmix)
    fade = fade_of(gate)

    @pl.when(step == 0)
    def _():
        gain_grad_ref[...] = gain_grad
        dkv_ref[...] = part
        reach_ref[...] = jnp.broadcast_to(fade, reach_ref.shape)

    @pl.when(step > 0)
    def _():
        gain_grad_ref[...] += gain_grad
        reach = reach_ref[...]
        dkv_ref[...] += jnp.concatenate([reach] * (dkv_ref.shape[1] // reach.shape[1]), 1) * part
        reach_ref[...] = reach * fade


def state_grads(dl, probs, first, q, dmix):
    a, b = (dl * first).astype(BF), (probs * first).astype(BF)
    return jnp.concatenate(
        [jnp.concatenate([tn(slots(a, h), head(q, h)), tn(slots(b, h), head(dmix, h))], 1) for h in range(2)], 0
    )


def grad_kernel(
    tp_ref, q_ref, k_ref, v_ref, dsq_ref, dsk_ref, gate_ref, weight_ref, dz_ref, logit_ref, kvs_ref, dmix_ref, dl_ref, y_ref,
    end_ref, flow_ref, sums_ref, pairs_ref, flipped_ref, back_ref, wq_ref, wk_ref, wv_ref, wf_ref,
    d_ref, bias_ref, own_ref, other_ref, dkv_ref, carry_ref,
):
    step = pl.program_id(0)

    @pl.when(step == 0)
    def _():
        dkv_ref[...] = end_ref[...]
        carry_ref[...] = flow_ref[...]

    q, k, v, dmix = q_ref[...], k_ref[...], v_ref[...], dmix_ref[...]
    gate, weight = gate_ref[...], weight_ref[...]
    dl = dl_ref[...]
    first, last, rows, cols, slopes = decays(gate, weight, sums_ref)
    probs = softmax2(logit_ref[...])
    kv, dkv = kvs_ref[0], dkv_ref[...]
    low, dlow = kv.astype(BF), dkv.astype(BF)
    r0, r1, s0, s1 = back_through([probs, dl], rows, cols, pairs_ref)
    turned = [
        nt(head(a, h), head(b, h)) for h in range(2) for a, b in ((k, q), (v, dmix))
    ]
    dw = last * jnp.concatenate(
        [nt(jnp.concatenate([head(k, h), head(v, h)], 1), state(dlow, h)) for h in range(2)], 1
    )
    for i in range(len(rows)):
        keep = flipped_ref[i] != 0
        left = jnp.concatenate([jnp.where(keep, x, 0.0).astype(BF) for x in turned], 1)
        a, b = halves((dl * rows[i]).astype(BF)), halves((probs * rows[i]).astype(BF))
        dw = dw + slopes[i] * dot(left, jnp.concatenate([a[0], b[0], a[1], b[1]], 0))
    trail = (last * weight).astype(BF)
    spread = (dl * first).astype(BF)
    reading, dscore = [r0.astype(BF), r1.astype(BF)], [s0.astype(BF), s1.astype(BF)]
    dq, dk, dv = [], [], []
    for h in range(2):
        dq.append(dot(dscore[h], head(k, h)) + dot(slots(spread, h), state(low, h)[:, :DH]))
        dk.append(tn(dscore[h], head(q, h)) + dot(slots(trail, h), state(dlow, h)[:, :DH]))
        dv.append(tn(reading[h], head(dmix, h)) + dot(slots(trail, h), state(dlow, h)[:, DH:]))
    dq = (jnp.concatenate(dq, 1) * dsq_ref[...].astype(F32)).astype(BF)
    dk = (jnp.concatenate(dk, 1) * dsk_ref[...].astype(F32)).astype(BF)
    dv = jnp.concatenate(dv, 1).astype(BF)
    both = dot(back_ref[...], split3(y_ref[...] - weight * dw))
    cut = gate[BUCKET : BUCKET + 1] < 0.5 * RESET_LOG
    late = lax.broadcasted_iota(jnp.int32, gate.shape, 0) >= BUCKET
    flow = jnp.where(cut, both[CH:], both[:CH]) + jnp.where(cut & jnp.logical_not(late), 0.0, carry_ref[...])
    df = ((flow - jnp.exp(gate) * dw) * dz_ref[...]).astype(BF)
    d_ref[...] = jnp.concatenate([dq, dk, dv, df], 1)
    bias_part = jnp.sum(df.astype(F32), axis=0, keepdims=True)
    new = fade_of(gate) * dkv + state_grads(dl, probs, first, q, dmix)
    dkv_ref[...] = new
    carry_ref[...] = jnp.sum((kv * new).T, axis=0, keepdims=True)
    dx = (nt(dq, wq_ref[...]) + nt(dk, wk_ref[...]) + nt(dv, wv_ref[...]) + nt(df, wf_ref[...])).astype(BF)
    n = pl.num_programs(0)
    mine = (n - 1 - step) // (n // 2) == tp_ref[0]

    @pl.when(mine)
    def _():
        own_ref[...] = dx

    @pl.when(jnp.logical_not(mine))
    def _():
        other_ref[...] = dx

    @pl.when(step == 0)
    def _():
        bias_ref[...] = bias_part

    @pl.when(step > 0)
    def _():
        bias_ref[...] += bias_part


def line_sizes(count):
    return {16: (2, 2, 4), 64: (4, 4, 4)}.get(count, (count, 1, 1))


def reduce_kernel(sizes, jobs, slots_of, *refs):
    arrays = len({a for a, *_ in jobs})
    small_ref, ins, small_out, outs = refs[0], refs[1 : arrays + 1], refs[arrays + 1], refs[arrays + 2 : 2 * arrays + 2]
    rest = list(refs[2 * arrays + 2 :])
    small_held, small_got, small_send, small_recv, send_sem, recv_sem, local_sem = rest[-7:]
    index = lax.axis_index("seq")
    strides = (1, sizes[0], sizes[0] * sizes[1])
    place = [lax.rem(index // s, m) for s, m in zip(strides, sizes)]

    def peer(axis, d):
        m = sizes[axis]
        return index + (lax.rem(place[axis] + d, m) - place[axis]) * strides[axis]

    barrier = pltpu.get_barrier_semaphore()
    partners = [(axis, d) for axis in range(3) for d in range(1, sizes[axis])]
    for axis, d in partners:
        pl.semaphore_signal(barrier, inc=1, device_id={"seq": peer(axis, d)}, device_id_type=MESH)
    pl.semaphore_wait(barrier, len(partners))

    work = []
    for a, first, units, order in jobs:
        shape = []
        rows, offset = UNIT, 0
        for axis in order:
            rows = rows // sizes[axis]
            offset = offset + place[axis] * rows
            shape.append((axis, rows, pl.multiple_of(place[axis] * rows, 16), pl.multiple_of(offset, 16)))
        held, got = [], []
        for _ in range(3):
            held.append(rest.pop(0))
            got.append(rest.pop(0))
        own = rest.pop(0)
        work.append((ins[a], outs[a], pl.ds(first, units), units, shape, held, got, own))

    pending = []

    def remote(j, stage, axis, d, src, dst):
        return pltpu.make_async_remote_copy(
            src_ref=src, dst_ref=dst, send_sem=send_sem.at[j, stage, d - 1], recv_sem=recv_sem.at[j, stage, d - 1],
            device_id={"seq": peer(axis, d)}, device_id_type=MESH,
        )

    flight = {}

    def scatter(j, stage):
        src, _, at, units, shape, held, got, own = work[j]
        axis, rows, _, _ = shape[stage]
        if stage == 0:
            copy = pltpu.make_async_copy(
                src.at[at, pl.ds(shape[0][2], rows), :], own, local_sem.at[j, 0]
            )
            copy.start()
            flight[j, "own"] = copy
        else:
            src, at = held[stage - 1], slice(None)
        flight[j, stage] = []
        for d in range(1, sizes[axis]):
            target = pl.multiple_of(lax.rem(place[axis] + d, sizes[axis]) * rows, 16)
            copy = remote(j, stage, axis, d, src.at[at, pl.ds(target, rows), :], got[stage].at[d - 1])
            copy.start()
            flight[j, stage].append(copy)

    def add(j, stage):
        _, out, at, units, shape, held, got, own = work[j]
        axis, rows, mine, _ = shape[stage]
        if stage == 0:
            flight[j, "own"].wait()
        for copy in flight[j, stage]:
            copy.wait_recv()

        def one(u, _):
            if stage == 0:
                total = own[u].astype(F32)
            else:
                total = held[stage - 1][u, pl.ds(mine, rows), :].astype(F32)
            for d in range(sizes[axis] - 1):
                total = total + got[stage][d, u].astype(F32)
            held[stage][u] = total.astype(BF)
            return 0

        lax.fori_loop(0, units, one, 0)

    def gather(j, stage):
        _, out, at, units, shape, held, got, own = work[j]
        axis, rows, _, offset = shape[stage]
        here = out.at[at, pl.ds(offset, rows), :]
        src = here
        if stage == 2:
            src = held[2]
            copy = pltpu.make_async_copy(src, here, local_sem.at[j, 1])
            copy.start()
            flight[j, "home"] = copy
        flight[j, 5 - stage] = []
        for d in range(1, sizes[axis]):
            copy = remote(j, 5 - stage, axis, d, src, here)
            copy.start()
            flight[j, 5 - stage].append(copy)

    def landed(j, stage):
        if stage == 2:
            flight[j, "home"].wait()
        for copy in flight[j, 5 - stage]:
            copy.wait_recv()

    def step(j, s):
        if s == 0:
            scatter(j, 0)
        elif s <= 2:
            add(j, s - 1)
            scatter(j, s)
        elif s == 3:
            add(j, 2)
            gather(j, 2)
        elif s <= 5:
            landed(j, 6 - s)
            gather(j, 5 - s)
        else:
            landed(j, 0)

    def small_step(s):
        if s > 0:
            total = small_held[s - 1]
            for copy in flight["small", s - 1]:
                copy.wait_recv()
            for d in range(sizes[s - 1] - 1):
                total = total + small_got[s - 1, d]
            if s == 3:
                small_out[...] = total
                return
            small_held[s] = total
        else:
            small_held[0] = small_ref[...]
        flight["small", s] = []
        for d in range(1, sizes[s]):
            copy = pltpu.make_async_remote_copy(
                src_ref=small_held.at[s], dst_ref=small_got.at[s, d - 1], send_sem=small_send.at[s, d - 1],
                recv_sem=small_recv.at[s, d - 1], device_id={"seq": peer(s, d)}, device_id_type=MESH,
            )
            copy.start()
            flight["small", s].append(copy)

    for slot in range(max(slots_of) + 7):
        if slot <= 3:
            small_step(slot)
        for j, begin in enumerate(slots_of):
            if 0 <= slot - begin <= 6:
                step(j, slot - begin)
    for copies in flight.values():
        if isinstance(copies, list):
            for copy in copies:
                copy.wait_send()


def reduce_units(small, arrays, jobs, slots_of):
    sizes = line_sizes(lax.axis_size("seq"))
    scratch = []
    for _, _, units, order in jobs:
        rows = UNIT
        for axis in order:
            rows = rows // sizes[axis]
            scratch.append(pltpu.VMEM((units, rows, 128), BF))
            scratch.append(pltpu.VMEM((max(sizes[axis] - 1, 1), units, rows, 128), BF))
        scratch.append(pltpu.VMEM((units, UNIT // sizes[order[0]], 128), BF))
    most = max(max(sizes) - 1, 1)
    scratch += [pltpu.VMEM((3, *small.shape), F32), pltpu.VMEM((3, most, *small.shape), F32)]
    scratch += [pltpu.SemaphoreType.DMA((3, most))] * 2
    scratch += [pltpu.SemaphoreType.DMA((len(jobs), 6, most))] * 2 + [pltpu.SemaphoreType.DMA((len(jobs), 2))]
    return pl.pallas_call(
        functools.partial(reduce_kernel, sizes, jobs, slots_of),
        out_shape=[jax.ShapeDtypeStruct(small.shape, F32)] + [jax.ShapeDtypeStruct(a.shape, BF) for a in arrays],
        in_specs=[pl.BlockSpec(memory_space=pltpu.VMEM)] + [pl.BlockSpec(memory_space=pl.ANY)] * len(arrays),
        out_specs=[pl.BlockSpec(memory_space=pltpu.VMEM)] + [pl.BlockSpec(memory_space=pl.ANY)] * len(arrays),
        scratch_shapes=scratch,
        compiler_params=pltpu.CompilerParams(
            collective_id=0, has_side_effects=True, vmem_limit_bytes=VMEM_LIMIT
        ),
        name="reduce",
    )(small, *arrays)


def units_kernel(a_ref, b_ref, out_ref):
    part = tn(a_ref[...], b_ref[...]).astype(BF)
    for c in range(out_ref.shape[0]):
        out_ref[c] = part[:, c * 128 : (c + 1) * 128]


def outer_units(a, b, name):
    span, tall = a.shape
    steps = -(-b.shape[1] // 512)
    return pl.pallas_call(
        units_kernel,
        grid=(steps,),
        in_specs=[pl.BlockSpec((span, tall), lambda i: (0, 0)), pl.BlockSpec((span, 512), lambda i: (0, i))],
        out_specs=pl.BlockSpec((4, tall, 128), lambda i: (i, 0, 0)),
        out_shape=jax.ShapeDtypeStruct((4 * steps, tall, 128), BF),
        compiler_params=pltpu.CompilerParams(dimension_semantics=("arbitrary",), vmem_limit_bytes=VMEM_LIMIT),
        cost_estimate=pl.CostEstimate(flops=2 * span * tall * b.shape[1], bytes_accessed=8 << 20, transcendentals=0),
        name=name,
    )(a, b)


def widen_kernel(parts, *refs):
    for (which, first, count), out_ref in zip(parts, refs[-len(parts) :]):
        for c in range(count):
            out_ref[:, c * 128 : (c + 1) * 128] = refs[which][first + c].astype(F32)


def widen(arrays, parts, steps, name):
    spec = lambda shape, index: pl.BlockSpec(shape, index)
    return pl.pallas_call(
        functools.partial(widen_kernel, parts),
        grid=(steps,),
        in_specs=[spec((a.shape[0], a.shape[1] // steps, 128), lambda i: (0, i, 0)) for a in arrays],
        out_specs=[spec((arrays[w].shape[1] // steps, n * 128), lambda i: (i, 0)) for w, _, n in parts],
        out_shape=[jax.ShapeDtypeStruct((arrays[w].shape[1], n * 128), F32) for w, _, n in parts],
        compiler_params=pltpu.CompilerParams(dimension_semantics=("arbitrary",), vmem_limit_bytes=VMEM_LIMIT),
        name=name,
    )(*arrays)


X, Y, Z = 0, 1, 2
PLAN = (
    (1, 0, 2, (Y, X, Z), 2), (2, 0, 6, (X, Y, Z), 1), (0, 0, 8, (X, Y, Z), 2), (0, 8, 6, (Y, X, Z), 2),
    (1, 2, 9, (X, Y, Z), 3), (0, 14, 8, (Y, X, Z), 3), (2, 6, 3, (Z, X, Y), 2), (2, 9, 1, (Y, X, Z), 3),
    (2, 10, 1, (Y, X, Z), 0), (2, 11, 2, (Z, Y, X), 1), (3, 0, 4, (Y, X, Z), 0),
)


def call(kernel, count, ins, outs, scratch=(), tp=None, flops=0, moved=0, name=None):
    grid_spec = pltpu.PrefetchScalarGridSpec(
        num_scalar_prefetch=1,
        grid=(count,),
        in_specs=[pl.BlockSpec(block, index) for _, block, index in ins],
        out_specs=[pl.BlockSpec(block, index) for _, _, block, index in outs],
        scratch_shapes=list(scratch),
    )
    return pl.pallas_call(
        kernel,
        grid_spec=grid_spec,
        out_shape=[jax.ShapeDtypeStruct(shape, dtype) for shape, dtype, _, _ in outs],
        compiler_params=pltpu.CompilerParams(
            dimension_semantics=("arbitrary",), vmem_limit_bytes=VMEM_LIMIT
        ),
        cost_estimate=pl.CostEstimate(flops=flops, bytes_accessed=moved, transcendentals=0),
        name=name,
    )(tp, *[a for a, _, _ in ins])


def whole(array):
    return (array, array.shape, lambda i, tp: (0,) * array.ndim)


def rows_of(array):
    return (array, (CH, array.shape[1]), lambda i, tp: (i, 0))


def swap(x):
    return lax.ppermute(x, "tp", [(0, 1), (1, 0)])


def scan_states(total, fade, earlier):
    count = lax.axis_size("seq")
    index = lax.axis_index("seq")
    entering, entering_fade = jnp.zeros_like(total), jnp.ones_like(fade)
    for bit in range(count.bit_length() - 1):
        high = fade.astype(BF)
        sent = jnp.concatenate([total.astype(BF), high, (fade - high.astype(F32)).astype(BF)], 1)
        got = lax.ppermute(sent, "seq", [(i, i ^ (1 << bit)) for i in range(count)])
        width = total.shape[1]
        part = got[:, :width].astype(F32)
        part_fade = got[:, width : width + CH].astype(F32) + got[:, width + CH :].astype(F32)
        behind = ((index >> bit) & 1) == (1 if earlier else 0)
        entering = jnp.where(behind, entering_fade[:, :1] * part + entering, entering)
        entering_fade = jnp.where(behind, entering_fade * part_fade, entering_fade)
        total = jnp.where(behind, fade[:, :1] * part + total, part_fade[:, :1] * total + part)
        fade = fade * part_fade
    return entering


def token_code(lengths, positions):
    buckets = (lengths + BUCKET - 1) // BUCKET
    spans = buckets * BUCKET
    starts = jnp.cumsum(spans) - spans
    segment = jnp.sum((positions[:, None] >= starts[None, :]).astype(jnp.int32), axis=1) - 1
    picked = segment[:, None] == jnp.arange(lengths.shape[0], dtype=jnp.int32)[None, :]
    begin = jnp.sum(jnp.where(picked, starts[None, :], 0), axis=1)
    length = jnp.sum(jnp.where(picked, lengths[None, :], 0), axis=1)
    offset = positions - begin
    return jnp.where(offset == 0, 2.0, jnp.where(offset < length, 1.0, 0.0)).astype(F32)


def row_norm(x, gain):
    r = lax.rsqrt(jnp.mean(x * x, axis=-1, keepdims=True) + EPS)
    return x * r * gain


def row_norm_back(x, gain, grad):
    r = lax.rsqrt(jnp.mean(x * x, axis=-1, keepdims=True) + EPS)
    n = x * r
    u = grad * gain
    return r * (u - n * jnp.mean(u * n, axis=-1, keepdims=True)), jnp.sum(grad * n, axis=0)


def per_device(
    tokens, norm_gain, query_weight, key_weight, value_weight, forget_weight, forget_bias, head_gain,
    out_weight, feed_gain, gate_weight, up_weight, down_weight, lengths, cotangent,
):
    half, width = tokens.shape
    span = 2 * half
    count = span // CH
    cols = query_weight.shape[1]
    lanes = forget_weight.shape[1]
    tp = lax.axis_index("tp").astype(jnp.int32)[None]
    sums, pairs, flipped, back = tables()
    sums, back = jnp.asarray(sums, BF), jnp.asarray(back, BF)
    pairs, flipped = jnp.asarray(pairs), jnp.asarray(flipped)

    tokens_other, cot_other = swap(tokens), swap(cotangent)
    positions = lax.axis_index("seq") * span + jnp.arange(span, dtype=jnp.int32)
    code = jnp.broadcast_to(token_code(lengths, positions)[:, None], (span, lanes))
    half_map = lambda i, tp: (i % (count // 2), 0)
    own_map = lambda i, tp: (jnp.clip(i - tp[0] * (count // 2), 0, count // 2 - 1), 0)
    other_map = lambda i, tp: (jnp.clip(i - (1 - tp[0]) * (count // 2), 0, count // 2 - 1), 0)
    block = (CH, width)
    row = lambda n, d: ((span, n), d, (CH, n), lambda i, tp: (i, 0))
    fixed = lambda shape: (shape, F32, shape, lambda i, tp: (0,) * len(shape))

    xn, q, k, v, dsq, dsk, gate, weight, dzf, kv_run, fade_run = call(
        project_kernel, count,
        [(tokens, block, half_map), (tokens_other, block, half_map), whole(norm_gain[None]), whole(query_weight),
         whole(key_weight), whole(value_weight), whole(forget_weight), whole(forget_bias[None]), rows_of(code), whole(sums)],
        [row(width, BF)] + [row(cols, BF)] * 5 + [row(lanes, F32)] * 3 + [fixed((lanes, 2 * DH)), fixed((lanes, CH))],
        tp=tp, flops=2 * span * width * (3 * cols + lanes), moved=16 << 20, name="project",
    )

    kv_start = scan_states(kv_run, fade_run, True)

    logits, kvs, mixed, normed, attn_own, attn_other = call(
        mix_kernel, count,
        [rows_of(q), rows_of(k), rows_of(v), rows_of(gate), rows_of(weight), rows_of(code), whole(kv_start), whole(sums),
         whole(pairs), whole(head_gain[None]), whole(out_weight)],
        [row(lanes, F32), ((count, lanes, 2 * DH), F32, (1, lanes, 2 * DH), lambda i, tp: (i, 0, 0)), row(cols, F32),
         row(cols, BF), ((half, width), BF, block, own_map), ((half, width), BF, block, other_map)],
        scratch=[pltpu.VMEM((lanes, 2 * DH), F32)],
        tp=tp, flops=4 * span * width * cols, moved=16 << 20, name="mix",
    )

    own = tokens.astype(F32)
    resid = own + (attn_own.astype(F32) + swap(attn_other).astype(F32))
    hidden_own = row_norm(resid, feed_gain).astype(BF)
    hidden = jnp.concatenate([hidden_own, swap(hidden_own)], 0)
    cot = jnp.concatenate([cotangent, cot_other], 0)
    ff_gate = dot(hidden, gate_weight)
    ff_up = dot(hidden, up_weight)
    dact = nt(cot, down_weight)
    sig = jax.nn.sigmoid(ff_gate)
    act = (ff_gate * sig * ff_up).astype(BF)
    dgate = (dact * ff_up * sig * (1.0 + ff_gate * (1.0 - sig))).astype(BF)
    dup = (dact * ff_gate * sig).astype(BF)
    feed = dot(act, down_weight).astype(BF)
    dhidden = (nt(dgate, gate_weight) + nt(dup, up_weight)).astype(BF)
    down_units = outer_units(act, cot, "down_units")
    ff_units = outer_units(hidden, jnp.concatenate([dgate, dup], 1), "ff_units")

    dhidden_own = dhidden[:half].astype(F32) + swap(dhidden[half:]).astype(F32)
    block_out = (resid + (feed[:half].astype(F32) + swap(feed[half:]).astype(F32))).astype(BF)
    dresid_norm, feed_gain_part = row_norm_back(resid, feed_gain, dhidden_own)
    dresid = cotangent.astype(F32) + dresid_norm
    da_own = dresid.astype(BF)
    da_other = swap(da_own)

    da, dmix, dl, y, head_gain_grad, dkv_run, reach = call(
        score_kernel, count,
        [(da_own, block, half_map), (da_other, block, half_map), whole(out_weight), rows_of(mixed), rows_of(code),
         whole(head_gain[None]), rows_of(q), rows_of(k), rows_of(v), rows_of(gate), rows_of(weight), rows_of(logits),
         (kvs, (1, lanes, 2 * DH), lambda i, tp: (i, 0, 0)), whole(sums), whole(pairs)],
        [row(width, BF), row(cols, BF), row(lanes, F32), row(lanes, F32), fixed((1, cols)), fixed((lanes, 2 * DH)),
         fixed((lanes, CH))],
        tp=tp, flops=4 * span * width * cols, moved=16 << 20, name="score",
    )

    dkv_end = scan_states(dkv_run, reach, False)
    out_units = outer_units(normed, da, "out_units")
    kv_end = fade_run[:, :1] * kv_start + kv_run
    flow = jnp.sum(kv_end * dkv_end, axis=1)[None]

    turn = lambda i: count - 1 - i
    rows_back = lambda a: (a, (CH, a.shape[1]), lambda i, tp: (turn(i), 0))
    row_back = lambda n, d: ((span, n), d, (CH, n), lambda i, tp: (turn(i), 0))
    d_all, bias_grad, dx_own, dx_other = call(
        grad_kernel, count,
        [rows_back(a) for a in (q, k, v, dsq, dsk, gate, weight, dzf, logits)]
        + [(kvs, (1, lanes, 2 * DH), lambda i, tp: (turn(i), 0, 0)), rows_back(dmix), rows_back(dl), rows_back(y),
           whole(dkv_end), whole(flow), whole(sums), whole(pairs), whole(flipped), whole(back),
           whole(query_weight), whole(key_weight), whole(value_weight), whole(forget_weight)],
        [row_back(3 * cols + lanes, BF), fixed((1, lanes)),
         ((half, width), BF, block, lambda i, tp: own_map(turn(i), tp)),
         ((half, width), BF, block, lambda i, tp: other_map(turn(i), tp))],
        scratch=[pltpu.VMEM((lanes, 2 * DH), F32), pltpu.VMEM((1, lanes), F32)],
        tp=tp, flops=2 * span * width * (3 * cols + lanes), moved=24 << 20, name="grad",
    )

    mixer_units = outer_units(xn, d_all, "mixer_units")
    dx = dx_own.astype(F32) + swap(dx_other).astype(F32)
    own_grad, norm_gain_part = row_norm_back(own, norm_gain, dx)
    tokens_grad = (dresid + own_grad).astype(BF)
    small = jnp.concatenate([norm_gain_part, feed_gain_part, bias_grad[0], head_gain_grad[0]]).reshape(-1, 128)
    small = jnp.pad(small, ((0, -small.shape[0] % 8), (0, 0)))

    def stacked(units):
        return units.reshape(-1, UNIT, 128)

    small_sum, ff_sum, down_sum, mixer_sum, out_sum = reduce_units(
        small, [ff_units, stacked(down_units), mixer_units, stacked(out_units)],
        tuple(p[:4] for p in PLAN), tuple(p[4] for p in PLAN),
    )
    vectors = small_sum.reshape(-1)[: 2 * width + lanes + cols]
    gains = vectors[: 2 * width].reshape(2, width)
    gains = gains + swap(gains)
    blocks, ff_blocks = cols // 128, gate_weight.shape[1] // 128
    gate_sum, up_sum = widen([ff_sum], ((0, 0, ff_blocks), (0, ff_blocks, ff_blocks)), 8, "wide_ff")
    (down_sum,) = widen([down_sum.reshape(down_units.shape)], ((0, 0, width // 128),), 4, "wide_down")
    parts = tuple((0, i * blocks, blocks) for i in range(3)) + ((0, 3 * blocks, 1),)
    query_sum, key_sum, value_sum, forget_sum = widen([mixer_sum], parts, 4, "wide_mixer")
    (out_sum,) = widen([out_sum.reshape(out_units.shape)], ((0, 0, width // 128),), 2, "wide_out")
    return (
        block_out, tokens_grad, gains[0], query_sum, key_sum, value_sum, forget_sum,
        vectors[2 * width : 2 * width + lanes], vectors[2 * width + lanes :], out_sum, gains[1], gate_sum, up_sum, down_sum,
    )


def solution(mesh):
    rows, by_col, by_row = P(("seq", "tp"), None), P(None, "tp"), P("tp", None)
    return jax.shard_map(
        per_device,
        mesh=mesh,
        in_specs=(
            rows, P(), by_col, by_col, by_col, by_col, P("tp"), P("tp"), by_row, P(), by_col, by_col, by_row, P(), rows,
        ),
        out_specs=(
            rows, rows, P(), by_col, by_col, by_col, by_col, P("tp"), P("tp"), by_row, P(), by_col, by_col, by_row,
        ),
        check_vma=False,
    )
```

```python
import functools

import jax
import jax.numpy as jnp
import numpy as np
from jax import lax
from jax.experimental import pallas as pl
from jax.experimental.pallas import tpu as pltpu
from jax.sharding import PartitionSpec as P

DH = 256
SLOTS = 64
BUCKET = 64
CH = 128
BASE = 8
HALVES = (64, 32, 16, 8)
RESET_LOG = -16384.0
LIFT = 2.0**20
SCALE = DH**-0.5

EPS = 1e-06
NORMALIZER = 8.0

BF = jnp.bfloat16
F32 = jnp.float32
VMEM_LIMIT = 56 * 1024 * 1024
UNIT = 1024
MESH = pl.DeviceIdType.MESH


def dot(a, b):
    return lax.dot_general(a, b, (((1,), (0,)), ((), ())), preferred_element_type=F32)


def nt(a, b):
    return lax.dot_general(a, b, (((1,), (1,)), ((), ())), preferred_element_type=F32)


def tn(a, b):
    return lax.dot_general(a, b, (((0,), (0,)), ((), ())), preferred_element_type=F32)


def tables():
    t, u = np.arange(CH)[:, None], np.arange(CH)[None, :]
    sums, pairs = [u <= t, u > t], []
    for half in HALVES:
        mid = t // (2 * half) * (2 * half) + half
        sums.append(np.where(t >= mid, (u >= mid) & (u <= t), (u > t) & (u < mid)))
        pairs.append(
            (t // (2 * half) == u // (2 * half)) & (t % (2 * half) >= half) & (u % (2 * half) < half)
        )
    ref = t // BASE * BASE + BASE // 2 - 1
    sums.append(((u > ref) & (u <= t)).astype(int) - ((u > t) & (u <= ref)).astype(int))
    pairs.append((t // BASE == u // BASE) & (u <= t))
    stacked = np.concatenate([s.astype(np.float32) for s in sums], 0)
    back = np.concatenate([(u >= t), (u >= t) & ((t >= BUCKET) | (u < BUCKET))], 0).astype(np.float32)
    return (
        np.concatenate([stacked] * 3, 1),
        np.stack(pairs).astype(np.float32),
        np.stack([p.T for p in pairs]).astype(np.float32),
        np.concatenate([back] * 3, 1),
    )


def split3(x):
    high = x.astype(BF)
    rest = x - high.astype(F32)
    middle = rest.astype(BF)
    low = (rest - middle.astype(F32)).astype(BF)
    return jnp.concatenate([high, middle, low], 0)


def decays(gate, weight, sums_ref):
    sums = dot(sums_ref[...], split3(gate))
    part = [sums[i * CH : (i + 1) * CH] for i in range(3 + len(HALVES))]
    first, last = jnp.exp(part[0]), jnp.exp(part[1])
    rows = [jnp.exp(p) for p in part[2:-1]]
    cols = [r * weight for r in rows]
    slopes = list(rows)
    rows.append(jnp.exp(part[-1]) * LIFT)
    slopes.append(jnp.exp(-part[-1]) * (1 / LIFT))
    cols.append(slopes[-1] * weight)
    return first, last, rows, cols, slopes


def halves(x):
    left = lax.broadcasted_iota(jnp.int32, x.shape, 1) < SLOTS
    zero = jnp.zeros_like(x)
    return jnp.where(left, x, zero), jnp.where(left, zero, x)


def head(x, h):
    return x[:, h * DH : (h + 1) * DH]


def slots(x, h):
    return x[:, h * SLOTS : (h + 1) * SLOTS]


def state(x, h):
    return x[h * SLOTS : (h + 1) * SLOTS]


def through(pairwise, rows, cols, pairs_ref):
    total = None
    for i in range(len(rows)):
        keep = pairs_ref[i] != 0
        left = jnp.concatenate([jnp.where(keep, p, 0.0).astype(BF) for p in pairwise], 1)
        right = jnp.concatenate(halves(cols[i].astype(BF)), 0)
        term = rows[i] * dot(left, right)
        total = term if total is None else total + term
    return total


def back_through(values, rows, cols, pairs_ref):
    totals = None
    for i in range(len(rows)):
        keep = pairs_ref[i] != 0
        stack = [part for v in values for part in halves((v * rows[i]).astype(BF))]
        out = nt(jnp.concatenate(stack, 0), cols[i].astype(BF))
        terms = [jnp.where(keep, out[n * CH : (n + 1) * CH], 0.0) for n in range(len(stack))]
        totals = terms if totals is None else [a + b for a, b in zip(totals, terms)]
    return totals


def softmax2(logits):
    out = []
    for h in range(2):
        x = slots(logits, h) * SCALE
        e = jnp.exp(x - jnp.max(x, axis=-1, keepdims=True))
        out.append(e / jnp.sum(e, axis=-1, keepdims=True))
    return jnp.concatenate(out, 1)


def fade_of(gate):
    return jnp.exp(jnp.sum(gate.T, axis=1, keepdims=True))


def run_part(trail, keys, values):
    return jnp.concatenate(
        [
            jnp.concatenate([tn(slots(trail, h), head(keys, h)), tn(slots(trail, h), head(values, h))], 1)
            for h in range(2)
        ],
        0,
    )


def project_kernel(
    tp_ref, own_ref, other_ref, gain_ref, wq_ref, wk_ref, wv_ref, wf_ref, bias_ref, code_ref, sums_ref,
    xn_ref, q_ref, k_ref, v_ref, dsq_ref, dsk_ref, gate_ref, weight_ref, dz_ref, kv_ref, fade_ref,
):
    step = pl.program_id(0)
    mine = step // (pl.num_programs(0) // 2) == tp_ref[0]
    x = jnp.where(mine, own_ref[...], other_ref[...]).astype(F32)
    mean = jnp.mean(x * x, axis=-1, keepdims=True)
    xn = (x * lax.rsqrt(mean + EPS) * gain_ref[...]).astype(BF)
    xn_ref[...] = xn

    def silu(raw):
        s = 1.0 / (1.0 + jnp.exp(-raw))
        return (raw * s).astype(BF), (s * (1.0 + raw * (1.0 - s))).astype(BF)

    q, dsq = silu(dot(xn, wq_ref[...]))
    q_ref[...], dsq_ref[...] = q, dsq
    k, dsk = silu(dot(xn, wk_ref[...]))
    k_ref[...], dsk_ref[...] = k, dsk
    v = dot(xn, wv_ref[...]).astype(BF)
    v_ref[...] = v
    z = dot(xn, wf_ref[...]) + bias_ref[...]
    code = code_ref[...]
    valid, reset = code > 0.5, code > 1.5
    soft = jnp.log(1.0 + jnp.exp(-jnp.abs(z)))
    log_sig = jnp.minimum(z, 0.0) - soft
    gate = jnp.where(valid, log_sig * (1.0 / NORMALIZER), 0.0)
    weight = jnp.where(reset, 1.0, 1.0 - jnp.exp(gate))
    gate = jnp.where(reset, RESET_LOG, gate)
    down = jnp.exp(-jnp.abs(z))
    sig_neg = jnp.where(z > 0, down, 1.0) / (1.0 + down)
    gate_ref[...] = gate
    weight_ref[...] = weight
    dz_ref[...] = jnp.where(valid & (code < 1.5), sig_neg * (1.0 / NORMALIZER), 0.0)
    last = jnp.exp(dot(sums_ref[CH : 2 * CH], split3(gate)))
    part = run_part((last * weight).astype(BF), k, v)
    fade = fade_of(gate)

    @pl.when(step == 0)
    def _():
        kv_ref[...] = part
        fade_ref[...] = jnp.broadcast_to(fade, fade_ref.shape)

    @pl.when(step > 0)
    def _():
        kv_ref[...] = fade * kv_ref[...] + part
        fade_ref[...] = fade_ref[...] * fade


def mix_kernel(
    tp_ref, q_ref, k_ref, v_ref, gate_ref, weight_ref, code_ref, start_ref, sums_ref, pairs_ref, gain_ref, wo_ref,
    logit_ref, kvs_ref, mixed_ref, normed_ref, own_ref, other_ref, kv_ref,
):
    step = pl.program_id(0)

    @pl.when(step == 0)
    def _():
        kv_ref[...] = start_ref[...]

    q, k, v = q_ref[...], k_ref[...], v_ref[...]
    gate, weight = gate_ref[...], weight_ref[...]
    first, last, rows, cols, _ = decays(gate, weight, sums_ref)
    kv = kv_ref[...]
    kvs_ref[0] = kv
    low = kv.astype(BF)
    scores = [nt(head(q, h), head(k, h)) for h in range(2)]
    outer = jnp.concatenate([nt(head(q, h), state(low, h)[:, :DH]) for h in range(2)], 1)
    logits = first * outer + through(scores, rows, cols, pairs_ref)
    logit_ref[...] = logits
    probs = softmax2(logits)
    reading = back_through([probs], rows, cols, pairs_ref)
    spread = (probs * first).astype(BF)
    kv_ref[...] = fade_of(gate) * kv + run_part((last * weight).astype(BF), k, v)
    code = code_ref[:, :1]
    normed = []
    for h in range(2):
        mixed = dot(slots(spread, h), state(low, h)[:, DH:]) + dot(reading[h].astype(BF), head(v, h))
        mixed_ref[:, h * DH : (h + 1) * DH] = mixed
        r = lax.rsqrt(jnp.mean(mixed * mixed, axis=-1, keepdims=True) + EPS)
        r = jnp.where(code > 0.5, r, 0.0)
        normed.append((mixed * r * gain_ref[:, h * DH : (h + 1) * DH]).astype(BF))
    normed = jnp.concatenate(normed, 1)
    normed_ref[...] = normed
    attn = dot(normed, wo_ref[...]).astype(BF)
    mine = step // (pl.num_programs(0) // 2) == tp_ref[0]

    @pl.when(mine)
    def _():
        own_ref[...] = attn

    @pl.when(jnp.logical_not(mine))
    def _():
        other_ref[...] = attn


def state_grads(dl, probs, first, q, dmix):
    a, b = (dl * first).astype(BF), (probs * first).astype(BF)
    return jnp.concatenate(
        [jnp.concatenate([tn(slots(a, h), head(q, h)), tn(slots(b, h), head(dmix, h))], 1) for h in range(2)], 0
    )


def line_sizes(count):
    return {16: (2, 2, 4), 64: (4, 4, 4)}.get(count, (count, 1, 1))


class Lines:
    def __init__(self, sizes):
        self.sizes = sizes
        self.index = lax.axis_index("seq")
        self.half = lax.axis_index("tp")
        self.strides = (1, sizes[0], sizes[0] * sizes[1])
        self.place = [lax.rem(self.index // s, m) for s, m in zip(self.strides, sizes)]

    def peer(self, axis, d):
        m = self.sizes[axis]
        return self.index + (lax.rem(self.place[axis] + d, m) - self.place[axis]) * self.strides[axis]

    def greet(self):
        barrier = pltpu.get_barrier_semaphore()
        count = 1
        pl.semaphore_signal(barrier, inc=1, device_id={"tp": 1 - self.half}, device_id_type=MESH)
        for axis in range(3):
            for d in range(1, self.sizes[axis]):
                pl.semaphore_signal(barrier, inc=1, device_id={"seq": self.peer(axis, d)}, device_id_type=MESH)
                count += 1
        pl.semaphore_wait(barrier, count)


def remote(src, dst, sems, at, device):
    return pltpu.make_async_remote_copy(
        src_ref=src, dst_ref=dst, send_sem=sems[0].at[at], recv_sem=sems[1].at[at], device_id=device, device_id_type=MESH
    )


def job_scratch(sizes, jobs):
    scratch = []
    for _, _, units, order in jobs:
        rows = UNIT
        for axis in order:
            rows = rows // sizes[axis]
            scratch.append(pltpu.VMEM((units, rows, 128), BF))
            scratch.append(pltpu.VMEM((max(sizes[axis] - 1, 1), units, rows, 128), BF))
    most = max(max(sizes) - 1, 1)
    return scratch + [pltpu.SemaphoreType.DMA((len(jobs), 6, most))] * 2 + [pltpu.SemaphoreType.DMA((len(jobs), 2))]


class Jobs:
    def __init__(self, lines, jobs, ins, outs, inside, scratch):
        self.lines, self.jobs, self.ins, self.outs, self.inside = lines, jobs, ins, outs, inside
        self.sems, self.local = scratch[-3:-1], scratch[-1]
        self.held, self.got, self.shape = [], [], []
        for j, (_, _, _, order) in enumerate(jobs):
            rows, offset, shape = UNIT, 0, []
            for axis in order:
                rows = rows // lines.sizes[axis]
                mine = lines.place[axis] * rows
                offset = offset + mine
                shape.append((axis, rows, pl.multiple_of(mine, 16), pl.multiple_of(offset, 16)))
            self.shape.append(shape)
            self.held.append(scratch[6 * j : 6 * j + 6 : 2])
            self.got.append(scratch[6 * j + 1 : 6 * j + 6 : 2])

    def copies(self, j, s):
        lines, (a, first, units, _) = self.lines, self.jobs[j]
        stage = s if s < 3 else 5 - s
        axis, rows, _, offset = self.shape[j][stage]
        out = []
        for d in range(1, lines.sizes[axis]):
            if s < 3:
                target = pl.multiple_of(lax.rem(lines.place[axis] + d, lines.sizes[axis]) * rows, 16)
                if s == 0:
                    src = self.ins[a].at[pl.ds(first, units), pl.ds(target, rows), :]
                else:
                    src = self.held[j][s - 1].at[:, pl.ds(target, rows), :]
                dst = self.got[j][s].at[d - 1]
            else:
                dst = self.outs[a].at[pl.ds(first, units), pl.ds(offset, rows), :]
                src = self.held[j][2] if s == 3 else dst
            out.append(remote(src, dst, self.sems, (j, s, d - 1), {"seq": lines.peer(axis, d)}))
        return out

    def own(self, j):
        a, first, units, _ = self.jobs[j]
        _, rows, mine, _ = self.shape[j][0]
        src = self.ins[a].at[pl.ds(first, units), pl.ds(mine, rows), :]
        return pltpu.make_async_copy(src, self.held[j][0], self.local.at[j, 0])

    def home(self, j):
        a, first, units, _ = self.jobs[j]
        _, rows, _, offset = self.shape[j][2]
        dst = self.outs[a].at[pl.ds(first, units), pl.ds(offset, rows), :]
        return pltpu.make_async_copy(self.held[j][2], dst, self.local.at[j, 1])

    def add(self, j, stage):
        a, first, units, _ = self.jobs[j]
        axis, rows, mine, _ = self.shape[j][stage]
        held, got = self.held[j], self.got[j]

        def one(u, carry):
            if stage > 0:
                total = held[stage - 1][u, pl.ds(mine, rows), :].astype(F32)
            elif self.inside[a]:
                total = self.ins[a][first + u, pl.ds(mine, rows), :].astype(F32)
            else:
                total = held[0][u].astype(F32)
            for d in range(self.lines.sizes[axis] - 1):
                total = total + got[stage][d, u].astype(F32)
            held[stage][u] = total.astype(BF)
            return carry

        lax.fori_loop(0, units, one, 0)

    def step(self, j, s):
        if s == 0 and not self.inside[self.jobs[j][0]]:
            self.own(j).start()
        if s == 1 and not self.inside[self.jobs[j][0]]:
            self.own(j).wait()
        if s == 4:
            self.home(j).wait()
        if s > 0:
            for copy in self.copies(j, s - 1):
                copy.wait_recv()
        if 1 <= s <= 3:
            self.add(j, s - 1)
        if s == 3:
            self.home(j).start()
        if s < 6:
            for copy in self.copies(j, s):
                copy.start()

    def finish(self):
        for j in range(len(self.jobs)):
            for s in range(6):
                for copy in self.copies(j, s):
                    copy.wait_send()


def scan_lines(lines, total_ref, fade_ref, enter_ref, reach_ref, sent_ref, got_ref, sems, earlier, between):
    width = total_ref.shape[1]
    enter_ref[...] = jnp.zeros_like(enter_ref)
    reach_ref[...] = jnp.ones_like(reach_ref)
    count = lines.sizes[0] * lines.sizes[1] * lines.sizes[2]
    rounds = count.bit_length() - 1
    side = [lax.rem(lines.index // (1 << bit), 2) for bit in range(rounds)]

    def copy(bit):
        partner = lines.index + (1 - 2 * side[bit]) * (1 << bit)
        return remote(sent_ref.at[bit], got_ref.at[bit], sems, bit, {"seq": partner})

    for bit in range(rounds):
        fade = fade_ref[...]
        high = fade.astype(BF)
        sent_ref[bit, :, :width] = total_ref[...].astype(BF)
        sent_ref[bit, :, width : width + CH] = high
        sent_ref[bit, :, width + CH :] = (fade - high.astype(F32)).astype(BF)
        copy(bit).start()
        between(bit)
        copy(bit).wait_recv()
        part = got_ref[bit, :, :width].astype(F32)
        part_fade = got_ref[bit, :, width : width + CH].astype(F32) + got_ref[bit, :, width + CH :].astype(F32)
        behind = side[bit] == (1 if earlier else 0)
        enter, reach, total = enter_ref[...], reach_ref[...], total_ref[...]
        enter_ref[...] = jnp.where(behind, reach[:, :1] * part + enter, enter)
        reach_ref[...] = jnp.where(behind, reach * part_fade, reach)
        total_ref[...] = jnp.where(behind, fade[:, :1] * part + total, part_fade[:, :1] * total + part)
        fade_ref[...] = fade * part_fade
    return [copy(bit) for bit in range(rounds)]


def chunk_rows(c):
    return pl.ds(pl.multiple_of(c * CH, CH), CH)


def score_chunk(c, s):
    at = chunk_rows(c)
    dnormed = nt(s.da[at], s.wo[...])
    dnormed = jnp.where(s.code[at, :1] > 0.5, dnormed, 0.0)
    dmix = []
    for h in range(2):
        mixed = s.mixed[at, h * DH : (h + 1) * DH]
        r = lax.rsqrt(jnp.mean(mixed * mixed, axis=-1, keepdims=True) + EPS)
        n = mixed * r
        d = head(dnormed, h)
        u = d * s.gain[:, h * DH : (h + 1) * DH]
        s.gain_grad[:, h * DH : (h + 1) * DH] += jnp.sum(d * n, axis=0, keepdims=True)
        dmix.append((r * (u - n * jnp.mean(u * n, axis=-1, keepdims=True))).astype(BF))
    dmix = jnp.concatenate(dmix, 1)
    s.dmix[at] = dmix
    q, v = s.q[at], s.v[at]
    gate, weight = s.gate[at], s.weight[at]
    first, _, rows, cols, _ = decays(gate, weight, s.sums)
    logits = s.logits[at]
    probs = softmax2(logits)
    low = s.kvs[c].astype(BF)
    reads = [nt(head(dmix, h), head(v, h)) for h in range(2)]
    outer = jnp.concatenate([nt(head(dmix, h), state(low, h)[:, DH:]) for h in range(2)], 1)
    dprobs = first * outer + through(reads, rows, cols, s.pairs)
    weighted = probs * dprobs
    sums = [
        jnp.broadcast_to(jnp.sum(slots(weighted, h), axis=-1, keepdims=True), (CH, SLOTS)) for h in range(2)
    ]
    dl = (weighted - probs * jnp.concatenate(sums, 1)) * SCALE
    s.dl[at] = dl
    s.y[at] = dl * logits + weighted
    part = state_grads(dl, probs, first, q, dmix)
    reach = s.fade[...]
    s.dkv[...] += jnp.concatenate([reach] * (s.dkv.shape[1] // reach.shape[1]), 1) * part
    s.fade[...] = reach * fade_of(gate)


def grad_chunk(c, s):
    at = chunk_rows(c)
    q, k, v, dmix = s.q[at], s.k[at], s.v[at], s.dmix[at]
    gate, weight = s.gate[at], s.weight[at]
    dl = s.dl[at]
    first, last, rows, cols, slopes = decays(gate, weight, s.sums)
    probs = softmax2(s.logits[at])
    kv, dkv = s.kvs[c], s.enter[...]
    low, dlow = kv.astype(BF), dkv.astype(BF)
    r0, r1, s0, s1 = back_through([probs, dl], rows, cols, s.pairs)
    turned = [nt(head(a, h), head(b, h)) for h in range(2) for a, b in ((k, q), (v, dmix))]
    dw = last * jnp.concatenate(
        [nt(jnp.concatenate([head(k, h), head(v, h)], 1), state(dlow, h)) for h in range(2)], 1
    )
    for i in range(len(rows)):
        keep = s.flipped[i] != 0
        left = jnp.concatenate([jnp.where(keep, x, 0.0).astype(BF) for x in turned], 1)
        a, b = halves((dl * rows[i]).astype(BF)), halves((probs * rows[i]).astype(BF))
        dw = dw + slopes[i] * dot(left, jnp.concatenate([a[0], b[0], a[1], b[1]], 0))
    trail = (last * weight).astype(BF)
    spread = (dl * first).astype(BF)
    reading, dscore = [r0.astype(BF), r1.astype(BF)], [s0.astype(BF), s1.astype(BF)]
    dq, dk, dv = [], [], []
    for h in range(2):
        dq.append(dot(dscore[h], head(k, h)) + dot(slots(spread, h), state(low, h)[:, :DH]))
        dk.append(tn(dscore[h], head(q, h)) + dot(slots(trail, h), state(dlow, h)[:, :DH]))
        dv.append(tn(reading[h], head(dmix, h)) + dot(slots(trail, h), state(dlow, h)[:, DH:]))
    dq = (jnp.concatenate(dq, 1) * s.dsq[at].astype(F32)).astype(BF)
    dk = (jnp.concatenate(dk, 1) * s.dsk[at].astype(F32)).astype(BF)
    dv = jnp.concatenate(dv, 1).astype(BF)
    both = dot(s.back[...], split3(s.y[at] - weight * dw))
    cut = gate[BUCKET : BUCKET + 1] < 0.5 * RESET_LOG
    late = lax.broadcasted_iota(jnp.int32, gate.shape, 0) >= BUCKET
    flow = jnp.where(cut, both[CH:], both[:CH]) + jnp.where(cut & jnp.logical_not(late), 0.0, s.carry[...])
    df = ((flow - jnp.exp(gate) * dw) * s.dzf[at]).astype(BF)
    s.d_all[at] = jnp.concatenate([dq, dk, dv, df], 1)
    s.bias_grad[...] += jnp.sum(df.astype(F32), axis=0, keepdims=True)
    new = fade_of(gate) * dkv + state_grads(dl, probs, first, q, dmix)
    s.enter[...] = new
    s.carry[...] = jnp.sum((kv * new).T, axis=0, keepdims=True)
    dx = nt(dq, s.wq[...]) + nt(dk, s.wk[...]) + nt(dv, s.wv[...]) + nt(df, s.wf[...])
    s.norm_grad[...] += jnp.sum(dx * s.xn[at].astype(F32), axis=0, keepdims=True)
    s.dx[at] = dx.astype(BF)


class Bag:
    pass


LOADED = (
    "wo", "mixed", "code", "gain", "q", "k", "v", "gate", "weight", "logits", "kvs", "sums", "pairs", "flipped", "back",
    "dsq", "dsk", "dzf", "wq", "wk", "wv", "wf", "xn", "normed", "kv_end", "norm_gain", "feed_part",
)


def back_kernel(sizes, jobs, ticks, shapes, *refs):
    refs = list(refs)
    take = lambda n: [refs.pop(0) for _ in range(n)]
    da_own, da_other, ff_in, down_in = take(4)
    sources = take(len(LOADED))
    small_out, dx_own_out, dx_got, ff_out, down_out, mixer_out, out_out = take(7)
    s = Bag()
    for name in LOADED:
        setattr(s, name, refs.pop(0))
    for name in ("da", "dmix", "dl", "y", "d_all", "dx", "gain_grad", "bias_grad", "norm_grad", "dkv", "fade", "enter",
                 "reach", "carry", "mixer_units", "out_units", "sent", "got", "small_held", "small_got"):
        setattr(s, name, refs.pop(0))
    load_sem, da_sem, out_sem = take(3)
    scan_sems, small_sems, dx_sems = take(2), take(2), take(2)
    lines = Lines(sizes)
    half = da_own.shape[0]
    count = 2 * half // CH

    loads = {n: pltpu.make_async_copy(src, getattr(s, n), load_sem.at[i]) for i, (n, src) in enumerate(zip(LOADED, sources))}
    own_rows = pl.ds(pl.multiple_of(lines.half * half, half), half)
    other_rows = pl.ds(pl.multiple_of((1 - lines.half) * half, half), half)
    da_loads = [
        pltpu.make_async_copy(da_own, s.da.at[own_rows], da_sem.at[0]),
        pltpu.make_async_copy(da_other, s.da.at[other_rows], da_sem.at[1]),
    ]
    for copy in da_loads + list(loads.values()):
        copy.start()
    for ref in (s.gain_grad, s.bias_grad, s.norm_grad, s.dkv):
        ref[...] = jnp.zeros_like(ref)
    s.fade[...] = jnp.ones_like(s.fade)
    lines.greet()
    work = Jobs(
        lines, jobs, [ff_in, down_in, s.mixer_units, s.out_units], [ff_out, down_out, mixer_out, out_out],
        (False, False, True, True), refs,
    )
    pending = [list(t) for t in ticks]

    def tick():
        for j, step in pending.pop(0):
            work.step(j, step)

    def loop(body):
        todo = [pending.pop(0) for _ in range(count)]

        def one(i, carry):
            body(i)
            for k, steps in enumerate(todo):
                if steps:

                    @pl.when(i == k)
                    def _():
                        for j, step in steps:
                            work.step(j, step)

            return carry

        lax.fori_loop(0, count, one, 0)

    tick()
    for copy in da_loads + list(loads.values()):
        copy.wait()
    loop(lambda i: score_chunk(i, s))

    width = s.xn.shape[1]

    def out_part(n):
        wide = width // 4
        part = tn(s.normed[...], s.da[:, n * wide : (n + 1) * wide]).astype(BF)
        tall = part.shape[0]
        for c in range(wide // 128):
            row = (n * (wide // 128) + c) * tall
            s.out_units[row // UNIT, row % UNIT : row % UNIT + tall] = part[:, c * 128 : (c + 1) * 128]

    def between(n):
        if n < 4:
            out_part(n)
            tick()

    scans = scan_lines(lines, s.dkv, s.fade, s.enter, s.reach, s.sent, s.got, scan_sems, False, between)
    s.carry[...] = jnp.sum((s.kv_end[...] * s.enter[...]).T, axis=0, keepdims=True)
    loop(lambda i: grad_chunk(count - 1 - i, s))

    dx_copy = remote(s.dx.at[other_rows], dx_got, dx_sems, 0, {"tp": 1 - lines.half})
    dx_copy.start()
    dx_home = pltpu.make_async_copy(s.dx.at[own_rows], dx_own_out, out_sem.at[0])
    dx_home.start()
    lanes = s.bias_grad.shape[1]
    vectors = [s.norm_grad[...] / s.norm_gain[...], s.feed_part[...], s.bias_grad[...], s.gain_grad[...]]
    row = 0
    for v in vectors:
        for c in range(v.shape[1] // lanes):
            s.small_held[0, row : row + 1] = v[:, c * lanes : (c + 1) * lanes]
            row += 1
    s.small_held[0, row:] = jnp.zeros_like(s.small_held[0, row:])

    def small_copies(n):
        return [
            remote(s.small_held.at[n], s.small_got.at[n, d - 1], small_sems, (n, d - 1), {"seq": lines.peer(n, d)})
            for d in range(1, sizes[n])
        ]

    def small_step(n):
        if n > 0:
            for copy in small_copies(n - 1):
                copy.wait_recv()
            total = s.small_held[n - 1]
            for d in range(sizes[n - 1] - 1):
                total = total + s.small_got[n - 1, d]
            if n == 3:
                small_out[...] = total
                return
            s.small_held[n] = total
        for copy in small_copies(n):
            copy.start()

    blocks = s.d_all.shape[1] // 128
    for n in range(-(-blocks // 4)):
        some = min(4, blocks - 4 * n)
        part = tn(s.xn[...], s.d_all[:, n * 512 : n * 512 + some * 128]).astype(BF)
        for c in range(some):
            s.mixer_units[4 * n + c] = part[:, c * 128 : (c + 1) * 128]
        if n < 4:
            small_step(n)
        tick()
    while pending:
        tick()
    dx_copy.wait()
    dx_home.wait()
    for copy in scans + [c for n in range(3) for c in small_copies(n)]:
        copy.wait_send()
    work.finish()


def back_call(da_own, da_other, ff_units, down_units, loaded, jobs, ticks):
    sizes = line_sizes(lax.axis_size("seq"))
    rounds = (sizes[0] * sizes[1] * sizes[2]).bit_length() - 1
    most = max(max(sizes) - 1, 1)
    half, width = da_own.shape
    span = 2 * half
    lanes, cols = loaded["wf"].shape[1], loaded["wq"].shape[1]
    rows = (2 * width + lanes + cols) // lanes
    small = (rows + -rows % 8, lanes)
    mixer = (3 * cols + lanes) // 128
    shapes = [
        ((span, width), BF), ((span, cols), BF), ((span, lanes), F32), ((span, lanes), F32), ((span, 3 * cols + lanes), BF),
        ((span, width), BF), ((1, cols), F32), ((1, lanes), F32), ((1, width), F32), ((lanes, 2 * DH), F32), ((lanes, CH), F32),
        ((lanes, 2 * DH), F32), ((lanes, CH), F32), ((1, lanes), F32), ((mixer, UNIT, 128), BF),
        ((cols * width // 128 // UNIT, UNIT, 128), BF), ((rounds, lanes, 2 * DH + 2 * CH), BF),
        ((rounds, lanes, 2 * DH + 2 * CH), BF), ((3, *small), F32), ((3, most, *small), F32),
    ]
    dma = pltpu.SemaphoreType.DMA
    scratch = [pltpu.VMEM(loaded[n].shape, loaded[n].dtype) for n in LOADED] + [pltpu.VMEM(*x) for x in shapes]
    scratch += [dma((len(LOADED),)), dma((2,)), dma((1,))]
    scratch += [dma((rounds,))] * 2 + [dma((3, most))] * 2 + [dma((1,))] * 2
    scratch += job_scratch(sizes, jobs)
    anywhere = pl.BlockSpec(memory_space=pl.ANY)
    return pl.pallas_call(
        functools.partial(back_kernel, sizes, jobs, ticks, shapes),
        out_shape=[
            jax.ShapeDtypeStruct(small, F32), jax.ShapeDtypeStruct((half, width), BF), jax.ShapeDtypeStruct((half, width), BF),
            jax.ShapeDtypeStruct(ff_units.shape, BF), jax.ShapeDtypeStruct(down_units.shape, BF),
            jax.ShapeDtypeStruct((mixer, UNIT, 128), BF), jax.ShapeDtypeStruct((cols * width // 128 // UNIT, UNIT, 128), BF),
        ],
        in_specs=[anywhere] * (4 + len(LOADED)),
        out_specs=[pl.BlockSpec(memory_space=pltpu.VMEM)] + [anywhere] * 6,
        scratch_shapes=scratch,
        compiler_params=pltpu.CompilerParams(collective_id=0, has_side_effects=True, vmem_limit_bytes=63 * 1024 * 1024),
        name="back",
    )(da_own, da_other, ff_units, down_units, *[loaded[n] for n in LOADED])


def units_kernel(a_ref, b_ref, out_ref):
    part = tn(a_ref[...], b_ref[...]).astype(BF)
    for c in range(out_ref.shape[0]):
        out_ref[c] = part[:, c * 128 : (c + 1) * 128]


def outer_units(a, b, name):
    span, tall = a.shape
    steps = -(-b.shape[1] // 512)
    return pl.pallas_call(
        units_kernel,
        grid=(steps,),
        in_specs=[pl.BlockSpec((span, tall), lambda i: (0, 0)), pl.BlockSpec((span, 512), lambda i: (0, i))],
        out_specs=pl.BlockSpec((4, tall, 128), lambda i: (i, 0, 0)),
        out_shape=jax.ShapeDtypeStruct((4 * steps, tall, 128), BF),
        compiler_params=pltpu.CompilerParams(dimension_semantics=("arbitrary",), vmem_limit_bytes=VMEM_LIMIT),
        cost_estimate=pl.CostEstimate(flops=2 * span * tall * b.shape[1], bytes_accessed=8 << 20, transcendentals=0),
        name=name,
    )(a, b)


def widen_kernel(parts, *refs):
    for (which, first, count), out_ref in zip(parts, refs[-len(parts) :]):
        for c in range(count):
            out_ref[:, c * 128 : (c + 1) * 128] = refs[which][first + c].astype(F32)


def widen(arrays, parts, steps, name):
    spec = lambda shape, index: pl.BlockSpec(shape, index)
    return pl.pallas_call(
        functools.partial(widen_kernel, parts),
        grid=(steps,),
        in_specs=[spec((a.shape[0], a.shape[1] // steps, 128), lambda i: (0, i, 0)) for a in arrays],
        out_specs=[spec((arrays[w].shape[1] // steps, n * 128), lambda i: (i, 0)) for w, _, n in parts],
        out_shape=[jax.ShapeDtypeStruct((arrays[w].shape[1], n * 128), F32) for w, _, n in parts],
        compiler_params=pltpu.CompilerParams(dimension_semantics=("arbitrary",), vmem_limit_bytes=VMEM_LIMIT),
        name=name,
    )(*arrays)


X, Y, Z = 0, 1, 2
JOBS = (
    (2, 0, 3, (X, Y, Z)),
    (1, 0, 2, (Y, X, Z)),
    (2, 3, 3, (X, Y, Z)),
    (0, 0, 8, (X, Y, Z)),
    (1, 2, 6, (Z, Y, X)),
    (2, 6, 4, (X, Y, Z)),
    (0, 8, 5, (Y, X, Z)),
    (3, 0, 3, (X, Y, Z)),
    (2, 10, 3, (Y, X, Z)),
    (0, 13, 5, (Y, X, Z)),
    (1, 8, 3, (Y, X, Z)),
    (0, 18, 4, (Y, X, Z)),
    (3, 3, 1, (X, Z, Y)),
)
TICKS = (
    ((3, 0), (4, 0), (11, 0),), ((10, 0),), (), (), ((11, 1),), (), ((9, 0),), (), ((10, 1),),
    ((3, 1), (1, 0), (6, 0),), ((11, 2),), ((10, 2), (4, 1), (9, 1),), ((11, 3),), ((7, 0), (12, 0),),
    ((10, 3), (9, 2), (3, 2),), (), ((11, 4), (1, 1),), ((7, 1), (10, 4),), ((12, 1),), (), ((9, 3), (11, 5),),
    ((1, 2), (6, 1),), ((0, 0),), ((10, 5), (4, 2), (2, 0),), ((3, 3), (5, 0),), ((8, 0),), ((7, 2),), ((12, 2),),
    ((6, 2),), ((9, 4),), ((0, 1),), ((1, 3),), ((11, 6),), ((4, 3),), ((10, 6),), ((2, 1),), ((3, 4),), ((7, 3),),
    ((8, 1),), ((12, 3),), ((0, 2),), ((5, 1),), ((6, 3),), ((1, 4),), ((2, 2),), ((9, 5),), ((7, 4),), ((4, 4),),
    ((0, 3),), ((8, 2),), ((3, 5),), ((12, 4),), ((1, 5),), ((6, 4),), ((5, 2),), ((2, 3),), ((0, 4),), ((8, 3),),
    ((12, 5),), ((9, 6),), ((3, 6),), ((7, 5),), ((5, 3),), ((4, 5),), ((2, 4),), ((6, 5),), ((8, 4),), ((12, 6),),
    ((1, 6),), ((0, 5),), ((5, 4),), ((7, 6),), ((2, 5),), ((8, 5),), ((0, 6),), ((6, 6),), ((5, 5),), ((2, 6),),
    ((8, 6),), ((4, 6),), ((5, 6),),
)


def call(kernel, count, ins, outs, scratch=(), tp=None, flops=0, moved=0, name=None):
    grid_spec = pltpu.PrefetchScalarGridSpec(
        num_scalar_prefetch=1,
        grid=(count,),
        in_specs=[pl.BlockSpec(block, index) for _, block, index in ins],
        out_specs=[pl.BlockSpec(block, index) for _, _, block, index in outs],
        scratch_shapes=list(scratch),
    )
    return pl.pallas_call(
        kernel,
        grid_spec=grid_spec,
        out_shape=[jax.ShapeDtypeStruct(shape, dtype) for shape, dtype, _, _ in outs],
        compiler_params=pltpu.CompilerParams(
            dimension_semantics=("arbitrary",), vmem_limit_bytes=VMEM_LIMIT
        ),
        cost_estimate=pl.CostEstimate(flops=flops, bytes_accessed=moved, transcendentals=0),
        name=name,
    )(tp, *[a for a, _, _ in ins])


def whole(array):
    return (array, array.shape, lambda i, tp: (0,) * array.ndim)


def rows_of(array):
    return (array, (CH, array.shape[1]), lambda i, tp: (i, 0))


def swap(x):
    return lax.ppermute(x, "tp", [(0, 1), (1, 0)])


def scan_states(total, fade, earlier):
    count = lax.axis_size("seq")
    index = lax.axis_index("seq")
    entering, entering_fade = jnp.zeros_like(total), jnp.ones_like(fade)
    for bit in range(count.bit_length() - 1):
        high = fade.astype(BF)
        sent = jnp.concatenate([total.astype(BF), high, (fade - high.astype(F32)).astype(BF)], 1)
        got = lax.ppermute(sent, "seq", [(i, i ^ (1 << bit)) for i in range(count)])
        width = total.shape[1]
        part = got[:, :width].astype(F32)
        part_fade = got[:, width : width + CH].astype(F32) + got[:, width + CH :].astype(F32)
        behind = ((index >> bit) & 1) == (1 if earlier else 0)
        entering = jnp.where(behind, entering_fade[:, :1] * part + entering, entering)
        entering_fade = jnp.where(behind, entering_fade * part_fade, entering_fade)
        total = jnp.where(behind, fade[:, :1] * part + total, part_fade[:, :1] * total + part)
        fade = fade * part_fade
    return entering


def token_code(lengths, positions):
    buckets = (lengths + BUCKET - 1) // BUCKET
    spans = buckets * BUCKET
    starts = jnp.cumsum(spans) - spans
    segment = jnp.sum((positions[:, None] >= starts[None, :]).astype(jnp.int32), axis=1) - 1
    picked = segment[:, None] == jnp.arange(lengths.shape[0], dtype=jnp.int32)[None, :]
    begin = jnp.sum(jnp.where(picked, starts[None, :], 0), axis=1)
    length = jnp.sum(jnp.where(picked, lengths[None, :], 0), axis=1)
    offset = positions - begin
    return jnp.where(offset == 0, 2.0, jnp.where(offset < length, 1.0, 0.0)).astype(F32)


def row_norm(x, gain):
    r = lax.rsqrt(jnp.mean(x * x, axis=-1, keepdims=True) + EPS)
    return x * r * gain


def row_norm_back(x, gain, grad):
    r = lax.rsqrt(jnp.mean(x * x, axis=-1, keepdims=True) + EPS)
    n = x * r
    u = grad * gain
    return r * (u - n * jnp.mean(u * n, axis=-1, keepdims=True)), jnp.sum(grad * n, axis=0)


def per_device(
    tokens, norm_gain, query_weight, key_weight, value_weight, forget_weight, forget_bias, head_gain,
    out_weight, feed_gain, gate_weight, up_weight, down_weight, lengths, cotangent,
):
    half, width = tokens.shape
    span = 2 * half
    count = span // CH
    cols = query_weight.shape[1]
    lanes = forget_weight.shape[1]
    tp = lax.axis_index("tp").astype(jnp.int32)[None]
    sums, pairs, flipped, back = tables()
    sums, back = jnp.asarray(sums, BF), jnp.asarray(back, BF)
    pairs, flipped = jnp.asarray(pairs), jnp.asarray(flipped)

    tokens_other, cot_other = swap(tokens), swap(cotangent)
    positions = lax.axis_index("seq") * span + jnp.arange(span, dtype=jnp.int32)
    code = jnp.broadcast_to(token_code(lengths, positions)[:, None], (span, lanes))
    half_map = lambda i, tp: (i % (count // 2), 0)
    own_map = lambda i, tp: (jnp.clip(i - tp[0] * (count // 2), 0, count // 2 - 1), 0)
    other_map = lambda i, tp: (jnp.clip(i - (1 - tp[0]) * (count // 2), 0, count // 2 - 1), 0)
    block = (CH, width)
    row = lambda n, d: ((span, n), d, (CH, n), lambda i, tp: (i, 0))
    fixed = lambda shape: (shape, F32, shape, lambda i, tp: (0,) * len(shape))

    xn, q, k, v, dsq, dsk, gate, weight, dzf, kv_run, fade_run = call(
        project_kernel, count,
        [(tokens, block, half_map), (tokens_other, block, half_map), whole(norm_gain[None]), whole(query_weight),
         whole(key_weight), whole(value_weight), whole(forget_weight), whole(forget_bias[None]), rows_of(code), whole(sums)],
        [row(width, BF)] + [row(cols, BF)] * 5 + [row(lanes, F32)] * 3 + [fixed((lanes, 2 * DH)), fixed((lanes, CH))],
        tp=tp, flops=2 * span * width * (3 * cols + lanes), moved=16 << 20, name="project",
    )

    kv_start = scan_states(kv_run, fade_run, True)

    logits, kvs, mixed, normed, attn_own, attn_other = call(
        mix_kernel, count,
        [rows_of(q), rows_of(k), rows_of(v), rows_of(gate), rows_of(weight), rows_of(code), whole(kv_start), whole(sums),
         whole(pairs), whole(head_gain[None]), whole(out_weight)],
        [row(lanes, F32), ((count, lanes, 2 * DH), F32, (1, lanes, 2 * DH), lambda i, tp: (i, 0, 0)), row(cols, F32),
         row(cols, BF), ((half, width), BF, block, own_map), ((half, width), BF, block, other_map)],
        scratch=[pltpu.VMEM((lanes, 2 * DH), F32)],
        tp=tp, flops=4 * span * width * cols, moved=16 << 20, name="mix",
    )

    own = tokens.astype(F32)
    resid = own + (attn_own.astype(F32) + swap(attn_other).astype(F32))
    hidden_own = row_norm(resid, feed_gain).astype(BF)
    hidden = jnp.concatenate([hidden_own, swap(hidden_own)], 0)
    cot = jnp.concatenate([cotangent, cot_other], 0)
    ff_gate = dot(hidden, gate_weight)
    ff_up = dot(hidden, up_weight)
    dact = nt(cot, down_weight)
    sig = jax.nn.sigmoid(ff_gate)
    act = (ff_gate * sig * ff_up).astype(BF)
    dgate = (dact * ff_up * sig * (1.0 + ff_gate * (1.0 - sig))).astype(BF)
    dup = (dact * ff_gate * sig).astype(BF)
    feed = dot(act, down_weight).astype(BF)
    dhidden = (nt(dgate, gate_weight) + nt(dup, up_weight)).astype(BF)
    down_units = outer_units(act, cot, "down_units")
    ff_units = outer_units(hidden, jnp.concatenate([dgate, dup], 1), "ff_units")

    dhidden_own = dhidden[:half].astype(F32) + swap(dhidden[half:]).astype(F32)
    block_out = (resid + (feed[:half].astype(F32) + swap(feed[half:]).astype(F32))).astype(BF)
    dresid_norm, feed_gain_part = row_norm_back(resid, feed_gain, dhidden_own)
    dresid = cotangent.astype(F32) + dresid_norm
    da_own = dresid.astype(BF)
    da_other = swap(da_own)

    def stacked(units):
        return units.reshape(-1, UNIT, 128)

    loaded = dict(
        wo=out_weight, mixed=mixed, code=code, gain=head_gain[None], q=q, k=k, v=v, gate=gate, weight=weight, logits=logits,
        kvs=kvs, sums=sums, pairs=pairs, flipped=flipped, back=back, dsq=dsq, dsk=dsk, dzf=dzf, wq=query_weight,
        wk=key_weight, wv=value_weight, wf=forget_weight, xn=xn, normed=normed,
        kv_end=fade_run[:, :1] * kv_start + kv_run, norm_gain=norm_gain[None], feed_part=feed_gain_part[None],
    )
    small_sum, dx_own, dx_got, ff_sum, down_sum, mixer_sum, out_sum = back_call(
        da_own, da_other, ff_units, stacked(down_units), loaded, JOBS, TICKS
    )
    dx = dx_own.astype(F32) + dx_got.astype(F32)
    own_grad = row_norm_back(own, norm_gain, dx)[0]
    tokens_grad = (dresid + own_grad).astype(BF)
    vectors = small_sum.reshape(-1)[: 2 * width + lanes + cols]
    gains = vectors[: 2 * width].reshape(2, width)
    gains = gains + swap(gains)
    blocks, ff_blocks = cols // 128, gate_weight.shape[1] // 128
    gate_sum, up_sum = widen([ff_sum], ((0, 0, ff_blocks), (0, ff_blocks, ff_blocks)), 8, "wide_ff")
    (down_sum,) = widen([down_sum.reshape(-1, down_weight.shape[0], 128)], ((0, 0, width // 128),), 4, "wide_down")
    parts = tuple((0, i * blocks, blocks) for i in range(3)) + ((0, 3 * blocks, 1),)
    query_sum, key_sum, value_sum, forget_sum = widen([mixer_sum], parts, 4, "wide_mixer")
    (out_sum,) = widen([out_sum.reshape(-1, out_weight.shape[0], 128)], ((0, 0, width // 128),), 2, "wide_out")
    return (
        block_out, tokens_grad, gains[0], query_sum, key_sum, value_sum, forget_sum,
        vectors[2 * width : 2 * width + lanes], vectors[2 * width + lanes :], out_sum, gains[1], gate_sum, up_sum, down_sum,
    )


def solution(mesh):
    rows, by_col, by_row = P(("seq", "tp"), None), P(None, "tp"), P("tp", None)
    return jax.shard_map(
        per_device,
        mesh=mesh,
        in_specs=(
            rows, P(), by_col, by_col, by_col, by_col, P("tp"), P("tp"), by_row, P(), by_col, by_col, by_row, P(), rows,
        ),
        out_specs=(
            rows, rows, P(), by_col, by_col, by_col, by_col, P("tp"), P("tp"), by_row, P(), by_col, by_col, by_row,
        ),
        check_vma=False,
    )
```

```python
import functools

import jax
import jax.numpy as jnp
import numpy as np
from jax import lax
from jax.experimental import pallas as pl
from jax.experimental.pallas import tpu as pltpu
from jax.sharding import PartitionSpec as P

DH = 256
SLOTS = 64
BUCKET = 64
CH = 128
BASE = 8
HALVES = (64, 32, 16, 8)
RESET_LOG = -16384.0
LIFT = 2.0**20
SCALE = DH**-0.5

EPS = 1e-06
NORMALIZER = 8.0

BF = jnp.bfloat16
F32 = jnp.float32
VMEM_LIMIT = 56 * 1024 * 1024
UNIT = 1024
MESH = pl.DeviceIdType.MESH


def dot(a, b):
    return lax.dot_general(a, b, (((1,), (0,)), ((), ())), preferred_element_type=F32)


def nt(a, b):
    return lax.dot_general(a, b, (((1,), (1,)), ((), ())), preferred_element_type=F32)


def tn(a, b):
    return lax.dot_general(a, b, (((0,), (0,)), ((), ())), preferred_element_type=F32)


def tables():
    t, u = np.arange(CH)[:, None], np.arange(CH)[None, :]
    sums, pairs = [u <= t, u > t], []
    for half in HALVES:
        mid = t // (2 * half) * (2 * half) + half
        sums.append(np.where(t >= mid, (u >= mid) & (u <= t), (u > t) & (u < mid)))
        pairs.append(
            (t // (2 * half) == u // (2 * half)) & (t % (2 * half) >= half) & (u % (2 * half) < half)
        )
    ref = t // BASE * BASE + BASE // 2 - 1
    sums.append(((u > ref) & (u <= t)).astype(int) - ((u > t) & (u <= ref)).astype(int))
    pairs.append((t // BASE == u // BASE) & (u <= t))
    stacked = np.concatenate([s.astype(np.float32) for s in sums], 0)
    back = np.concatenate([(u >= t), (u >= t) & ((t >= BUCKET) | (u < BUCKET))], 0).astype(np.float32)
    return (
        np.concatenate([stacked] * 3, 1),
        np.stack(pairs).astype(np.float32),
        np.stack([p.T for p in pairs]).astype(np.float32),
        np.concatenate([back] * 3, 1),
    )


def split3(x):
    high = x.astype(BF)
    rest = x - high.astype(F32)
    middle = rest.astype(BF)
    low = (rest - middle.astype(F32)).astype(BF)
    return jnp.concatenate([high, middle, low], 0)


def decays(gate, weight, sums_ref):
    sums = dot(sums_ref[...], split3(gate))
    part = [sums[i * CH : (i + 1) * CH] for i in range(3 + len(HALVES))]
    first, last = jnp.exp(part[0]), jnp.exp(part[1])
    rows = [jnp.exp(p) for p in part[2:-1]]
    cols = [r * weight for r in rows]
    slopes = list(rows)
    rows.append(jnp.exp(part[-1]) * LIFT)
    slopes.append(jnp.exp(-part[-1]) * (1 / LIFT))
    cols.append(slopes[-1] * weight)
    return first, last, rows, cols, slopes


def halves(x):
    left = lax.broadcasted_iota(jnp.int32, x.shape, 1) < SLOTS
    zero = jnp.zeros_like(x)
    return jnp.where(left, x, zero), jnp.where(left, zero, x)


def head(x, h):
    return x[:, h * DH : (h + 1) * DH]


def slots(x, h):
    return x[:, h * SLOTS : (h + 1) * SLOTS]


def state(x, h):
    return x[h * SLOTS : (h + 1) * SLOTS]


def through(pairwise, rows, cols, pairs_ref):
    total = None
    for i in range(len(rows)):
        keep = pairs_ref[i] != 0
        left = jnp.concatenate([jnp.where(keep, p, 0.0).astype(BF) for p in pairwise], 1)
        right = jnp.concatenate(halves(cols[i].astype(BF)), 0)
        term = rows[i] * dot(left, right)
        total = term if total is None else total + term
    return total


def back_through(values, rows, cols, pairs_ref):
    totals = None
    for i in range(len(rows)):
        keep = pairs_ref[i] != 0
        stack = [part for v in values for part in halves((v * rows[i]).astype(BF))]
        out = nt(jnp.concatenate(stack, 0), cols[i].astype(BF))
        terms = [jnp.where(keep, out[n * CH : (n + 1) * CH], 0.0) for n in range(len(stack))]
        totals = terms if totals is None else [a + b for a, b in zip(totals, terms)]
    return totals


def softmax2(logits):
    out = []
    for h in range(2):
        x = slots(logits, h) * SCALE
        e = jnp.exp(x - jnp.max(x, axis=-1, keepdims=True))
        out.append(e / jnp.sum(e, axis=-1, keepdims=True))
    return jnp.concatenate(out, 1)


def fade_of(gate):
    return jnp.exp(jnp.sum(gate.T, axis=1, keepdims=True))


def run_part(trail, keys, values):
    return jnp.concatenate(
        [
            jnp.concatenate([tn(slots(trail, h), head(keys, h)), tn(slots(trail, h), head(values, h))], 1)
            for h in range(2)
        ],
        0,
    )


def project_kernel(
    tp_ref, own_ref, other_ref, gain_ref, wq_ref, wk_ref, wv_ref, wf_ref, bias_ref, code_ref, sums_ref,
    xn_ref, q_ref, k_ref, v_ref, dsq_ref, dsk_ref, gate_ref, weight_ref, dz_ref, kv_ref, fade_ref,
):
    step = pl.program_id(0)
    mine = step // (pl.num_programs(0) // 2) == tp_ref[0]
    x = jnp.where(mine, own_ref[...], other_ref[...]).astype(F32)
    mean = jnp.mean(x * x, axis=-1, keepdims=True)
    xn = (x * lax.rsqrt(mean + EPS) * gain_ref[...]).astype(BF)
    xn_ref[...] = xn

    def silu(raw):
        s = 1.0 / (1.0 + jnp.exp(-raw))
        return (raw * s).astype(BF), (s * (1.0 + raw * (1.0 - s))).astype(BF)

    q, dsq = silu(dot(xn, wq_ref[...]))
    q_ref[...], dsq_ref[...] = q, dsq
    k, dsk = silu(dot(xn, wk_ref[...]))
    k_ref[...], dsk_ref[...] = k, dsk
    v = dot(xn, wv_ref[...]).astype(BF)
    v_ref[...] = v
    z = dot(xn, wf_ref[...]) + bias_ref[...]
    code = code_ref[...]
    valid, reset = code > 0.5, code > 1.5
    soft = jnp.log(1.0 + jnp.exp(-jnp.abs(z)))
    log_sig = jnp.minimum(z, 0.0) - soft
    gate = jnp.where(valid, log_sig * (1.0 / NORMALIZER), 0.0)
    weight = jnp.where(reset, 1.0, 1.0 - jnp.exp(gate))
    gate = jnp.where(reset, RESET_LOG, gate)
    down = jnp.exp(-jnp.abs(z))
    sig_neg = jnp.where(z > 0, down, 1.0) / (1.0 + down)
    gate_ref[...] = gate
    weight_ref[...] = weight
    dz_ref[...] = jnp.where(valid & (code < 1.5), sig_neg * (1.0 / NORMALIZER), 0.0)
    last = jnp.exp(dot(sums_ref[CH : 2 * CH], split3(gate)))
    part = run_part((last * weight).astype(BF), k, v)
    fade = fade_of(gate)

    @pl.when(step == 0)
    def _():
        kv_ref[...] = part
        fade_ref[...] = jnp.broadcast_to(fade, fade_ref.shape)

    @pl.when(step > 0)
    def _():
        kv_ref[...] = fade * kv_ref[...] + part
        fade_ref[...] = fade_ref[...] * fade


def mix_kernel(
    tp_ref, q_ref, k_ref, v_ref, gate_ref, weight_ref, code_ref, start_ref, sums_ref, pairs_ref, gain_ref, wo_ref,
    logit_ref, kvs_ref, mixed_ref, normed_ref, own_ref, other_ref, kv_ref,
):
    step = pl.program_id(0)

    @pl.when(step == 0)
    def _():
        kv_ref[...] = start_ref[...]

    q, k, v = q_ref[...], k_ref[...], v_ref[...]
    gate, weight = gate_ref[...], weight_ref[...]
    first, last, rows, cols, _ = decays(gate, weight, sums_ref)
    kv = kv_ref[...]
    low = kv.astype(BF)
    kvs_ref[0] = low
    scores = [nt(head(q, h), head(k, h)) for h in range(2)]
    outer = jnp.concatenate([nt(head(q, h), state(low, h)[:, :DH]) for h in range(2)], 1)
    logits = first * outer + through(scores, rows, cols, pairs_ref)
    logit_ref[...] = logits
    probs = softmax2(logits)
    reading = back_through([probs], rows, cols, pairs_ref)
    spread = (probs * first).astype(BF)
    kv_ref[...] = fade_of(gate) * kv + run_part((last * weight).astype(BF), k, v)
    code = code_ref[:, :1]
    normed = []
    for h in range(2):
        mixed = dot(slots(spread, h), state(low, h)[:, DH:]) + dot(reading[h].astype(BF), head(v, h))
        mixed_ref[:, h * DH : (h + 1) * DH] = mixed
        r = lax.rsqrt(jnp.mean(mixed * mixed, axis=-1, keepdims=True) + EPS)
        r = jnp.where(code > 0.5, r, 0.0)
        normed.append((mixed * r * gain_ref[:, h * DH : (h + 1) * DH]).astype(BF))
    normed = jnp.concatenate(normed, 1)
    normed_ref[...] = normed
    attn = dot(normed, wo_ref[...]).astype(BF)
    mine = step // (pl.num_programs(0) // 2) == tp_ref[0]

    @pl.when(mine)
    def _():
        own_ref[...] = attn

    @pl.when(jnp.logical_not(mine))
    def _():
        other_ref[...] = attn


def state_grads(dl, probs, first, q, dmix):
    a, b = (dl * first).astype(BF), (probs * first).astype(BF)
    return jnp.concatenate(
        [jnp.concatenate([tn(slots(a, h), head(q, h)), tn(slots(b, h), head(dmix, h))], 1) for h in range(2)], 0
    )


def line_sizes(count):
    return {16: (2, 2, 4), 64: (4, 4, 4)}.get(count, (count, 1, 1))


class Lines:
    def __init__(self, sizes):
        self.sizes = sizes
        self.index = lax.axis_index("seq")
        self.half = lax.axis_index("tp")
        self.strides = (1, sizes[0], sizes[0] * sizes[1])
        self.place = [lax.rem(self.index // s, m) for s, m in zip(self.strides, sizes)]

    def peer(self, axis, d):
        m = self.sizes[axis]
        return self.index + (lax.rem(self.place[axis] + d, m) - self.place[axis]) * self.strides[axis]

    def greet(self):
        barrier = pltpu.get_barrier_semaphore()
        count = 1
        pl.semaphore_signal(barrier, inc=1, device_id={"tp": 1 - self.half}, device_id_type=MESH)
        for axis in range(3):
            for d in range(1, self.sizes[axis]):
                pl.semaphore_signal(barrier, inc=1, device_id={"seq": self.peer(axis, d)}, device_id_type=MESH)
                count += 1
        pl.semaphore_wait(barrier, count)


def remote(src, dst, sems, at, device):
    return pltpu.make_async_remote_copy(
        src_ref=src, dst_ref=dst, send_sem=sems[0].at[at], recv_sem=sems[1].at[at], device_id=device, device_id_type=MESH
    )


def job_scratch(sizes, jobs, inside):
    scratch = []
    for a, _, units, order in jobs:
        rows = UNIT
        if not inside[a]:
            scratch.append(pltpu.VMEM((units, UNIT // sizes[order[0]], 128), BF))
        for axis in order:
            rows = rows // sizes[axis]
            scratch.append(pltpu.VMEM((max(sizes[axis] - 1, 1), units, rows, 128), BF))
    most = max(max(sizes) - 1, 1)
    return scratch + [pltpu.SemaphoreType.DMA((len(jobs), 6, most))] * 2 + [pltpu.SemaphoreType.DMA((len(jobs), 2))]


class Jobs:
    def __init__(self, lines, jobs, ins, outs, inside, scratch):
        self.lines, self.jobs, self.ins, self.outs, self.inside = lines, jobs, ins, outs, inside
        self.sems, self.local = scratch[-3:-1], scratch[-1]
        self.mine, self.held, self.got, self.shape = [], [], [], []
        scratch = list(scratch)
        for j, (a, _, _, order) in enumerate(jobs):
            rows, offset, shape = UNIT, 0, []
            for axis in order:
                rows = rows // lines.sizes[axis]
                mine = lines.place[axis] * rows
                offset = offset + mine
                shape.append((axis, rows, pl.multiple_of(mine, 16), pl.multiple_of(offset, 16)))
            self.shape.append(shape)
            self.mine.append(None if inside[a] else scratch.pop(0))
            self.got.append([scratch.pop(0) for _ in range(3)])
            self.held.append([got.at[0] for got in self.got[j]])

    def copies(self, j, s):
        lines, (a, first, units, _) = self.lines, self.jobs[j]
        stage = s if s < 3 else 5 - s
        axis, rows, _, offset = self.shape[j][stage]
        out = []
        for d in range(1, lines.sizes[axis]):
            if s < 3:
                target = pl.multiple_of(lax.rem(lines.place[axis] + d, lines.sizes[axis]) * rows, 16)
                if s == 0:
                    src = self.ins[a].at[pl.ds(first, units), pl.ds(target, rows), :]
                else:
                    src = self.held[j][s - 1].at[:, pl.ds(target, rows), :]
                dst = self.got[j][s].at[d - 1]
            else:
                dst = self.outs[a].at[pl.ds(first, units), pl.ds(offset, rows), :]
                src = self.held[j][2] if s == 3 else dst
            out.append(remote(src, dst, self.sems, (j, s, d - 1), {"seq": lines.peer(axis, d)}))
        return out

    def own(self, j):
        a, first, units, _ = self.jobs[j]
        _, rows, mine, _ = self.shape[j][0]
        src = self.ins[a].at[pl.ds(first, units), pl.ds(mine, rows), :]
        return pltpu.make_async_copy(src, self.mine[j], self.local.at[j, 0])

    def home(self, j):
        a, first, units, _ = self.jobs[j]
        _, rows, _, offset = self.shape[j][2]
        dst = self.outs[a].at[pl.ds(first, units), pl.ds(offset, rows), :]
        return pltpu.make_async_copy(self.held[j][2], dst, self.local.at[j, 1])

    def add(self, j, stage):
        a, first, units, _ = self.jobs[j]
        axis, rows, mine, _ = self.shape[j][stage]
        held, got = self.held[j], self.got[j]

        def one(u, carry):
            if stage > 0:
                total = held[stage - 1][u, pl.ds(mine, rows), :].astype(F32)
            elif self.inside[a]:
                total = self.ins[a][first + u, pl.ds(mine, rows), :].astype(F32)
            else:
                total = self.mine[j][u].astype(F32)
            for d in range(self.lines.sizes[axis] - 1):
                total = total + got[stage][d, u].astype(F32)
            held[stage][u] = total.astype(BF)
            return carry

        lax.fori_loop(0, units, one, 0)

    def step(self, j, s):
        if s == 0 and not self.inside[self.jobs[j][0]]:
            self.own(j).start()
        if s == 1 and not self.inside[self.jobs[j][0]]:
            self.own(j).wait()
        if s == 4:
            self.home(j).wait()
        if s > 0:
            for copy in self.copies(j, s - 1):
                copy.wait_recv()
        if 1 <= s <= 3:
            self.add(j, s - 1)
        if s == 3:
            self.home(j).start()
        if s < 6:
            for copy in self.copies(j, s):
                copy.start()

    def finish(self):
        for j in range(len(self.jobs)):
            for s in range(6):
                for copy in self.copies(j, s):
                    copy.wait_send()


def scan_lines(lines, total_ref, fade_ref, enter_ref, reach_ref, sent_ref, got_ref, sems, earlier, between):
    width = total_ref.shape[1]
    enter_ref[...] = jnp.zeros_like(enter_ref)
    reach_ref[...] = jnp.ones_like(reach_ref)
    count = lines.sizes[0] * lines.sizes[1] * lines.sizes[2]
    rounds = count.bit_length() - 1
    side = [lax.rem(lines.index // (1 << bit), 2) for bit in range(rounds)]

    def copy(bit):
        partner = lines.index + (1 - 2 * side[bit]) * (1 << bit)
        return remote(sent_ref.at[bit], got_ref.at[bit], sems, bit, {"seq": partner})

    for bit in range(rounds):
        fade = fade_ref[...]
        high = fade.astype(BF)
        sent_ref[bit, :, :width] = total_ref[...].astype(BF)
        sent_ref[bit, :, width : width + CH] = high
        sent_ref[bit, :, width + CH :] = (fade - high.astype(F32)).astype(BF)
        copy(bit).start()
        between(bit)
        copy(bit).wait_recv()
        part = got_ref[bit, :, :width].astype(F32)
        part_fade = got_ref[bit, :, width : width + CH].astype(F32) + got_ref[bit, :, width + CH :].astype(F32)
        behind = side[bit] == (1 if earlier else 0)
        enter, reach, total = enter_ref[...], reach_ref[...], total_ref[...]
        enter_ref[...] = jnp.where(behind, reach[:, :1] * part + enter, enter)
        reach_ref[...] = jnp.where(behind, reach * part_fade, reach)
        total_ref[...] = jnp.where(behind, fade[:, :1] * part + total, part_fade[:, :1] * total + part)
        fade_ref[...] = fade * part_fade
    return [copy(bit) for bit in range(rounds)]


def chunk_rows(c):
    return pl.ds(pl.multiple_of(c * CH, CH), CH)


def score_chunk(c, s):
    at = chunk_rows(c)
    dnormed = nt(s.da[at], s.wo[...])
    dnormed = jnp.where(s.code[at, :1] > 0.5, dnormed, 0.0)
    dmix = []
    for h in range(2):
        mixed = s.mixed[at, h * DH : (h + 1) * DH]
        r = lax.rsqrt(jnp.mean(mixed * mixed, axis=-1, keepdims=True) + EPS)
        n = mixed * r
        d = head(dnormed, h)
        u = d * s.gain[:, h * DH : (h + 1) * DH]
        s.gain_grad[:, h * DH : (h + 1) * DH] += jnp.sum(d * n, axis=0, keepdims=True)
        dmix.append((r * (u - n * jnp.mean(u * n, axis=-1, keepdims=True))).astype(BF))
    dmix = jnp.concatenate(dmix, 1)
    s.dmix[at] = dmix
    q, v = s.q[at], s.v[at]
    gate, weight = s.gate[at], s.weight[at]
    first, _, rows, cols, _ = decays(gate, weight, s.sums)
    logits = s.logits[at]
    probs = softmax2(logits)
    low = s.kvs[c]
    reads = [nt(head(dmix, h), head(v, h)) for h in range(2)]
    outer = jnp.concatenate([nt(head(dmix, h), state(low, h)[:, DH:]) for h in range(2)], 1)
    dprobs = first * outer + through(reads, rows, cols, s.pairs)
    weighted = probs * dprobs
    sums = [
        jnp.broadcast_to(jnp.sum(slots(weighted, h), axis=-1, keepdims=True), (CH, SLOTS)) for h in range(2)
    ]
    dl = (weighted - probs * jnp.concatenate(sums, 1)) * SCALE
    s.dl[at] = dl
    s.y[at] = dl * logits + weighted
    part = state_grads(dl, probs, first, q, dmix)
    reach = s.fade[...]
    s.dkv[...] += jnp.concatenate([reach] * (s.dkv.shape[1] // reach.shape[1]), 1) * part
    s.fade[...] = reach * fade_of(gate)


def grad_chunk(c, s):
    at = chunk_rows(c)
    q, k, v, dmix = s.q[at], s.k[at], s.v[at], s.dmix[at]
    gate, weight = s.gate[at], s.weight[at]
    dl = s.dl[at]
    first, last, rows, cols, slopes = decays(gate, weight, s.sums)
    probs = softmax2(s.logits[at])
    low, dkv = s.kvs[c], s.enter[...]
    dlow = dkv.astype(BF)
    r0, r1, s0, s1 = back_through([probs, dl], rows, cols, s.pairs)
    turned = [nt(head(a, h), head(b, h)) for h in range(2) for a, b in ((k, q), (v, dmix))]
    dw = last * jnp.concatenate(
        [nt(jnp.concatenate([head(k, h), head(v, h)], 1), state(dlow, h)) for h in range(2)], 1
    )
    for i in range(len(rows)):
        keep = s.flipped[i] != 0
        left = jnp.concatenate([jnp.where(keep, x, 0.0).astype(BF) for x in turned], 1)
        a, b = halves((dl * rows[i]).astype(BF)), halves((probs * rows[i]).astype(BF))
        dw = dw + slopes[i] * dot(left, jnp.concatenate([a[0], b[0], a[1], b[1]], 0))
    trail = (last * weight).astype(BF)
    spread = (dl * first).astype(BF)
    reading, dscore = [r0.astype(BF), r1.astype(BF)], [s0.astype(BF), s1.astype(BF)]
    dq, dk, dv = [], [], []
    for h in range(2):
        dq.append(dot(dscore[h], head(k, h)) + dot(slots(spread, h), state(low, h)[:, :DH]))
        dk.append(tn(dscore[h], head(q, h)) + dot(slots(trail, h), state(dlow, h)[:, :DH]))
        dv.append(tn(reading[h], head(dmix, h)) + dot(slots(trail, h), state(dlow, h)[:, DH:]))
    dq = (jnp.concatenate(dq, 1) * s.dsq[at].astype(F32)).astype(BF)
    dk = (jnp.concatenate(dk, 1) * s.dsk[at].astype(F32)).astype(BF)
    dv = jnp.concatenate(dv, 1).astype(BF)
    both = dot(s.back[...], split3(s.y[at] - weight * dw))
    cut = gate[BUCKET : BUCKET + 1] < 0.5 * RESET_LOG
    late = lax.broadcasted_iota(jnp.int32, gate.shape, 0) >= BUCKET
    flow = jnp.where(cut, both[CH:], both[:CH]) + jnp.where(cut & jnp.logical_not(late), 0.0, s.carry[...])
    df = ((flow - jnp.exp(gate) * dw) * s.dzf[at]).astype(BF)
    s.d_all[at] = jnp.concatenate([dq, dk, dv, df], 1)
    s.bias_grad[...] += jnp.sum(df.astype(F32), axis=0, keepdims=True)
    new = fade_of(gate) * dkv + state_grads(dl, probs, first, q, dmix)
    s.enter[...] = new
    s.carry[...] = jnp.sum((low.astype(F32) * new).T, axis=0, keepdims=True)
    dx = nt(dq, s.wq[...]) + nt(dk, s.wk[...]) + nt(dv, s.wv[...]) + nt(df, s.wf[...])
    s.norm_grad[...] += jnp.sum(dx * s.xn[at].astype(F32), axis=0, keepdims=True)
    s.dx[at] = dx.astype(BF)


class Bag:
    pass


LOADED = (
    "wo", "mixed", "code", "gain", "q", "k", "v", "gate", "weight", "logits", "kvs", "sums", "pairs", "flipped", "back",
    "dsq", "dsk", "dzf", "wq", "wk", "wv", "wf", "xn", "normed", "kv_end", "norm_gain", "feed_part",
)


FF_STEPS = ((0, 1), (2, 3), (4,), (5,))
INSIDE = (True, False, True, True)
ROWS = 128


def back_kernel(sizes, jobs, ticks, pieces, *refs):
    refs = list(refs)
    take = lambda n: [refs.pop(0) for _ in range(n)]
    da_own, hn_own, hn_other, dgate, dup, feed, resid, dresid, tokens, down_in = take(10)
    sources = take(len(LOADED))
    gains_out, bias_out, head_out, block_out, tokens_out, feed_got, dx_got, ff_out, down_out, mixer_out, out_out = take(11)
    s = Bag()
    for name in LOADED:
        setattr(s, name, refs.pop(0))
    for name in ("hn", "da", "dmix", "dl", "y", "wide_grads", "gain_grad", "bias_grad", "norm_grad", "dkv", "fade", "enter",
                 "reach", "carry", "ff_units", "mixer_units", "out_units", "sent", "got", "small_held", "small_got",
                 "wide", "narrow", "result"):
        setattr(s, name, refs.pop(0))
    s.dx = s.da
    hidden = dgate.shape[1]
    s.dgate, s.dup = s.wide_grads.at[:, :hidden], s.wide_grads.at[:, hidden:]
    s.d_all = s.wide_grads.at[:, : 3 * s.wq.shape[1] + s.wf.shape[1]]
    load_sem, row_sem, piece_sem = take(3)
    scan_sems, small_sems, swap_sems = take(2), take(2), take(2)
    lines = Lines(sizes)
    half = da_own.shape[0]
    count = 2 * half // CH
    tp_peer = {"tp": 1 - lines.half}

    own_rows = pl.ds(pl.multiple_of(lines.half * half, half), half)
    other_rows = pl.ds(pl.multiple_of((1 - lines.half) * half, half), half)
    loads = [
        pltpu.make_async_copy(da_own, s.da.at[own_rows], row_sem.at[0]),
        pltpu.make_async_copy(hn_own, s.hn.at[pl.ds(0, half)], row_sem.at[1]),
        pltpu.make_async_copy(hn_other, s.hn.at[pl.ds(half, half)], row_sem.at[2]),
        pltpu.make_async_copy(dgate, s.dgate, row_sem.at[3]),
        pltpu.make_async_copy(dup, s.dup, row_sem.at[4]),
    ]
    loads += [pltpu.make_async_copy(x, getattr(s, n), load_sem.at[i]) for i, (n, x) in enumerate(zip(LOADED, sources))]
    for copy in loads:
        copy.start()
    for ref in (s.gain_grad, s.bias_grad, s.norm_grad, s.dkv):
        ref[...] = jnp.zeros_like(ref)
    s.fade[...] = jnp.ones_like(s.fade)
    lines.greet()
    da_swap = remote(da_own, s.da.at[own_rows], swap_sems, 0, tp_peer)
    feed_swap = remote(feed.at[pl.ds(half, half)], feed_got, swap_sems, 1, tp_peer)
    dx_swap = remote(s.dx.at[other_rows], dx_got, swap_sems, 2, tp_peer)
    da_swap.start()
    feed_swap.start()
    work = Jobs(
        lines, jobs, [s.ff_units, down_in, s.mixer_units, s.out_units], [ff_out, down_out, mixer_out, out_out], INSIDE, refs
    )
    pending = [list(t) for t in ticks]

    def tick():
        for j, step in pending.pop(0):
            work.step(j, step)

    def loop(body):
        todo = [pending.pop(0) for _ in range(count)]

        def one(i, carry):
            body(i)
            for k, steps in enumerate(todo):
                if steps:

                    @pl.when(i == k)
                    def _():
                        for j, step in steps:
                            work.step(j, step)

            return carry

        lax.fori_loop(0, count, one, 0)

    tick()
    for copy in loads:
        copy.wait()
    da_swap.wait_recv()
    loop(lambda i: score_chunk(i, s))
    da_swap.wait_send()

    width = s.xn.shape[1]

    def out_part(n):
        wide = width // 4
        part = tn(s.normed[...], s.da[:, n * wide : (n + 1) * wide]).astype(BF)
        tall = part.shape[0]
        for c in range(wide // 128):
            row = (n * (wide // 128) + c) * tall
            s.out_units[row // UNIT, row % UNIT : row % UNIT + tall] = part[:, c * 128 : (c + 1) * 128]

    def ff_part(n):
        at = slice(n * 256, min((n + 1) * 256, s.dgate.shape[1]))
        part = tn(s.hn[...], jnp.concatenate([s.dgate[:, at], s.dup[:, at]], 1)).astype(BF)
        for c in range(part.shape[1] // 128):
            s.ff_units[4 * n + c] = part[:, c * 128 : (c + 1) * 128]

    def between(n):
        if n < 4:
            out_part(n)
            for m in FF_STEPS[n]:
                ff_part(m)
            tick()

    scans = scan_lines(lines, s.dkv, s.fade, s.enter, s.reach, s.sent, s.got, scan_sems, False, between)
    s.carry[...] = jnp.sum((s.kv_end[...] * s.enter[...]).T, axis=0, keepdims=True)
    loop(lambda i: grad_chunk(count - 1 - i, s))
    dx_swap.start()

    lanes = s.bias_grad.shape[1]
    vectors = [s.norm_grad[...] / s.norm_gain[...], s.feed_part[...], s.bias_grad[...], s.gain_grad[...]]
    row = 0
    for v in vectors:
        for c in range(v.shape[1] // lanes):
            s.small_held[0, row : row + 1] = v[:, c * lanes : (c + 1) * lanes]
            row += 1
    s.small_held[0, row:] = jnp.zeros_like(s.small_held[0, row:])

    def small_copies(n):
        if n == 3:
            return [remote(s.small_held.at[3], s.small_got.at[3, 0], small_sems, (3, 0), tp_peer)]
        return [
            remote(s.small_held.at[n], s.small_got.at[n, d - 1], small_sems, (n, d - 1), {"seq": lines.peer(n, d)})
            for d in range(1, sizes[n])
        ]

    def small_step(n):
        if n > 0:
            for copy in small_copies(n - 1):
                copy.wait_recv()
            total = s.small_held[n - 1]
            if n <= 3:
                for d in range(sizes[n - 1] - 1):
                    total = total + s.small_got[n - 1, d]
                s.small_held[n] = total
            else:
                both = total + s.small_got[3, 0]
                wide = width // lanes
                for c in range(2 * wide):
                    gains_out[c // wide : c // wide + 1, (c % wide) * lanes : (c % wide + 1) * lanes] = both[c : c + 1]
                bias_out[...] = total[2 * wide : 2 * wide + 1]
                for c in range(head_out.shape[1] // lanes):
                    head_out[:, c * lanes : (c + 1) * lanes] = total[2 * wide + 1 + c : 2 * wide + 2 + c]
        if n <= 3:
            for copy in small_copies(n):
                copy.start()

    def piece(n):
        at = pl.ds(n * ROWS, ROWS)
        copies = [
            pltpu.make_async_copy(src.at[at], dst, piece_sem.at[n, i])
            for i, (src, dst) in enumerate(
                ((resid, s.wide.at[0]), (dresid, s.wide.at[1]), (tokens, s.narrow.at[0]), (feed, s.narrow.at[1]),
                 (feed_got, s.narrow.at[2]), (dx_got, s.narrow.at[3]))
            )
        ]
        for copy in copies:
            copy.start()
        for copy in copies:
            copy.wait()
        s.result[0] = (s.wide[0] + (s.narrow[1].astype(F32) + s.narrow[2].astype(F32))).astype(BF)
        mine = s.dx[pl.ds(pl.multiple_of(lines.half * half + n * ROWS, ROWS), ROWS)]
        dx = mine.astype(F32) + s.narrow[3].astype(F32)
        x = s.narrow[0].astype(F32)
        r = lax.rsqrt(jnp.mean(x * x, axis=-1, keepdims=True) + EPS)
        norm = x * r
        u = dx * s.norm_gain[...]
        s.result[1] = (s.wide[1] + r * (u - norm * jnp.mean(u * norm, axis=-1, keepdims=True))).astype(BF)
        ends = [
            pltpu.make_async_copy(s.result.at[i], out.at[at], piece_sem.at[n, 6 + i])
            for i, out in enumerate((block_out, tokens_out))
        ]
        for copy in ends:
            copy.start()
        for copy in ends:
            copy.wait()

    blocks = s.d_all.shape[1] // 128
    for n in range(-(-blocks // 4)):
        some = min(4, blocks - 4 * n)
        part = tn(s.xn[...], s.d_all[:, n * 512 : n * 512 + some * 128]).astype(BF)
        for c in range(some):
            s.mixer_units[4 * n + c] = part[:, c * 128 : (c + 1) * 128]
        small_step(n)
        tick()
    feed_swap.wait()
    dx_swap.wait()
    left = list(range(half // ROWS))
    step = 0
    while pending:
        tick()
        step += 1
        if step == 1:
            small_step(4)
        if left and step % pieces == 0:
            piece(left.pop(0))
    for n in left:
        piece(n)
    for copy in scans + [c for n in range(4) for c in small_copies(n)]:
        copy.wait_send()
    work.finish()


def back_call(rows, down_units, loaded, jobs, ticks, pieces):
    sizes = line_sizes(lax.axis_size("seq"))
    rounds = (sizes[0] * sizes[1] * sizes[2]).bit_length() - 1
    most = max(max(sizes) - 1, 1)
    half, width = rows[0].shape
    span, hidden = 2 * half, rows[3].shape[1]
    lanes, cols = loaded["wf"].shape[1], loaded["wq"].shape[1]
    small = (2 * width + lanes + cols) // lanes
    small = (small + -small % 8, lanes)
    mixer, ff = (3 * cols + lanes) // 128, 2 * hidden // 128
    out = cols * width // 128 // UNIT
    shapes = [
        ((span, width), BF), ((span, width), BF), ((span, cols), BF), ((span, lanes), F32), ((span, lanes), F32),
        ((span, 2 * hidden), BF), ((1, cols), F32), ((1, lanes), F32), ((1, width), F32), ((lanes, 2 * DH), F32),
        ((lanes, CH), F32), ((lanes, 2 * DH), F32), ((lanes, CH), F32), ((1, lanes), F32), ((ff, UNIT, 128), BF),
        ((mixer, UNIT, 128), BF), ((out, UNIT, 128), BF), ((rounds, lanes, 2 * DH + 2 * CH), BF),
        ((rounds, lanes, 2 * DH + 2 * CH), BF), ((4, *small), F32), ((4, most, *small), F32), ((2, ROWS, width), F32),
        ((4, ROWS, width), BF), ((2, ROWS, width), BF),
    ]
    dma = pltpu.SemaphoreType.DMA
    scratch = [pltpu.VMEM(loaded[n].shape, loaded[n].dtype) for n in LOADED] + [pltpu.VMEM(*x) for x in shapes]
    scratch += [dma((len(LOADED),)), dma((5,)), dma((half // ROWS, 8))]
    scratch += [dma((rounds,))] * 2 + [dma((4, most))] * 2 + [dma((3,))] * 2
    scratch += job_scratch(sizes, jobs, INSIDE)
    anywhere, vmem = pl.BlockSpec(memory_space=pl.ANY), pl.BlockSpec(memory_space=pltpu.VMEM)
    units = [(ff, UNIT, 128), down_units.shape, (mixer, UNIT, 128), (out, UNIT, 128)]
    return pl.pallas_call(
        functools.partial(back_kernel, sizes, jobs, ticks, pieces),
        out_shape=[jax.ShapeDtypeStruct(x, F32) for x in ((2, width), (1, lanes), (1, cols))]
        + [jax.ShapeDtypeStruct((half, width), BF)] * 4 + [jax.ShapeDtypeStruct(x, BF) for x in units],
        in_specs=[anywhere] * (len(rows) + 1 + len(LOADED)),
        out_specs=[vmem] * 3 + [anywhere] * 8,
        scratch_shapes=scratch,
        compiler_params=pltpu.CompilerParams(collective_id=0, has_side_effects=True, vmem_limit_bytes=63 * 1024 * 1024),
        name="back",
    )(*rows, down_units, *[loaded[n] for n in LOADED])


def units_kernel(a_ref, b_ref, out_ref):
    part = tn(a_ref[...], b_ref[...]).astype(BF)
    for c in range(out_ref.shape[0]):
        out_ref[c] = part[:, c * 128 : (c + 1) * 128]


def outer_units(a, b, name):
    span, tall = a.shape
    steps = -(-b.shape[1] // 512)
    return pl.pallas_call(
        units_kernel,
        grid=(steps,),
        in_specs=[pl.BlockSpec((span, tall), lambda i: (0, 0)), pl.BlockSpec((span, 512), lambda i: (0, i))],
        out_specs=pl.BlockSpec((4, tall, 128), lambda i: (i, 0, 0)),
        out_shape=jax.ShapeDtypeStruct((4 * steps, tall, 128), BF),
        compiler_params=pltpu.CompilerParams(dimension_semantics=("arbitrary",), vmem_limit_bytes=VMEM_LIMIT),
        cost_estimate=pl.CostEstimate(flops=2 * span * tall * b.shape[1], bytes_accessed=8 << 20, transcendentals=0),
        name=name,
    )(a, b)


def widen_kernel(parts, *refs):
    for (which, blocks), out_ref in zip(parts, refs[-len(parts) :]):
        for c, block in enumerate(blocks):
            out_ref[:, c * 128 : (c + 1) * 128] = refs[which][block].astype(F32)


def widen(arrays, parts, steps):
    return pl.pallas_call(
        functools.partial(widen_kernel, parts),
        grid=(steps,),
        in_specs=[pl.BlockSpec((a.shape[0], a.shape[1] // steps, 128), lambda i: (0, i, 0)) for a in arrays],
        out_specs=[pl.BlockSpec((arrays[w].shape[1] // steps, len(b) * 128), lambda i: (i, 0)) for w, b in parts],
        out_shape=[jax.ShapeDtypeStruct((arrays[w].shape[1], len(b) * 128), F32) for w, b in parts],
        compiler_params=pltpu.CompilerParams(dimension_semantics=("arbitrary",), vmem_limit_bytes=VMEM_LIMIT),
        name="widen",
    )(*arrays)


X, Y, Z = 0, 1, 2
PIECES = 4
JOBS = (
    (2, 0, 3, (Y, X, Z)),
    (1, 0, 4, (X, Z, Y)),
    (1, 4, 3, (Y, X, Z)),
    (1, 7, 4, (Y, X, Z)),
    (3, 0, 2, (X, Z, Y)),
    (3, 2, 1, (Y, X, Z)),
    (2, 3, 3, (X, Y, Z)),
    (3, 3, 1, (X, Z, Y)),
    (2, 6, 4, (Y, Z, X)),
    (0, 0, 2, (Y, X, Z)),
    (2, 10, 3, (X, Y, Z)),
    (0, 2, 9, (Y, X, Z)),
    (0, 11, 5, (X, Y, Z)),
    (0, 16, 6, (X, Y, Z)),
)
TICKS = (
    ((1, 0), (2, 0), (3, 0),), (), (), ((2, 1),), (), ((1, 1),), (), (), ((2, 2),), ((3, 1),),
    ((1, 2), (9, 0), (12, 0),), ((2, 3), (3, 2), (1, 3), (11, 0),), ((9, 1), (1, 4), (13, 0),),
    ((2, 4), (12, 1), (3, 3), (9, 2), (5, 0),), (), (), ((11, 1), (13, 1), (1, 5),), ((2, 5),), (),
    ((12, 2), (3, 4),), ((5, 1), (9, 3),), (), ((0, 0),), ((11, 2), (13, 2), (6, 0),), ((12, 3), (8, 0),), ((10, 0),),
    ((9, 4),), ((2, 6),), ((1, 6),), ((4, 0),), ((3, 5),), ((11, 3),), ((0, 1),), ((7, 0),), ((5, 2),), ((13, 3),),
    ((6, 1),), ((8, 1),), ((12, 4),), ((10, 1),), ((9, 5),), ((3, 6),), ((4, 1),), ((6, 2),), ((11, 4),), ((5, 3),),
    ((0, 2),), ((7, 1),), ((12, 5),), ((13, 4),), ((10, 2),), ((9, 6),), ((11, 5),), ((8, 2),), ((13, 5),), ((4, 2),),
    ((6, 3),), ((12, 6),), ((5, 4),), ((8, 3),), ((0, 3),), ((7, 2),), ((10, 3),), ((6, 4),), ((11, 6),), ((13, 6),),
    ((4, 3),), ((7, 3),), ((5, 5),), ((0, 4),), ((8, 4),), ((6, 5),), ((4, 4),), ((10, 4),), ((7, 4),), ((0, 5),),
    ((5, 6),), ((10, 5),), ((6, 6),), ((8, 5),), ((0, 6),), ((4, 5),), ((10, 6),), ((7, 5),), ((4, 6),), ((8, 6),),
    ((7, 6),),
)


def call(kernel, count, ins, outs, scratch=(), tp=None, flops=0, moved=0, name=None):
    grid_spec = pltpu.PrefetchScalarGridSpec(
        num_scalar_prefetch=1,
        grid=(count,),
        in_specs=[pl.BlockSpec(block, index) for _, block, index in ins],
        out_specs=[pl.BlockSpec(block, index) for _, _, block, index in outs],
        scratch_shapes=list(scratch),
    )
    return pl.pallas_call(
        kernel,
        grid_spec=grid_spec,
        out_shape=[jax.ShapeDtypeStruct(shape, dtype) for shape, dtype, _, _ in outs],
        compiler_params=pltpu.CompilerParams(
            dimension_semantics=("arbitrary",), vmem_limit_bytes=VMEM_LIMIT
        ),
        cost_estimate=pl.CostEstimate(flops=flops, bytes_accessed=moved, transcendentals=0),
        name=name,
    )(tp, *[a for a, _, _ in ins])


def whole(array):
    return (array, array.shape, lambda i, tp: (0,) * array.ndim)


def rows_of(array):
    return (array, (CH, array.shape[1]), lambda i, tp: (i, 0))


def swap(x):
    return lax.ppermute(x, "tp", [(0, 1), (1, 0)])


def scan_states(total, fade, earlier):
    count = lax.axis_size("seq")
    index = lax.axis_index("seq")
    entering, entering_fade = jnp.zeros_like(total), jnp.ones_like(fade)
    for bit in range(count.bit_length() - 1):
        high = fade.astype(BF)
        sent = jnp.concatenate([total.astype(BF), high, (fade - high.astype(F32)).astype(BF)], 1)
        got = lax.ppermute(sent, "seq", [(i, i ^ (1 << bit)) for i in range(count)])
        width = total.shape[1]
        part = got[:, :width].astype(F32)
        part_fade = got[:, width : width + CH].astype(F32) + got[:, width + CH :].astype(F32)
        behind = ((index >> bit) & 1) == (1 if earlier else 0)
        entering = jnp.where(behind, entering_fade[:, :1] * part + entering, entering)
        entering_fade = jnp.where(behind, entering_fade * part_fade, entering_fade)
        total = jnp.where(behind, fade[:, :1] * part + total, part_fade[:, :1] * total + part)
        fade = fade * part_fade
    return entering


def token_code(lengths, positions):
    buckets = (lengths + BUCKET - 1) // BUCKET
    spans = buckets * BUCKET
    starts = jnp.cumsum(spans) - spans
    segment = jnp.sum((positions[:, None] >= starts[None, :]).astype(jnp.int32), axis=1) - 1
    picked = segment[:, None] == jnp.arange(lengths.shape[0], dtype=jnp.int32)[None, :]
    begin = jnp.sum(jnp.where(picked, starts[None, :], 0), axis=1)
    length = jnp.sum(jnp.where(picked, lengths[None, :], 0), axis=1)
    offset = positions - begin
    return jnp.where(offset == 0, 2.0, jnp.where(offset < length, 1.0, 0.0)).astype(F32)


def row_norm(x, gain):
    r = lax.rsqrt(jnp.mean(x * x, axis=-1, keepdims=True) + EPS)
    return x * r * gain


def row_norm_back(x, gain, grad):
    r = lax.rsqrt(jnp.mean(x * x, axis=-1, keepdims=True) + EPS)
    n = x * r
    u = grad * gain
    return r * (u - n * jnp.mean(u * n, axis=-1, keepdims=True)), jnp.sum(grad * n, axis=0)


def per_device(
    tokens, norm_gain, query_weight, key_weight, value_weight, forget_weight, forget_bias, head_gain,
    out_weight, feed_gain, gate_weight, up_weight, down_weight, lengths, cotangent,
):
    half, width = tokens.shape
    span = 2 * half
    count = span // CH
    cols = query_weight.shape[1]
    lanes = forget_weight.shape[1]
    tp = lax.axis_index("tp").astype(jnp.int32)[None]
    sums, pairs, flipped, back = tables()
    sums, back = jnp.asarray(sums, BF), jnp.asarray(back, BF)
    pairs, flipped = jnp.asarray(pairs), jnp.asarray(flipped)

    tokens_other, cot_other = swap(tokens), swap(cotangent)
    positions = lax.axis_index("seq") * span + jnp.arange(span, dtype=jnp.int32)
    code = jnp.broadcast_to(token_code(lengths, positions)[:, None], (span, lanes))
    half_map = lambda i, tp: (i % (count // 2), 0)
    own_map = lambda i, tp: (jnp.clip(i - tp[0] * (count // 2), 0, count // 2 - 1), 0)
    other_map = lambda i, tp: (jnp.clip(i - (1 - tp[0]) * (count // 2), 0, count // 2 - 1), 0)
    block = (CH, width)
    row = lambda n, d: ((span, n), d, (CH, n), lambda i, tp: (i, 0))
    fixed = lambda shape: (shape, F32, shape, lambda i, tp: (0,) * len(shape))

    xn, q, k, v, dsq, dsk, gate, weight, dzf, kv_run, fade_run = call(
        project_kernel, count,
        [(tokens, block, half_map), (tokens_other, block, half_map), whole(norm_gain[None]), whole(query_weight),
         whole(key_weight), whole(value_weight), whole(forget_weight), whole(forget_bias[None]), rows_of(code), whole(sums)],
        [row(width, BF)] + [row(cols, BF)] * 5 + [row(lanes, F32)] * 3 + [fixed((lanes, 2 * DH)), fixed((lanes, CH))],
        tp=tp, flops=2 * span * width * (3 * cols + lanes), moved=16 << 20, name="project",
    )

    kv_start = scan_states(kv_run, fade_run, True)

    logits, kvs, mixed, normed, attn_own, attn_other = call(
        mix_kernel, count,
        [rows_of(q), rows_of(k), rows_of(v), rows_of(gate), rows_of(weight), rows_of(code), whole(kv_start), whole(sums),
         whole(pairs), whole(head_gain[None]), whole(out_weight)],
        [row(lanes, F32), ((count, lanes, 2 * DH), BF, (1, lanes, 2 * DH), lambda i, tp: (i, 0, 0)), row(cols, F32),
         row(cols, BF), ((half, width), BF, block, own_map), ((half, width), BF, block, other_map)],
        scratch=[pltpu.VMEM((lanes, 2 * DH), F32)],
        tp=tp, flops=4 * span * width * cols, moved=16 << 20, name="mix",
    )

    own = tokens.astype(F32)
    resid = own + (attn_own.astype(F32) + swap(attn_other).astype(F32))
    hidden_own = row_norm(resid, feed_gain).astype(BF)
    hidden_other = swap(hidden_own)
    hidden = jnp.concatenate([hidden_own, hidden_other], 0)
    cot = jnp.concatenate([cotangent, cot_other], 0)
    ff_gate = dot(hidden, gate_weight)
    ff_up = dot(hidden, up_weight)
    dact = nt(cot, down_weight)
    sig = jax.nn.sigmoid(ff_gate)
    act = (ff_gate * sig * ff_up).astype(BF)
    dgate = (dact * ff_up * sig * (1.0 + ff_gate * (1.0 - sig))).astype(BF)
    dup = (dact * ff_gate * sig).astype(BF)
    feed = dot(act, down_weight).astype(BF)
    dhidden = (nt(dgate, gate_weight) + nt(dup, up_weight)).astype(BF)
    down_units = outer_units(act, cot, "down_units")

    dhidden_own = dhidden[:half].astype(F32) + swap(dhidden[half:]).astype(F32)
    dresid_norm, feed_gain_part = row_norm_back(resid, feed_gain, dhidden_own)
    dresid = cotangent.astype(F32) + dresid_norm
    loaded = dict(
        wo=out_weight, mixed=mixed, code=code, gain=head_gain[None], q=q, k=k, v=v, gate=gate, weight=weight, logits=logits,
        kvs=kvs, sums=sums, pairs=pairs, flipped=flipped, back=back, dsq=dsq, dsk=dsk, dzf=dzf,
        wq=query_weight, wk=key_weight, wv=value_weight, wf=forget_weight, xn=xn, normed=normed,
        kv_end=fade_run[:, :1] * kv_start + kv_run, norm_gain=norm_gain[None], feed_part=feed_gain_part[None],
    )
    rows = (dresid.astype(BF), hidden_own, hidden_other, dgate, dup, feed, resid, dresid, tokens)
    gains, bias_sum, head_sum, block_out, tokens_grad, _, _, *sums = back_call(
        rows, down_units.reshape(-1, UNIT, 128), loaded, JOBS, TICKS, PIECES
    )
    ff_sum, down_sum, mixer_sum, out_sum = sums
    blocks, ff_blocks, wide = cols // 128, gate_weight.shape[1] // 128, tuple(range(width // 128))
    which = lambda up: tuple(4 * (c // 2) + 2 * up + c % 2 - (up if c == ff_blocks - 1 else 0) for c in range(ff_blocks))
    parts = [(0, tuple(range(i * blocks, (i + 1) * blocks))) for i in range(3)] + [(0, (3 * blocks,)), (1, wide)]
    parts += [(2, which(0)), (2, which(1)), (3, wide)]
    arrays = [mixer_sum, out_sum.reshape(-1, cols, 128), ff_sum, down_sum.reshape(-1, down_weight.shape[0], 128)]
    query_sum, key_sum, value_sum, forget_sum, out_grad, gate_grad, up_grad, down_grad = widen(arrays, parts, 8)
    return (
        block_out, tokens_grad, gains[0], query_sum, key_sum, value_sum, forget_sum, bias_sum[0], head_sum[0], out_grad,
        gains[1], gate_grad, up_grad, down_grad,
    )


def solution(mesh):
    rows, by_col, by_row = P(("seq", "tp"), None), P(None, "tp"), P("tp", None)
    return jax.shard_map(
        per_device,
        mesh=mesh,
        in_specs=(
            rows, P(), by_col, by_col, by_col, by_col, P("tp"), P("tp"), by_row, P(), by_col, by_col, by_row, P(), rows,
        ),
        out_specs=(
            rows, rows, P(), by_col, by_col, by_col, by_col, P("tp"), P("tp"), by_row, P(), by_col, by_col, by_row,
        ),
        check_vma=False,
    )
```

```python
import functools

import jax
import jax.numpy as jnp
import numpy as np
from jax import lax
from jax.experimental import pallas as pl
from jax.experimental.pallas import tpu as pltpu
from jax.sharding import PartitionSpec as P

DH = 256
SLOTS = 64
BUCKET = 64
CH = 128
BASE = 8
HALVES = (64, 32, 16, 8)
RESET_LOG = -16384.0
LIFT = 2.0**20
SCALE = DH**-0.5

EPS = 1e-06
NORMALIZER = 8.0

BF = jnp.bfloat16
F32 = jnp.float32
VMEM_LIMIT = 56 * 1024 * 1024
UNIT = 1024
MESH = pl.DeviceIdType.MESH


def dot(a, b):
    return lax.dot_general(a, b, (((1,), (0,)), ((), ())), preferred_element_type=F32)


def nt(a, b):
    return lax.dot_general(a, b, (((1,), (1,)), ((), ())), preferred_element_type=F32)


def tn(a, b):
    return lax.dot_general(a, b, (((0,), (0,)), ((), ())), preferred_element_type=F32)


def tables():
    t, u = np.arange(CH)[:, None], np.arange(CH)[None, :]
    sums, pairs = [u <= t, u > t], []
    for half in HALVES:
        mid = t // (2 * half) * (2 * half) + half
        sums.append(np.where(t >= mid, (u >= mid) & (u <= t), (u > t) & (u < mid)))
        pairs.append(
            (t // (2 * half) == u // (2 * half)) & (t % (2 * half) >= half) & (u % (2 * half) < half)
        )
    ref = t // BASE * BASE + BASE // 2 - 1
    sums.append(((u > ref) & (u <= t)).astype(int) - ((u > t) & (u <= ref)).astype(int))
    pairs.append((t // BASE == u // BASE) & (u <= t))
    stacked = np.concatenate([s.astype(np.float32) for s in sums], 0)
    return (
        np.concatenate([stacked] * 3, 1),
        np.stack(pairs).astype(np.float32),
        np.stack([p.T for p in pairs]).astype(np.float32),
        np.concatenate([stacked.T] * 2, 1),
    )


def split3(x):
    high = x.astype(BF)
    rest = x - high.astype(F32)
    middle = rest.astype(BF)
    low = (rest - middle.astype(F32)).astype(BF)
    return jnp.concatenate([high, middle, low], 0)


def split2(x):
    high = x.astype(BF)
    return jnp.concatenate([high, (x - high.astype(F32)).astype(BF)], 0)


def decays(gate, weight, sums_ref):
    sums = dot(sums_ref[...], split3(gate))
    part = [sums[i * CH : (i + 1) * CH] for i in range(3 + len(HALVES))]
    first, last = jnp.exp(part[0]), jnp.exp(part[1])
    rows = [jnp.exp(p) for p in part[2:-1]]
    cols = [r * weight for r in rows]
    slopes = list(rows)
    rows.append(jnp.exp(part[-1]) * LIFT)
    slopes.append(jnp.exp(-part[-1]) * (1 / LIFT))
    cols.append(slopes[-1] * weight)
    return first, last, rows, cols, slopes


def halves(x):
    left = lax.broadcasted_iota(jnp.int32, x.shape, 1) < SLOTS
    zero = jnp.zeros_like(x)
    return jnp.where(left, x, zero), jnp.where(left, zero, x)


def head(x, h):
    return x[:, h * DH : (h + 1) * DH]


def slots(x, h):
    return x[:, h * SLOTS : (h + 1) * SLOTS]


def state(x, h):
    return x[h * SLOTS : (h + 1) * SLOTS]


def through(pairwise, rows, cols, pairs_ref):
    total = None
    for i in range(len(rows)):
        keep = pairs_ref[i].astype(F32) != 0
        left = jnp.concatenate([jnp.where(keep, p, 0.0).astype(BF) for p in pairwise], 1)
        right = jnp.concatenate(halves(cols[i].astype(BF)), 0)
        term = rows[i] * dot(left, right)
        total = term if total is None else total + term
    return total


def back_through(values, rows, cols, pairs_ref):
    totals = None
    for i in range(len(rows)):
        keep = pairs_ref[i].astype(F32) != 0
        stack = [part for v in values for part in halves((v * rows[i]).astype(BF))]
        out = nt(jnp.concatenate(stack, 0), cols[i].astype(BF))
        terms = [jnp.where(keep, out[n * CH : (n + 1) * CH], 0.0) for n in range(len(stack))]
        totals = terms if totals is None else [a + b for a, b in zip(totals, terms)]
    return totals


def softmax2(logits):
    out = []
    for h in range(2):
        x = slots(logits, h) * SCALE
        e = jnp.exp(x - jnp.max(x, axis=-1, keepdims=True))
        out.append(e / jnp.sum(e, axis=-1, keepdims=True))
    return jnp.concatenate(out, 1)


def fade_of(gate):
    return jnp.exp(jnp.sum(gate.T, axis=1, keepdims=True))


def run_part(trail, keys, values):
    return jnp.concatenate(
        [
            jnp.concatenate([tn(slots(trail, h), head(keys, h)), tn(slots(trail, h), head(values, h))], 1)
            for h in range(2)
        ],
        0,
    )


def state_grads(dl, probs, first, q, dmix):
    a, b = (dl * first).astype(BF), (probs * first).astype(BF)
    return jnp.concatenate(
        [jnp.concatenate([tn(slots(a, h), head(q, h)), tn(slots(b, h), head(dmix, h))], 1) for h in range(2)], 0
    )


def line_sizes(count):
    return {16: (2, 2, 4), 64: (4, 4, 4)}.get(count, (count, 1, 1))


class Lines:
    def __init__(self, sizes):
        self.sizes = sizes
        self.index = lax.axis_index("seq")
        self.half = lax.axis_index("tp")
        self.strides = (1, sizes[0], sizes[0] * sizes[1])
        self.place = [lax.rem(self.index // s, m) for s, m in zip(self.strides, sizes)]

    def peer(self, axis, d):
        m = self.sizes[axis]
        return self.index + (lax.rem(self.place[axis] + d, m) - self.place[axis]) * self.strides[axis]

    def greet(self):
        barrier = pltpu.get_barrier_semaphore()
        count = 1
        pl.semaphore_signal(barrier, inc=1, device_id={"tp": 1 - self.half}, device_id_type=MESH)
        for axis in range(3):
            for d in range(1, self.sizes[axis]):
                pl.semaphore_signal(barrier, inc=1, device_id={"seq": self.peer(axis, d)}, device_id_type=MESH)
                count += 1
        pl.semaphore_wait(barrier, count)


def remote(src, dst, sems, at, device):
    return pltpu.make_async_remote_copy(
        src_ref=src, dst_ref=dst, send_sem=sems[0].at[at], recv_sem=sems[1].at[at], device_id=device, device_id_type=MESH
    )


def job_scratch(sizes, jobs, inside):
    scratch = []
    for a, _, units, order in jobs:
        rows = UNIT
        if not inside[a]:
            scratch.append(pltpu.VMEM((units, UNIT // sizes[order[0]], 128), BF))
        for axis in order:
            rows = rows // sizes[axis]
            scratch.append(pltpu.VMEM((max(sizes[axis] - 1, 1), units, rows, 128), BF))
    most = max(max(sizes) - 1, 1)
    return scratch + [pltpu.SemaphoreType.DMA((len(jobs), 6, most))] * 2 + [pltpu.SemaphoreType.DMA((len(jobs), 2))]


class Jobs:
    def __init__(self, lines, jobs, ins, outs, inside, scratch):
        self.lines, self.jobs, self.ins, self.outs, self.inside = lines, jobs, ins, outs, inside
        self.sems, self.local = scratch[-3:-1], scratch[-1]
        self.mine, self.held, self.got, self.shape = [], [], [], []
        scratch = list(scratch)
        for j, (a, _, _, order) in enumerate(jobs):
            rows, offset, shape = UNIT, 0, []
            for axis in order:
                rows = rows // lines.sizes[axis]
                mine = lines.place[axis] * rows
                offset = offset + mine
                shape.append((axis, rows, pl.multiple_of(mine, 16), pl.multiple_of(offset, 16)))
            self.shape.append(shape)
            self.mine.append(None if inside[a] else scratch.pop(0))
            self.got.append([scratch.pop(0) for _ in range(3)])
            self.held.append([got.at[0] for got in self.got[j]])

    def copies(self, j, s):
        lines, (a, first, units, _) = self.lines, self.jobs[j]
        stage = s if s < 3 else 5 - s
        axis, rows, _, offset = self.shape[j][stage]
        out = []
        for d in range(1, lines.sizes[axis]):
            if s < 3:
                target = pl.multiple_of(lax.rem(lines.place[axis] + d, lines.sizes[axis]) * rows, 16)
                if s == 0:
                    src = self.ins[a].at[pl.ds(first, units), pl.ds(target, rows), :]
                else:
                    src = self.held[j][s - 1].at[:, pl.ds(target, rows), :]
                dst = self.got[j][s].at[d - 1]
            else:
                dst = self.outs[a].at[pl.ds(first, units), pl.ds(offset, rows), :]
                src = self.held[j][2] if s == 3 else dst
            out.append(remote(src, dst, self.sems, (j, s, d - 1), {"seq": lines.peer(axis, d)}))
        return out

    def own(self, j):
        a, first, units, _ = self.jobs[j]
        _, rows, mine, _ = self.shape[j][0]
        src = self.ins[a].at[pl.ds(first, units), pl.ds(mine, rows), :]
        return pltpu.make_async_copy(src, self.mine[j], self.local.at[j, 0])

    def home(self, j):
        a, first, units, _ = self.jobs[j]
        _, rows, _, offset = self.shape[j][2]
        dst = self.outs[a].at[pl.ds(first, units), pl.ds(offset, rows), :]
        return pltpu.make_async_copy(self.held[j][2], dst, self.local.at[j, 1])

    def add(self, j, stage):
        a, first, units, _ = self.jobs[j]
        axis, rows, mine, _ = self.shape[j][stage]
        held, got = self.held[j], self.got[j]

        def one(u, carry):
            if stage > 0:
                total = held[stage - 1][u, pl.ds(mine, rows), :].astype(F32)
            elif self.inside[a]:
                total = self.ins[a][first + u, pl.ds(mine, rows), :].astype(F32)
            else:
                total = self.mine[j][u].astype(F32)
            for d in range(self.lines.sizes[axis] - 1):
                total = total + got[stage][d, u].astype(F32)
            held[stage][u] = total.astype(BF)
            return carry

        lax.fori_loop(0, units, one, 0)

    def step(self, j, s):
        if s == 0 and not self.inside[self.jobs[j][0]]:
            self.own(j).start()
        if s == 1 and not self.inside[self.jobs[j][0]]:
            self.own(j).wait()
        if s == 4:
            self.home(j).wait()
        if s > 0:
            for copy in self.copies(j, s - 1):
                copy.wait_recv()
        if 1 <= s <= 3:
            self.add(j, s - 1)
        if s == 3:
            self.home(j).start()
        if s < 6:
            for copy in self.copies(j, s):
                copy.start()

    def finish(self):
        for j in range(len(self.jobs)):
            for s in range(6):
                for copy in self.copies(j, s):
                    copy.wait_send()


def scan_lines(lines, total_ref, fade_ref, enter_ref, reach_ref, sent_ref, got_ref, sems, earlier, between):
    width = total_ref.shape[1]
    enter_ref[...] = jnp.zeros_like(enter_ref)
    reach_ref[...] = jnp.ones_like(reach_ref)
    count = lines.sizes[0] * lines.sizes[1] * lines.sizes[2]
    rounds = count.bit_length() - 1
    side = [lax.rem(lines.index // (1 << bit), 2) for bit in range(rounds)]

    def copy(bit):
        partner = lines.index + (1 - 2 * side[bit]) * (1 << bit)
        return remote(sent_ref.at[bit], got_ref.at[bit], sems, bit, {"seq": partner})

    for bit in range(rounds):
        fade = fade_ref[...]
        high = fade.astype(BF)
        sent_ref[bit, :, :width] = total_ref[...].astype(BF)
        sent_ref[bit, :, width : width + CH] = high
        sent_ref[bit, :, width + CH :] = (fade - high.astype(F32)).astype(BF)
        copy(bit).start()
        between(bit)
        copy(bit).wait_recv()
        part = got_ref[bit, :, :width].astype(F32)
        part_fade = got_ref[bit, :, width : width + CH].astype(F32) + got_ref[bit, :, width + CH :].astype(F32)
        behind = side[bit] == (1 if earlier else 0)
        enter, reach, total = enter_ref[...], reach_ref[...], total_ref[...]
        enter_ref[...] = jnp.where(behind, reach[:, :1] * part + enter, enter)
        reach_ref[...] = jnp.where(behind, reach * part_fade, reach)
        total_ref[...] = jnp.where(behind, fade[:, :1] * part + total, part_fade[:, :1] * total + part)
        fade_ref[...] = fade * part_fade
    return [copy(bit) for bit in range(rounds)]


def chunk_rows(c):
    return pl.ds(pl.multiple_of(c * CH, CH), CH)


def score_chunk(c, s):
    at = chunk_rows(c)
    dnormed = nt(s.da[at], s.wo[...])
    dnormed = jnp.where(s.code[at, :1] > 0.5, dnormed, 0.0)
    dmix = []
    for h in range(2):
        mixed = s.mixed[at, h * DH : (h + 1) * DH]
        r = lax.rsqrt(jnp.mean(mixed * mixed, axis=-1, keepdims=True) + EPS)
        n = mixed * r
        d = head(dnormed, h)
        u = d * s.gain[:, h * DH : (h + 1) * DH]
        s.gain_grad[:, h * DH : (h + 1) * DH] += jnp.sum(d * n, axis=0, keepdims=True)
        dmix.append(r * (u - n * jnp.mean(u * n, axis=-1, keepdims=True)))
    wide = jnp.concatenate(dmix, 1)
    dmix = wide.astype(BF)
    s.dmix[at] = dmix
    rest = (wide - dmix.astype(F32)).astype(BF)
    exact = [jnp.concatenate([head(dmix, h), head(rest, h)], 0) for h in range(2)]
    q, v = s.q[at], s.v[at]
    gate, weight = s.gate[at], s.weight[at]
    first, _, rows, cols, _ = decays(gate, weight, s.sums)
    logits = s.logits[at]
    probs = softmax2(logits)
    low = s.kvs[c]
    fold = lambda x: x[:CH] + x[CH:]
    reads = [fold(nt(exact[h], head(v, h))) for h in range(2)]
    outer = jnp.concatenate([fold(nt(exact[h], state(low, h)[:, DH:])) for h in range(2)], 1)
    dprobs = first * outer + through(reads, rows, cols, s.pairs)
    weighted = probs * dprobs
    sums = [
        jnp.broadcast_to(jnp.sum(slots(weighted, h), axis=-1, keepdims=True), (CH, SLOTS)) for h in range(2)
    ]
    dl = (weighted - probs * jnp.concatenate(sums, 1)) * SCALE
    s.dl[at] = dl
    part = state_grads(dl, probs, first, q, dmix)
    reach = s.fade[...]
    s.dkv[...] += jnp.concatenate([reach] * (s.dkv.shape[1] // reach.shape[1]), 1) * part
    s.fade[...] = reach * fade_of(gate)


def grad_chunk(c, s):
    at = chunk_rows(c)
    q, k, v, dmix = s.q[at], s.k[at], s.v[at], s.dmix[at]
    gate, weight = s.gate[at], s.weight[at]
    dl = s.dl[at]
    first, last, rows, cols, slopes = decays(gate, weight, s.sums)
    probs = softmax2(s.logits[at])
    low, dkv = s.kvs[c], s.enter[...]
    dlow = dkv.astype(BF)
    r0, r1, s0, s1 = back_through([probs, dl], rows, cols, s.pairs)
    turned = [nt(head(a, h), head(b, h)) for h in range(2) for a, b in ((k, q), (v, dmix))]
    dw = last * jnp.concatenate(
        [nt(jnp.concatenate([head(k, h), head(v, h)], 1), state(dlow, h)) for h in range(2)], 1
    )
    parts = [None, weight * dw]
    scores = [nt(head(q, h), head(k, h)) for h in range(2)]
    reads = [nt(head(dmix, h), head(v, h)) for h in range(2)]
    outer = [
        jnp.concatenate([nt(head(x, h), state(low, h)[:, at_state]) for h in range(2)], 1)
        for x, at_state in ((q, slice(0, DH)), (dmix, slice(DH, 2 * DH)))
    ]
    parts[0] = first * (dl * outer[0] + probs * outer[1])
    for i in range(len(rows)):
        keep = s.flipped[i].astype(F32) != 0
        left = jnp.concatenate([jnp.where(keep, x, 0.0).astype(BF) for x in turned], 1)
        a, b = halves((dl * rows[i]).astype(BF)), halves((probs * rows[i]).astype(BF))
        late = slopes[i] * dot(left, jnp.concatenate([a[0], b[0], a[1], b[1]], 0))
        dw = dw + late
        keep = s.pairs[i].astype(F32) != 0
        left = [jnp.concatenate([jnp.where(keep, x, 0.0).astype(BF) for x in both], 1) for both in (scores, reads)]
        early = dot(jnp.concatenate(left, 0), jnp.concatenate(halves(cols[i].astype(BF)), 0))
        early = rows[i] * (dl * early[:CH] + probs * early[CH:])
        parts.append(early + weight * late if i < len(HALVES) else early - weight * late)
    trail = (last * weight).astype(BF)
    spread = (dl * first).astype(BF)
    reading, dscore = [r0.astype(BF), r1.astype(BF)], [s0.astype(BF), s1.astype(BF)]
    dq, dk, dv = [], [], []
    for h in range(2):
        dq.append(dot(dscore[h], head(k, h)) + dot(slots(spread, h), state(low, h)[:, :DH]))
        dk.append(tn(dscore[h], head(q, h)) + dot(slots(trail, h), state(dlow, h)[:, :DH]))
        dv.append(tn(reading[h], head(dmix, h)) + dot(slots(trail, h), state(dlow, h)[:, DH:]))
    dq = (jnp.concatenate(dq, 1) * s.dsq[at].astype(F32)).astype(BF)
    dk = (jnp.concatenate(dk, 1) * s.dsk[at].astype(F32)).astype(BF)
    dv = jnp.concatenate(dv, 1).astype(BF)
    fade = fade_of(gate)
    across = jnp.sum(fade * low.astype(F32) * dkv, axis=1, keepdims=True)
    across = jnp.broadcast_to(across, (across.shape[0], CH)).T[:1]
    flow = dot(s.back[...], split2(jnp.concatenate(parts, 0))) + across
    df = ((flow - jnp.exp(gate) * dw) * s.dzf[at]).astype(BF)
    s.d_all[at] = jnp.concatenate([dq, dk, dv, df], 1)
    s.bias_grad[...] += jnp.sum(df.astype(F32), axis=0, keepdims=True)
    s.enter[...] = fade * dkv + state_grads(dl, probs, first, q, dmix)
    dx = nt(dq, s.wq[...]) + nt(dk, s.wk[...]) + nt(dv, s.wv[...]) + nt(df, s.wf[...])
    s.norm_grad[...] += jnp.sum(dx * s.xn[at].astype(F32), axis=0, keepdims=True)
    s.dx[at] = dx.astype(BF)


class Bag:
    pass


LOADED = (
    "wo", "mixed", "code", "gain", "q", "k", "v", "gate", "weight", "logits", "kvs", "sums", "pairs", "flipped", "back",
    "dsq", "dsk", "dzf", "wq", "wk", "wv", "wf", "normed", "norm_gain", "feed_gain",
)


FF_STEPS = ((0, 1), (2, 3), (4,), (5,))
INSIDE = (True, True, True, True)
ROWS = 128


def back_kernel(sizes, jobs, ticks, pieces, *refs):
    refs = list(refs)
    take = lambda n: [refs.pop(0) for _ in range(n)]
    dh_own, dh_got, act, cot, hn, dgate, dup, down_weight, resid, tokens, xn = take(11)
    sources = take(len(LOADED))
    gains_out, bias_out, head_out, block_out, tokens_out, feed_got, dx_got, dresid, *outs = take(12)
    s = Bag()
    for name in LOADED:
        setattr(s, name, refs.pop(0))
    for name in ("hn", "da", "dmix", "dl", "wide_grads", "gain_grad", "bias_grad", "norm_grad", "dkv", "fade", "enter",
                 "reach", "ff_units", "down_units", "mixer_units", "out_units", "feed_part", "sent", "got", "small_held", "small_got",
                 "wide", "narrow", "result"):
        setattr(s, name, refs.pop(0))
    s.dx = s.da
    hidden = dgate.shape[1]
    s.dgate, s.dup = s.wide_grads.at[:, :hidden], s.wide_grads.at[:, hidden:]
    s.d_all = s.wide_grads.at[:, : 3 * s.wq.shape[1] + s.wf.shape[1]]
    load_sem, row_sem, piece_sem, feed_sem = take(4)
    scan_sems, small_sems, swap_sems = take(2), take(2), take(2)
    lines = Lines(sizes)
    half, width = dh_own.shape
    count = 2 * half // CH
    tp_peer = {"tp": 1 - lines.half}

    other_rows = pl.ds(pl.multiple_of((1 - lines.half) * half, half), half)
    early = [
        pltpu.make_async_copy(act, s.wide_grads.at[:, :hidden], row_sem.at[0]),
        pltpu.make_async_copy(cot, s.wide_grads.at[:, hidden : hidden + width], row_sem.at[1]),
    ]
    loads = [pltpu.make_async_copy(x, getattr(s, n), load_sem.at[i]) for i, (n, x) in enumerate(zip(LOADED, sources))]
    late = [
        pltpu.make_async_copy(hn, s.hn, row_sem.at[2]),
        pltpu.make_async_copy(dgate, s.dgate, row_sem.at[3]),
        pltpu.make_async_copy(dup, s.dup, row_sem.at[4]),
    ]
    for copy in early + loads + late[:1]:
        copy.start()
    for ref in (s.gain_grad, s.bias_grad, s.norm_grad, s.feed_part, s.dkv):
        ref[...] = jnp.zeros_like(ref)
    s.fade[...] = jnp.ones_like(s.fade)
    lines.greet()
    dx_swap = remote(s.dx.at[other_rows], dx_got, swap_sems, 0, tp_peer)
    work = Jobs(
        lines, jobs, [s.ff_units, s.down_units, s.mixer_units, s.out_units], outs, INSIDE, refs
    )
    pending = [list(t) for t in ticks]

    def tick():
        for j, step in pending.pop(0):
            work.step(j, step)

    def loop(body):
        todo = [pending.pop(0) for _ in range(count)]

        def one(i, carry):
            body(i)
            for k, steps in enumerate(todo):
                if steps:

                    @pl.when(i == k)
                    def _():
                        for j, step in steps:
                            work.step(j, step)

            return carry

        lax.fori_loop(0, count, one, 0)

    for copy in early:
        copy.wait()

    def down_part(n):
        part = tn(s.wide_grads[:, :hidden], s.wide_grads[:, hidden + n * 256 : hidden + (n + 1) * 256]).astype(BF)
        for c in range(2):
            row, done = (2 * n + c) * hidden, 0
            while done < hidden:
                some = min(hidden - done, UNIT - (row + done) % UNIT)
                at = (row + done) % UNIT
                s.down_units[(row + done) // UNIT, at : at + some] = part[done : done + some, c * 128 : (c + 1) * 128]
                done += some

    def row_loads(n):
        at, slot = pl.ds(n * ROWS, ROWS), n % 2
        return [
            pltpu.make_async_copy(src.at[at], dst, piece_sem.at[n, 8 + i])
            for i, (src, dst) in enumerate(
                ((resid, s.wide.at[slot]), (dh_own, s.narrow.at[slot]), (dh_got, s.narrow.at[2 + slot]))
            )
        ]

    def mine(n):
        return pl.ds(pl.multiple_of(lines.half * half + n * ROWS, ROWS), ROWS)

    def dresid_save(n):
        return pltpu.make_async_copy(s.wide.at[n % 2], dresid.at[pl.ds(n * ROWS, ROWS)], piece_sem.at[n, 11])

    def row_grads(n):
        slot = n % 2
        for copy in row_loads(n):
            copy.wait()
        x = s.wide[slot]
        r = lax.rsqrt(jnp.mean(x * x, axis=-1, keepdims=True) + EPS)
        norm = x * r
        dh = s.narrow[slot].astype(F32) + s.narrow[2 + slot].astype(F32)
        s.feed_part[...] += jnp.sum(dh * norm, axis=0, keepdims=True)
        u = dh * s.feed_gain[...]
        full = s.wide_grads[n * ROWS : (n + 1) * ROWS, hidden : hidden + width].astype(F32)
        full = full + r * (u - norm * jnp.mean(u * norm, axis=-1, keepdims=True))
        s.wide[slot] = full
        s.da[mine(n)] = full.astype(BF)
        dresid_save(n).start()

    steps = half // ROWS
    da_swaps = [remote(s.da.at[mine(n)], s.da.at[mine(n)], swap_sems, 1 + n, tp_peer) for n in range(steps)]
    for n in range(2):
        for copy in row_loads(n):
            copy.start()
    for copy in loads:
        copy.wait()
    for n in range(steps):
        row_grads(n)
        da_swaps[n].start()
        down_part(n)
        dresid_save(n).wait()
        if n + 2 < steps:
            for copy in row_loads(n + 2):
                copy.start()
        tick()
    for copy in late[1:]:
        copy.start()
    for copy in da_swaps:
        copy.wait_recv()
    loop(lambda i: score_chunk(i, s))
    for copy in da_swaps:
        copy.wait_send()
    for copy in late:
        copy.wait()

    def out_part(n):
        wide = width // 4
        part = tn(s.normed[...], s.da[:, n * wide : (n + 1) * wide]).astype(BF)
        tall = part.shape[0]
        for c in range(wide // 128):
            row = (n * (wide // 128) + c) * tall
            s.out_units[row // UNIT, row % UNIT : row % UNIT + tall] = part[:, c * 128 : (c + 1) * 128]

    def ff_part(n):
        at = slice(n * 256, min((n + 1) * 256, s.dgate.shape[1]))
        part = tn(s.hn[...], jnp.concatenate([s.dgate[:, at], s.dup[:, at]], 1)).astype(BF)
        for c in range(part.shape[1] // 128):
            s.ff_units[4 * n + c] = part[:, c * 128 : (c + 1) * 128]

    def between(n):
        if n < 4:
            out_part(n)
            for m in FF_STEPS[n]:
                ff_part(m)
            if n == 3:
                xn_load.start()
            tick()

    xn_load = pltpu.make_async_copy(xn, s.hn, row_sem.at[5])

    scans = scan_lines(lines, s.dkv, s.fade, s.enter, s.reach, s.sent, s.got, scan_sems, False, between)
    xn_load.wait()
    s.xn = s.hn
    loop(lambda i: grad_chunk(count - 1 - i, s))
    dx_swap.start()

    lanes = s.bias_grad.shape[1]
    vectors = [s.norm_grad[...] / s.norm_gain[...], s.feed_part[...], s.bias_grad[...], s.gain_grad[...]]
    row = 0
    for v in vectors:
        for c in range(v.shape[1] // lanes):
            s.small_held[0, row : row + 1] = v[:, c * lanes : (c + 1) * lanes]
            row += 1
    s.small_held[0, row:] = jnp.zeros_like(s.small_held[0, row:])

    def small_copies(n):
        if n == 3:
            return [remote(s.small_held.at[3], s.small_got.at[3, 0], small_sems, (3, 0), tp_peer)]
        return [
            remote(s.small_held.at[n], s.small_got.at[n, d - 1], small_sems, (n, d - 1), {"seq": lines.peer(n, d)})
            for d in range(1, sizes[n])
        ]

    def small_step(n):
        if n > 0:
            for copy in small_copies(n - 1):
                copy.wait_recv()
            total = s.small_held[n - 1]
            if n <= 3:
                for d in range(sizes[n - 1] - 1):
                    total = total + s.small_got[n - 1, d]
                s.small_held[n] = total
            else:
                both = total + s.small_got[3, 0]
                wide = width // lanes
                for c in range(2 * wide):
                    gains_out[c // wide : c // wide + 1, (c % wide) * lanes : (c % wide + 1) * lanes] = both[c : c + 1]
                bias_out[...] = total[2 * wide : 2 * wide + 1]
                for c in range(head_out.shape[1] // lanes):
                    head_out[:, c * lanes : (c + 1) * lanes] = total[2 * wide + 1 + c : 2 * wide + 2 + c]
        if n <= 3:
            for copy in small_copies(n):
                copy.start()

    most = s.wide_grads.shape[0]
    weight_loads = [
        pltpu.make_async_copy(down_weight.at[:most], s.wide_grads.at[:, :width], row_sem.at[6]),
        pltpu.make_async_copy(
            down_weight.at[most:], s.wide_grads.at[: hidden - most, width : 2 * width], row_sem.at[7]
        ),
    ]
    feed_rows = 2 * ROWS
    act_at, feed_at = hidden - most, hidden - most + feed_rows
    feed_ref = s.wide_grads.at[feed_at : feed_at + feed_rows, width : 2 * width]

    def feed_swap(n):
        return remote(feed_ref, feed_got.at[pl.ds(n * feed_rows, feed_rows)], swap_sems, 1 + steps + n, tp_peer)

    def feed_part(n):
        there = n < half // feed_rows
        start = (half if there else 0) + n % (half // feed_rows) * feed_rows
        load = pltpu.make_async_copy(
            act.at[start : start + feed_rows], s.wide_grads.at[act_at : act_at + feed_rows, width : width + hidden],
            feed_sem.at[n],
        )
        load.start()
        if n == 0:
            for copy in weight_loads:
                copy.wait()
        load.wait()
        left = s.wide_grads[act_at : act_at + feed_rows, width : width + hidden]
        part = dot(left[:, :most], s.wide_grads[:, :width])
        part = part + dot(left[:, most:], s.wide_grads[: hidden - most, width : 2 * width])
        if 0 < n <= half // feed_rows:
            feed_swap(n - 1).wait_send()
        s.wide_grads[feed_at : feed_at + feed_rows, width : 2 * width] = part.astype(BF)
        if there:
            feed_swap(n).start()

    def piece(n):
        if n == 0:
            for m in range(half // feed_rows):
                feed_swap(m).wait_recv()
        at = pl.ds(n * ROWS, ROWS)
        copies = [
            pltpu.make_async_copy(src.at[at], dst, piece_sem.at[n, i])
            for i, (src, dst) in enumerate(
                ((resid, s.wide.at[0]), (dresid, s.wide.at[1]), (tokens, s.narrow.at[0]), (feed_got, s.narrow.at[2]),
                 (dx_got, s.narrow.at[3]))
            )
        ]
        for copy in copies:
            copy.start()
        for copy in copies:
            copy.wait()
        lo = feed_at + n % 2 * ROWS
        feed = s.wide_grads[lo : lo + ROWS, width : 2 * width].astype(F32) + s.narrow[2].astype(F32)
        s.result[0] = (s.wide[0] + feed).astype(BF)
        dx = s.dx[mine(n)].astype(F32) + s.narrow[3].astype(F32)
        x = s.narrow[0].astype(F32)
        r = lax.rsqrt(jnp.mean(x * x, axis=-1, keepdims=True) + EPS)
        norm = x * r
        u = dx * s.norm_gain[...]
        s.result[1] = (s.wide[1] + r * (u - norm * jnp.mean(u * norm, axis=-1, keepdims=True))).astype(BF)
        ends = [
            pltpu.make_async_copy(s.result.at[i], out.at[at], piece_sem.at[n, 6 + i])
            for i, out in enumerate((block_out, tokens_out))
        ]
        for copy in ends:
            copy.start()
        for copy in ends:
            copy.wait()

    blocks = s.d_all.shape[1] // 128
    for n in range(-(-blocks // 4)):
        some = min(4, blocks - 4 * n)
        part = tn(s.xn[...], s.d_all[:, n * 512 : n * 512 + some * 128]).astype(BF)
        for c in range(some):
            s.mixer_units[4 * n + c] = part[:, c * 128 : (c + 1) * 128]
        small_step(n)
        tick()
    for copy in weight_loads:
        copy.start()
    dx_swap.wait()
    extras = [lambda n=n: feed_part(n) for n in range(half // feed_rows)]
    for n in range(half // feed_rows):
        extras.append(lambda n=n: feed_part(half // feed_rows + n))
        extras += [lambda m=m: piece(m) for m in (2 * n, 2 * n + 1)]
    step = 0
    while pending:
        tick()
        step += 1
        if step == 1:
            small_step(4)
        if extras and step % pieces == 0:
            extras.pop(0)()
    for extra in extras:
        extra()
    for copy in scans + [c for n in range(4) for c in small_copies(n)]:
        copy.wait_send()
    work.finish()


def back_call(rows, loaded, jobs, ticks, pieces):
    sizes = line_sizes(lax.axis_size("seq"))
    rounds = (sizes[0] * sizes[1] * sizes[2]).bit_length() - 1
    most = max(max(sizes) - 1, 1)
    half, width = rows[0].shape
    span, hidden = 2 * half, rows[2].shape[1]
    lanes, cols = loaded["wf"].shape[1], loaded["wq"].shape[1]
    small = (2 * width + lanes + cols) // lanes
    small = (small + -small % 8, lanes)
    mixer, ff = (3 * cols + lanes) // 128, 2 * hidden // 128
    out, down = (n * width // 128 // UNIT for n in (cols, hidden))
    shapes = [
        ((span, width), BF), ((span, width), BF), ((span, cols), BF), ((span, lanes), F32),
        ((span, 2 * hidden), BF), ((1, cols), F32), ((1, lanes), F32), ((1, width), F32), ((lanes, 2 * DH), F32),
        ((lanes, CH), F32), ((lanes, 2 * DH), F32), ((lanes, CH), F32), ((ff, UNIT, 128), BF),
        ((down, UNIT, 128), BF), ((mixer, UNIT, 128), BF), ((out, UNIT, 128), BF), ((1, width), F32), ((rounds, lanes, 2 * DH + 2 * CH), BF),
        ((rounds, lanes, 2 * DH + 2 * CH), BF), ((4, *small), F32), ((4, most, *small), F32), ((2, ROWS, width), F32),
        ((4, ROWS, width), BF), ((2, ROWS, width), BF),
    ]
    dma = pltpu.SemaphoreType.DMA
    scratch = [pltpu.VMEM(loaded[n].shape, loaded[n].dtype) for n in LOADED] + [pltpu.VMEM(*x) for x in shapes]
    scratch += [dma((len(LOADED),)), dma((8,)), dma((half // ROWS, 12)), dma((half // ROWS,))]
    scratch += [dma((rounds,))] * 2 + [dma((4, most))] * 2 + [dma((1 + half // ROWS + half // (2 * ROWS),))] * 2
    scratch += job_scratch(sizes, jobs, INSIDE)
    anywhere, vmem = pl.BlockSpec(memory_space=pl.ANY), pl.BlockSpec(memory_space=pltpu.VMEM)
    units = [(n, UNIT, 128) for n in (ff, down, mixer, out)]
    return pl.pallas_call(
        functools.partial(back_kernel, sizes, jobs, ticks, pieces),
        out_shape=[jax.ShapeDtypeStruct(x, F32) for x in ((2, width), (1, lanes), (1, cols))]
        + [jax.ShapeDtypeStruct((half, width), BF)] * 4 + [jax.ShapeDtypeStruct((half, width), F32)]
        + [jax.ShapeDtypeStruct(x, BF) for x in units],
        in_specs=[anywhere] * (len(rows) + len(LOADED)),
        out_specs=[vmem] * 3 + [anywhere] * 9,
        scratch_shapes=scratch,
        compiler_params=pltpu.CompilerParams(collective_id=0, has_side_effects=True, vmem_limit_bytes=63 * 1024 * 1024),
        name="back",
    )(*rows, *[loaded[n] for n in LOADED])


FRONT_LOADED = (
    "wq", "wk", "wv", "wf", "norm_gain", "bias", "code", "sums", "pairs", "gain", "wo", "feed_gain", "wg", "wu", "wd",
)
FRONT_SAVED = ("xn", "q", "k", "v", "dsq", "dsk", "gate", "weight", "dzf", "logits", "kvs", "mixed", "normed", "resid")
WIDE = 256


def silu_pair(raw):
    s = 1.0 / (1.0 + jnp.exp(-raw))
    return (raw * s).astype(BF), (s * (1.0 + raw * (1.0 - s))).astype(BF)


def project_rows(i, s):
    at = pl.ds(pl.multiple_of(i * WIDE, WIDE), WIDE)
    x = s.tokens[at].astype(F32)
    xn = (x * lax.rsqrt(jnp.mean(x * x, axis=-1, keepdims=True) + EPS) * s.norm_gain[...]).astype(BF)
    s.xn[at] = xn
    s.q[at], s.dsq[at] = silu_pair(dot(xn, s.wq[...]))
    s.k[at], s.dsk[at] = silu_pair(dot(xn, s.wk[...]))
    s.v[at] = dot(xn, s.wv[...]).astype(BF)
    z = dot(xn, s.wf[...]) + s.bias[...]
    code = s.code[at]
    valid, reset = code > 0.5, code > 1.5
    down = jnp.exp(-jnp.abs(z))
    gate = jnp.where(valid, (jnp.minimum(z, 0.0) - jnp.log(1.0 + down)) * (1.0 / NORMALIZER), 0.0)
    s.weight[at] = jnp.where(reset, 1.0, 1.0 - jnp.exp(gate))
    s.gate[at] = jnp.where(reset, RESET_LOG, gate)
    sig_neg = jnp.where(z > 0, down, 1.0) / (1.0 + down)
    s.dzf[at] = jnp.where(valid & (code < 1.5), sig_neg * (1.0 / NORMALIZER), 0.0)
    for c in range(WIDE // CH):
        part = chunk_rows(i * (WIDE // CH) + c)
        gate = s.gate[part]
        last = jnp.exp(dot(s.sums[CH : 2 * CH], split3(gate)))
        fade = fade_of(gate)
        s.total[...] = fade * s.total[...] + run_part((last * s.weight[part]).astype(BF), s.k[part], s.v[part])
        s.fade[...] = s.fade[...] * fade


def inner_chunk(c, s):
    at = chunk_rows(c)
    _, _, rows, cols, _ = decays(s.gate[at], s.weight[at], s.sums)
    q, k = s.q[at], s.k[at]
    s.logits[at] = through([nt(head(q, h), head(k, h)) for h in range(2)], rows, cols, s.pairs)


def mix_chunk(c, s):
    at = chunk_rows(c)
    q, k, v = s.q[at], s.k[at], s.v[at]
    gate, weight = s.gate[at], s.weight[at]
    first, last, rows, cols, _ = decays(gate, weight, s.sums)
    kv = s.enter[...]
    low = kv.astype(BF)
    s.kvs[c] = low
    outer = jnp.concatenate([nt(head(q, h), state(low, h)[:, :DH]) for h in range(2)], 1)
    logits = first * outer + s.logits[at]
    s.logits[at] = logits
    probs = softmax2(logits)
    reading = back_through([probs], rows, cols, s.pairs)
    spread = (probs * first).astype(BF)
    s.enter[...] = fade_of(gate) * kv + run_part((last * weight).astype(BF), k, v)
    code = s.code[at, :1]
    for h in range(2):
        mine = slice(h * DH, (h + 1) * DH)
        mixed = dot(slots(spread, h), state(low, h)[:, DH:]) + dot(reading[h].astype(BF), head(v, h))
        s.mixed[at, mine] = mixed
        r = lax.rsqrt(jnp.mean(mixed * mixed, axis=-1, keepdims=True) + EPS)
        s.normed[at, mine] = (mixed * jnp.where(code > 0.5, r, 0.0) * s.gain[:, mine]).astype(BF)


def feed_rows(n, s):
    at = pl.ds(n * WIDE, WIDE)
    hn, cot = s.hidden[at], s.cot[at]
    wide = s.wg.shape[1]
    slot = n % 2
    for c in range(0, wide, 512):
        some = slice(c, min(c + 512, wide))
        gate, up, dact = dot(hn, s.wg[:, some]), dot(hn, s.wu[:, some]), nt(cot, s.wd[some])
        sig = 1.0 / (1.0 + jnp.exp(-gate))
        soft = gate * sig
        s.act[slot, :, some] = (soft * up).astype(BF)
        s.dgate[slot, :, some] = (dact * up * sig * (1.0 + gate * (1.0 - sig))).astype(BF)
        s.dup[slot, :, some] = (dact * soft).astype(BF)
    s.dh[at] = (nt(s.dgate[slot], s.wg[...]) + nt(s.dup[slot], s.wu[...])).astype(BF)


def front_kernel(sizes, *refs):
    refs = list(refs)
    take = lambda n: [refs.pop(0) for _ in range(n)]
    tokens_own, cot_own = take(2)
    sources, saves = take(len(FRONT_LOADED)), take(len(FRONT_SAVED))
    hidden_out, cot_out, act_out, dgate_out, dup_out, dh_out, dh_got = take(7)
    s = Bag()
    for name in FRONT_LOADED + FRONT_SAVED:
        setattr(s, name, refs.pop(0))
    for name in ("tokens", "total", "fade", "enter", "reach", "sent", "got", "attn", "attn_got", "hidden", "cot", "act",
                 "dgate", "dup", "dh"):
        setattr(s, name, refs.pop(0))
    load_sem, save_sem, row_sem, part_sem = take(4)
    scan_sems, swap_sems = take(2), take(2)
    lines = Lines(sizes)
    half, width = tokens_own.shape
    count = 2 * half // CH
    tp_peer = {"tp": 1 - lines.half}
    own_rows = pl.ds(pl.multiple_of(lines.half * half, half), half)
    loads = [pltpu.make_async_copy(x, getattr(s, n), load_sem.at[i]) for i, (n, x) in enumerate(zip(FRONT_LOADED, sources))]
    late = loads[FRONT_LOADED.index("wo") :] + [pltpu.make_async_copy(cot_own, s.cot.at[pl.ds(0, half)], row_sem.at[1])]
    loads = loads[: FRONT_LOADED.index("wo")] + [pltpu.make_async_copy(tokens_own, s.tokens.at[own_rows], row_sem.at[0])]
    for copy in loads:
        copy.start()
    s.total[...] = jnp.zeros_like(s.total)
    s.fade[...] = jnp.ones_like(s.fade)
    lines.greet()
    tokens_swap = remote(tokens_own, s.tokens.at[own_rows], swap_sems, 0, tp_peer)
    tokens_swap.start()
    cot_swap = remote(cot_own, s.cot.at[pl.ds(half, half)], swap_sems, 1, tp_peer)
    cot_swap.start()
    for copy in late:
        copy.start()
    for copy in loads:
        copy.wait()
    tokens_swap.wait()

    def save(*names):
        for n in names:
            i = FRONT_SAVED.index(n)
            pltpu.make_async_copy(getattr(s, n), saves[i], save_sem.at[i]).start()

    lax.fori_loop(0, 2 * half // WIDE, lambda i, carry: (project_rows(i, s), carry)[1], 0)
    early = ("xn", "q", "k", "v", "dsq", "dsk", "gate", "weight", "dzf")
    save(*early)

    def between(n):
        if n < 4:
            for c in range(n * count // 4, (n + 1) * count // 4):
                inner_chunk(c, s)

    scans = scan_lines(lines, s.total, s.fade, s.enter, s.reach, s.sent, s.got, scan_sems, True, between)
    lax.fori_loop(0, count, lambda c, carry: (mix_chunk(c, s), carry)[1], 0)
    save("logits", "kvs", "mixed", "normed")

    for copy in late:
        copy.wait()
    steps = half // WIDE
    swaps = [
        remote(s.attn.at[pl.ds(n * WIDE, WIDE)], s.attn_got.at[pl.ds(n * WIDE, WIDE)], swap_sems, 2 + n, tp_peer)
        for n in range(steps)
    ]
    for n in range(2 * steps):
        side = (1 - lines.half) if n < steps else lines.half
        rows = pl.ds(pl.multiple_of(side * half + n % steps * WIDE, WIDE), WIDE)
        s.attn[n * WIDE : (n + 1) * WIDE] = dot(s.normed[rows], s.wo[...]).astype(BF)
        if n < steps:
            swaps[n].start()
    for n in range(steps):
        at = pl.ds(n * WIDE, WIDE)
        swaps[n].wait_recv()
        attn = s.attn[half + n * WIDE : half + (n + 1) * WIDE].astype(F32) + s.attn_got[at].astype(F32)
        x = s.tokens[pl.ds(pl.multiple_of(lines.half * half + n * WIDE, WIDE), WIDE)].astype(F32) + attn
        s.resid[at] = x
        r = lax.rsqrt(jnp.mean(x * x, axis=-1, keepdims=True) + EPS)
        s.hidden[at] = (x * r * s.feed_gain[...]).astype(BF)
        there = s.hidden.at[pl.ds(half + n * WIDE, WIDE)]
        swaps.append(remote(s.hidden.at[at], there, swap_sems, 2 + steps + n, tp_peer))
        swaps[-1].start()
    save("resid")
    cot_swap.wait()
    cot_save = pltpu.make_async_copy(s.cot, cot_out, row_sem.at[2])
    cot_save.start()

    outs = ((s.act, act_out), (s.dgate, dgate_out), (s.dup, dup_out))
    part = lambda n: [
        pltpu.make_async_copy(src.at[n % 2], dst.at[pl.ds(n * WIDE, WIDE)], part_sem.at[n, i])
        for i, (src, dst) in enumerate(outs)
    ]
    back = [
        remote(s.dh.at[pl.ds(half + n * WIDE, WIDE)], dh_got.at[pl.ds(n * WIDE, WIDE)], swap_sems, 2 + 2 * steps + n, tp_peer)
        for n in range(steps)
    ]
    busy = {}
    for n in [0] + list(range(steps, 2 * steps)) + list(range(1, steps)):
        if n % 2 in busy:
            for copy in busy[n % 2]:
                copy.wait()
        if n >= steps:
            swaps[n].wait_recv()
        feed_rows(n, s)
        busy[n % 2] = part(n)
        for copy in busy[n % 2]:
            copy.start()
        if n >= steps:
            back[n - steps].start()
    ends = [
        pltpu.make_async_copy(s.hidden, hidden_out, row_sem.at[3]),
        pltpu.make_async_copy(s.dh.at[pl.ds(0, half)], dh_out, row_sem.at[4]),
    ]
    for copy in ends:
        copy.start()
    for copy in ends + busy[0] + busy[1] + [cot_save]:
        copy.wait()
    for i, n in enumerate(FRONT_SAVED):
        pltpu.make_async_copy(getattr(s, n), saves[i], save_sem.at[i]).wait()
    for copy in back:
        copy.wait()
    for copy in scans + swaps:
        copy.wait_send()


def front_call(tokens, cot, loaded):
    sizes = line_sizes(lax.axis_size("seq"))
    rounds = (sizes[0] * sizes[1] * sizes[2]).bit_length() - 1
    half, width = tokens.shape
    span = 2 * half
    lanes, cols, hidden = (loaded[n].shape[1] for n in ("wf", "wq", "wg"))
    shapes = dict(
        xn=((span, width), BF), q=((span, cols), BF), k=((span, cols), BF), v=((span, cols), BF), dsq=((span, cols), BF),
        dsk=((span, cols), BF), gate=((span, lanes), F32), weight=((span, lanes), F32), dzf=((span, lanes), F32),
        logits=((span, lanes), F32), kvs=((span // CH, lanes, 2 * DH), BF), mixed=((span, cols), F32),
        normed=((span, cols), BF), resid=((half, width), F32),
    )
    others = [
        ((span, width), BF), ((lanes, 2 * DH), F32), ((lanes, CH), F32), ((lanes, 2 * DH), F32), ((lanes, CH), F32),
        ((rounds, lanes, 2 * DH + 2 * CH), BF), ((rounds, lanes, 2 * DH + 2 * CH), BF), ((span, width), BF), ((half, width), BF),
        ((span, width), BF), ((span, width), BF), ((2, WIDE, hidden), BF), ((2, WIDE, hidden), BF), ((2, WIDE, hidden), BF),
        ((span, width), BF),
    ]
    more = [((span, width), BF)] * 2 + [((span, hidden), BF)] * 3 + [((half, width), BF)] * 2
    dma = pltpu.SemaphoreType.DMA
    scratch = [pltpu.VMEM(loaded[n].shape, loaded[n].dtype) for n in FRONT_LOADED]
    scratch += [pltpu.VMEM(*shapes[n]) for n in FRONT_SAVED] + [pltpu.VMEM(*x) for x in others]
    scratch += [dma((len(FRONT_LOADED),)), dma((len(FRONT_SAVED),)), dma((5,)), dma((span // WIDE, 3))]
    scratch += [dma((rounds,))] * 2 + [dma((2 + 3 * (half // WIDE),))] * 2
    anywhere = pl.BlockSpec(memory_space=pl.ANY)
    outs = pl.pallas_call(
        functools.partial(front_kernel, sizes),
        out_shape=[jax.ShapeDtypeStruct(*x) for x in [shapes[n] for n in FRONT_SAVED] + more],
        in_specs=[anywhere] * (2 + len(FRONT_LOADED)),
        out_specs=[anywhere] * (len(FRONT_SAVED) + len(more)),
        scratch_shapes=scratch,
        compiler_params=pltpu.CompilerParams(collective_id=1, has_side_effects=True, vmem_limit_bytes=VMEM_LIMIT),
        name="front",
    )(tokens, cot, *[loaded[n] for n in FRONT_LOADED])
    return dict(zip(FRONT_SAVED, outs)), outs[len(FRONT_SAVED) :]


def widen_kernel(parts, *refs):
    for (which, blocks), out_ref in zip(parts, refs[-len(parts) :]):
        for c, block in enumerate(blocks):
            out_ref[:, c * 128 : (c + 1) * 128] = refs[which][block].astype(F32)


def widen(arrays, parts, steps):
    return pl.pallas_call(
        functools.partial(widen_kernel, parts),
        grid=(steps,),
        in_specs=[pl.BlockSpec((a.shape[0], a.shape[1] // steps, 128), lambda i: (0, i, 0)) for a in arrays],
        out_specs=[pl.BlockSpec((arrays[w].shape[1] // steps, len(b) * 128), lambda i: (i, 0)) for w, b in parts],
        out_shape=[jax.ShapeDtypeStruct((arrays[w].shape[1], len(b) * 128), F32) for w, b in parts],
        compiler_params=pltpu.CompilerParams(dimension_semantics=("arbitrary",), vmem_limit_bytes=VMEM_LIMIT),
        name="widen",
    )(*arrays)


X, Y, Z = 0, 1, 2
PIECES = 4
JOBS = (
    (2, 0, 1, (Y, X, Z)),
    (2, 1, 4, (Y, X, Z)),
    (3, 0, 4, (Y, X, Z)),
    (1, 0, 3, (Y, Z, X)),
    (0, 0, 4, (X, Y, Z)),
    (2, 5, 3, (X, Z, Y)),
    (1, 3, 4, (X, Y, Z)),
    (0, 4, 8, (Y, X, Z)),
    (2, 8, 3, (X, Y, Z)),
    (0, 12, 6, (X, Y, Z)),
    (2, 11, 2, (Z, Y, X)),
    (0, 18, 3, (X, Y, Z)),
    (1, 7, 4, (Y, X, Z)),
    (0, 21, 1, (Y, X, Z)),
)
TICKS = (
    (), ((3, 0),), ((6, 0),), ((12, 0),), (), (), (), ((3, 1),), (), (), ((6, 1),), (), ((12, 1), (3, 2), (4, 0),),
    ((6, 2), (7, 0),), ((12, 2), (3, 3), (9, 0),), ((6, 3), (4, 1), (3, 4),), ((12, 3), (7, 1), (2, 0), (11, 0),),
    ((4, 2), (9, 1), (6, 4),), (), (), ((3, 5),), ((2, 1), (7, 2),), ((12, 4),), (), ((4, 3), (9, 2), (11, 1),), (),
    ((1, 0),), ((2, 2), (6, 5),), ((7, 3),), ((12, 5),), ((5, 0),), ((3, 6),), ((4, 4),), ((8, 0),), ((11, 2),),
    ((6, 6),), ((9, 3),), ((0, 0),), ((10, 0),), ((1, 1),), ((2, 3),), ((5, 1),), ((8, 1),), ((12, 6),), ((7, 4),),
    ((1, 2),), ((11, 3),), ((4, 5),), ((0, 1),), ((13, 0),), ((8, 2),), ((9, 4),), ((7, 5),), ((13, 1),), ((10, 1),),
    ((9, 5),), ((4, 6),), ((0, 2),), ((13, 2),), ((2, 4),), ((5, 2),), ((1, 3),), ((9, 6),), ((7, 6),), ((11, 4),),
    ((10, 2),), ((5, 3),), ((2, 5),), ((8, 3),), ((10, 3),), ((0, 3),), ((11, 5),), ((13, 3),), ((5, 4),), ((10, 4),),
    ((1, 4),), ((11, 6),), ((8, 4),), ((0, 4),), ((2, 6),), ((13, 4),), ((10, 5),), ((1, 5),), ((0, 5),), ((8, 5),),
    ((13, 5),), ((5, 5),), ((8, 6),), ((1, 6),), ((0, 6),), ((10, 6),), ((13, 6),), ((5, 6),),
)


def token_code(lengths, positions):
    buckets = (lengths + BUCKET - 1) // BUCKET
    spans = buckets * BUCKET
    starts = jnp.cumsum(spans) - spans
    segment = jnp.sum((positions[:, None] >= starts[None, :]).astype(jnp.int32), axis=1) - 1
    picked = segment[:, None] == jnp.arange(lengths.shape[0], dtype=jnp.int32)[None, :]
    begin = jnp.sum(jnp.where(picked, starts[None, :], 0), axis=1)
    length = jnp.sum(jnp.where(picked, lengths[None, :], 0), axis=1)
    offset = positions - begin
    return jnp.where(offset == 0, 2.0, jnp.where(offset < length, 1.0, 0.0)).astype(F32)


def per_device(
    tokens, norm_gain, query_weight, key_weight, value_weight, forget_weight, forget_bias, head_gain,
    out_weight, feed_gain, gate_weight, up_weight, down_weight, lengths, cotangent,
):
    half, width = tokens.shape
    span = 2 * half
    cols = query_weight.shape[1]
    lanes = forget_weight.shape[1]
    sums, pairs, flipped, back = tables()
    sums, back = jnp.asarray(sums, BF), jnp.asarray(back, BF)
    pairs, flipped = jnp.asarray(pairs, BF), jnp.asarray(flipped, BF)

    positions = lax.axis_index("seq") * span + jnp.arange(span, dtype=jnp.int32)
    code = jnp.broadcast_to(token_code(lengths, positions)[:, None], (span, lanes))
    weights = dict(wq=query_weight, wk=key_weight, wv=value_weight, wf=forget_weight, wo=out_weight)
    shared = dict(code=code, sums=sums, pairs=pairs, gain=head_gain[None], norm_gain=norm_gain[None])
    wide = dict(wg=gate_weight, wu=up_weight, wd=down_weight, bias=forget_bias[None], feed_gain=feed_gain[None])
    saved, (hidden, cot, act, dgate, dup, dh_own, dh_got) = front_call(tokens, cotangent, dict(weights, **shared, **wide))
    resid = saved["resid"]
    loaded = dict(weights, **shared, flipped=flipped, back=back, feed_gain=feed_gain[None])
    for name in ("q", "k", "v", "dsq", "dsk", "gate", "weight", "dzf", "logits", "kvs", "mixed", "normed"):
        loaded[name] = saved[name]
    rows = (dh_own, dh_got, act, cot, hidden, dgate, dup, down_weight, resid, tokens, saved["xn"])
    gains, bias_sum, head_sum, block_out, tokens_grad, _, _, _, *sums = back_call(rows, loaded, JOBS, TICKS, PIECES)
    ff_sum, down_sum, mixer_sum, out_sum = sums
    blocks, ff_blocks, wide = cols // 128, gate_weight.shape[1] // 128, tuple(range(width // 128))
    which = lambda up: tuple(4 * (c // 2) + 2 * up + c % 2 - (up if c == ff_blocks - 1 else 0) for c in range(ff_blocks))
    parts = [(0, tuple(range(i * blocks, (i + 1) * blocks))) for i in range(3)] + [(0, (3 * blocks,)), (1, wide)]
    parts += [(2, which(0)), (2, which(1)), (3, wide)]
    arrays = [mixer_sum, out_sum.reshape(-1, cols, 128), ff_sum, down_sum.reshape(-1, down_weight.shape[0], 128)]
    query_sum, key_sum, value_sum, forget_sum, out_grad, gate_grad, up_grad, down_grad = widen(arrays, parts, 8)
    return (
        block_out, tokens_grad, gains[0], query_sum, key_sum, value_sum, forget_sum, bias_sum[0], head_sum[0], out_grad,
        gains[1], gate_grad, up_grad, down_grad,
    )


def solution(mesh):
    rows, by_col, by_row = P(("seq", "tp"), None), P(None, "tp"), P("tp", None)
    return jax.shard_map(
        per_device,
        mesh=mesh,
        in_specs=(
            rows, P(), by_col, by_col, by_col, by_col, P("tp"), P("tp"), by_row, P(), by_col, by_col, by_row, P(), rows,
        ),
        out_specs=(
            rows, rows, P(), by_col, by_col, by_col, by_col, P("tp"), P("tp"), by_row, P(), by_col, by_col, by_row,
        ),
        check_vma=False,
    )
```

```python
import functools

import jax
import jax.numpy as jnp
import numpy as np
from jax import lax
from jax.experimental import pallas as pl
from jax.experimental.pallas import tpu as pltpu
from jax.sharding import PartitionSpec as P

DH = 256
SLOTS = 64
BUCKET = 64
CH = 128
BASE = 8
HALVES = (64, 32, 16, 8)
RESET_LOG = -16384.0
LIFT = 2.0**20
SCALE = DH**-0.5

EPS = 1e-06
NORMALIZER = 8.0

BF = jnp.bfloat16
F32 = jnp.float32
VMEM_LIMIT = 56 * 1024 * 1024
UNIT = 1024
MESH = pl.DeviceIdType.MESH


def dot(a, b):
    return lax.dot_general(a, b, (((1,), (0,)), ((), ())), preferred_element_type=F32)


def nt(a, b):
    return lax.dot_general(a, b, (((1,), (1,)), ((), ())), preferred_element_type=F32)


def tn(a, b):
    return lax.dot_general(a, b, (((0,), (0,)), ((), ())), preferred_element_type=F32)


def tables():
    t, u = np.arange(CH)[:, None], np.arange(CH)[None, :]
    sums, pairs = [u <= t, u > t], []
    for half in HALVES:
        mid = t // (2 * half) * (2 * half) + half
        sums.append(np.where(t >= mid, (u >= mid) & (u <= t), (u > t) & (u < mid)))
        pairs.append(
            (t // (2 * half) == u // (2 * half)) & (t % (2 * half) >= half) & (u % (2 * half) < half)
        )
    ref = t // BASE * BASE + BASE // 2 - 1
    sums.append(((u > ref) & (u <= t)).astype(int) - ((u > t) & (u <= ref)).astype(int))
    pairs.append((t // BASE == u // BASE) & (u <= t))
    stacked = np.concatenate([s.astype(np.float32) for s in sums], 0)
    return (
        np.concatenate([stacked] * 3, 1),
        np.stack(pairs).astype(np.float32),
        np.stack([p.T for p in pairs]).astype(np.float32),
        np.concatenate([stacked.T] * 2, 1),
    )


def split3(x):
    high = x.astype(BF)
    rest = x - high.astype(F32)
    middle = rest.astype(BF)
    low = (rest - middle.astype(F32)).astype(BF)
    return jnp.concatenate([high, middle, low], 0)


def split2(x):
    high = x.astype(BF)
    return jnp.concatenate([high, (x - high.astype(F32)).astype(BF)], 0)


def decays(gate, weight, sums_ref):
    sums = dot(sums_ref[...], split3(gate))
    part = [sums[i * CH : (i + 1) * CH] for i in range(3 + len(HALVES))]
    first, last = jnp.exp(part[0]), jnp.exp(part[1])
    rows = [jnp.exp(p) for p in part[2:-1]]
    cols = [r * weight for r in rows]
    slopes = list(rows)
    rows.append(jnp.exp(part[-1]) * LIFT)
    slopes.append(jnp.exp(-part[-1]) * (1 / LIFT))
    cols.append(slopes[-1] * weight)
    return first, last, rows, cols, slopes


def halves(x):
    left = lax.broadcasted_iota(jnp.int32, x.shape, 1) < SLOTS
    zero = jnp.zeros_like(x)
    return jnp.where(left, x, zero), jnp.where(left, zero, x)


def head(x, h):
    return x[:, h * DH : (h + 1) * DH]


def slots(x, h):
    return x[:, h * SLOTS : (h + 1) * SLOTS]


def state(x, h):
    return x[h * SLOTS : (h + 1) * SLOTS]


def through(pairwise, rows, cols, pairs_ref):
    total = None
    for i in range(len(rows)):
        keep = pairs_ref[i].astype(F32) != 0
        left = jnp.concatenate([jnp.where(keep, p, 0.0).astype(BF) for p in pairwise], 1)
        right = jnp.concatenate(halves(cols[i].astype(BF)), 0)
        term = rows[i] * dot(left, right)
        total = term if total is None else total + term
    return total


def back_through(values, rows, cols, pairs_ref):
    totals = None
    for i in range(len(rows)):
        keep = pairs_ref[i].astype(F32) != 0
        stack = [part for v in values for part in halves((v * rows[i]).astype(BF))]
        out = nt(jnp.concatenate(stack, 0), cols[i].astype(BF))
        terms = [jnp.where(keep, out[n * CH : (n + 1) * CH], 0.0) for n in range(len(stack))]
        totals = terms if totals is None else [a + b for a, b in zip(totals, terms)]
    return totals


def softmax2(logits):
    out = []
    for h in range(2):
        x = slots(logits, h) * SCALE
        e = jnp.exp(x - jnp.max(x, axis=-1, keepdims=True))
        out.append(e / jnp.sum(e, axis=-1, keepdims=True))
    return jnp.concatenate(out, 1)


def fade_of(gate):
    return jnp.exp(jnp.sum(gate.T, axis=1, keepdims=True))


def run_part(trail, keys, values):
    return jnp.concatenate(
        [
            jnp.concatenate([tn(slots(trail, h), head(keys, h)), tn(slots(trail, h), head(values, h))], 1)
            for h in range(2)
        ],
        0,
    )


def state_grads(dl, probs, first, q, dmix):
    a, b = (dl * first).astype(BF), (probs * first).astype(BF)
    return jnp.concatenate(
        [jnp.concatenate([tn(slots(a, h), head(q, h)), tn(slots(b, h), head(dmix, h))], 1) for h in range(2)], 0
    )


def line_sizes(count):
    return {16: (2, 2, 4), 64: (4, 4, 4)}.get(count, (count, 1, 1))


class Lines:
    def __init__(self, sizes):
        self.sizes = sizes
        self.index = lax.axis_index("seq")
        self.half = lax.axis_index("tp")
        self.strides = (1, sizes[0], sizes[0] * sizes[1])
        self.place = [lax.rem(self.index // s, m) for s, m in zip(self.strides, sizes)]

    def peer(self, axis, d):
        m = self.sizes[axis]
        return self.index + (lax.rem(self.place[axis] + d, m) - self.place[axis]) * self.strides[axis]

    def greet(self):
        barrier = pltpu.get_barrier_semaphore()
        count = 1
        pl.semaphore_signal(barrier, inc=1, device_id={"tp": 1 - self.half}, device_id_type=MESH)
        for axis in range(3):
            for d in range(1, self.sizes[axis]):
                pl.semaphore_signal(barrier, inc=1, device_id={"seq": self.peer(axis, d)}, device_id_type=MESH)
                count += 1
        pl.semaphore_wait(barrier, count)


def remote(src, dst, sems, at, device):
    return pltpu.make_async_remote_copy(
        src_ref=src, dst_ref=dst, send_sem=sems[0].at[at], recv_sem=sems[1].at[at], device_id=device, device_id_type=MESH
    )


def job_scratch(sizes, jobs, inside):
    scratch = []
    for a, _, units, order in jobs:
        rows = UNIT
        if not inside[a]:
            scratch.append(pltpu.VMEM((units, UNIT // sizes[order[0]], 128), BF))
        for axis in order:
            rows = rows // sizes[axis]
            scratch.append(pltpu.VMEM((max(sizes[axis] - 1, 1), units, rows, 128), BF))
    most = max(max(sizes) - 1, 1)
    return scratch + [pltpu.SemaphoreType.DMA((len(jobs), 6, most))] * 2 + [pltpu.SemaphoreType.DMA((len(jobs), 2))]


TAIL = 16


class Jobs:
    def __init__(self, lines, jobs, ins, outs, inside, scratch):
        self.lines, self.jobs, self.ins, self.outs, self.inside = lines, jobs, ins, outs, inside
        self.sems, self.local = scratch[-3:-1], scratch[-1]
        self.mine, self.held, self.got, self.shape = [], [], [], []
        scratch = list(scratch)
        for j, (a, _, _, order) in enumerate(jobs):
            rows, offset, shape = UNIT, 0, []
            for axis in order:
                rows = rows // lines.sizes[axis]
                mine = lines.place[axis] * rows
                offset = offset + mine
                shape.append((axis, rows, pl.multiple_of(mine, 16), pl.multiple_of(offset, 16)))
            self.shape.append(shape)
            self.mine.append(None if inside[a] else scratch.pop(0))
            self.got.append([scratch.pop(0) for _ in range(3)])
            self.held.append([got.at[0] for got in self.got[j]])

    def copies(self, j, s):
        lines, (a, first, units, _) = self.lines, self.jobs[j]
        stage = s if s < 3 else 5 - s
        axis, rows, _, offset = self.shape[j][stage]
        out = []
        for d in range(1, lines.sizes[axis]):
            if s < 3:
                target = pl.multiple_of(lax.rem(lines.place[axis] + d, lines.sizes[axis]) * rows, 16)
                if s == 0:
                    src = self.ins[a].at[pl.ds(first, units), pl.ds(target, rows), :]
                else:
                    src = self.held[j][s - 1].at[:, pl.ds(target, rows), :]
                dst = self.got[j][s].at[d - 1]
            else:
                dst = self.outs[a].at[pl.ds(first, units), pl.ds(offset, rows), :]
                src = self.held[j][2] if s == 3 else dst
            out.append(remote(src, dst, self.sems, (j, s, d - 1), {"seq": lines.peer(axis, d)}))
        return out

    def own(self, j):
        a, first, units, _ = self.jobs[j]
        _, rows, mine, _ = self.shape[j][0]
        src = self.ins[a].at[pl.ds(first, units), pl.ds(mine, rows), :]
        return pltpu.make_async_copy(src, self.mine[j], self.local.at[j, 0])

    def home(self, j):
        a, first, units, _ = self.jobs[j]
        _, rows, _, offset = self.shape[j][2]
        dst = self.outs[a].at[pl.ds(first, units), pl.ds(offset, rows), :]
        return pltpu.make_async_copy(self.held[j][2], dst, self.local.at[j, 1])

    def add(self, j, stage):
        a, first, units, _ = self.jobs[j]
        axis, rows, mine, _ = self.shape[j][stage]
        held, got = self.held[j], self.got[j]

        def one(u, carry):
            if stage > 0:
                total = held[stage - 1][u, pl.ds(mine, rows), :].astype(F32)
            elif self.inside[a]:
                total = self.ins[a][first + u, pl.ds(mine, rows), :].astype(F32)
            else:
                total = self.mine[j][u].astype(F32)
            for d in range(self.lines.sizes[axis] - 1):
                total = total + got[stage][d, u].astype(F32)
            held[stage][u] = total.astype(BF)
            return carry

        lax.fori_loop(0, units, one, 0)

    def step(self, j, s):
        if s == 0 and not self.inside[self.jobs[j][0]]:
            self.own(j).start()
        if s == 1 and not self.inside[self.jobs[j][0]]:
            self.own(j).wait()
        if s == 4:
            self.home(j).wait()
        if s > 0:
            for copy in self.copies(j, s - 1):
                copy.wait_recv()
        if 1 <= s <= 3:
            self.add(j, s - 1)
        if s == 3:
            self.home(j).start()
        if s < 6:
            for copy in self.copies(j, s):
                copy.start()

    def finish(self):
        for j in range(len(self.jobs)):
            for s in range(6):
                for copy in self.copies(j, s):
                    copy.wait_send()


def scan_lines(lines, total_ref, fade_ref, enter_ref, reach_ref, sent_ref, got_ref, sems, earlier, between):
    enter_ref[...] = jnp.zeros_like(enter_ref)
    for bit in range(sent_ref.shape[0]):
        sent_ref[bit, total_ref.shape[0] :] = jnp.zeros_like(sent_ref[bit, total_ref.shape[0] :])
    reach_ref[...] = jnp.ones_like(reach_ref)
    count = lines.sizes[0] * lines.sizes[1] * lines.sizes[2]
    rounds = count.bit_length() - 1
    side = [lax.rem(lines.index // (1 << bit), 2) for bit in range(rounds)]

    def copy(bit):
        partner = lines.index + (1 - 2 * side[bit]) * (1 << bit)
        return remote(sent_ref.at[bit], got_ref.at[bit], sems, bit, {"seq": partner})

    lanes = total_ref.shape[0]
    for bit in range(rounds):
        fade = fade_ref[...]
        flat = fade.T[:1]
        high = flat.astype(BF).astype(F32)
        sent_ref[bit, :lanes] = total_ref[...].astype(BF)
        row = lax.broadcasted_iota(jnp.int32, (TAIL, lanes), 0)
        sent_ref[bit, lanes:, :lanes] = jnp.where(row == 0, high, flat - high).astype(BF)
        copy(bit).start()
        between(bit)
        copy(bit).wait_recv()
        part = got_ref[bit, :lanes].astype(F32)
        flat = got_ref[bit, lanes:, :lanes].astype(F32)
        part_fade = jnp.broadcast_to(flat[:1] + flat[1:2], fade.shape).T
        behind = side[bit] == (1 if earlier else 0)
        enter, reach, total = enter_ref[...], reach_ref[...], total_ref[...]
        enter_ref[...] = jnp.where(behind, reach[:, :1] * part + enter, enter)
        reach_ref[...] = jnp.where(behind, reach * part_fade, reach)
        total_ref[...] = jnp.where(behind, fade[:, :1] * part + total, part_fade[:, :1] * total + part)
        fade_ref[...] = fade * part_fade
    return [copy(bit) for bit in range(rounds)]


def chunk_rows(c):
    return pl.ds(pl.multiple_of(c * CH, CH), CH)


def score_chunk(c, s):
    at = chunk_rows(c)
    dnormed = nt(s.da[at], s.wo[...])
    dnormed = jnp.where(s.code[at, :1] > 0.5, dnormed, 0.0)
    dmix = []
    for h in range(2):
        mixed = s.mixed[at, h * DH : (h + 1) * DH]
        r = lax.rsqrt(jnp.mean(mixed * mixed, axis=-1, keepdims=True) + EPS)
        n = mixed * r
        d = head(dnormed, h)
        u = d * s.gain[:, h * DH : (h + 1) * DH]
        s.gain_grad[:, h * DH : (h + 1) * DH] += jnp.sum(d * n, axis=0, keepdims=True)
        dmix.append(r * (u - n * jnp.mean(u * n, axis=-1, keepdims=True)))
    wide = jnp.concatenate(dmix, 1)
    dmix = wide.astype(BF)
    s.dmix[at] = dmix
    rest = (wide - dmix.astype(F32)).astype(BF)
    exact = [jnp.concatenate([head(dmix, h), head(rest, h)], 0) for h in range(2)]
    q, v = s.q[at], s.v[at]
    gate, weight = s.gate[at], s.weight[at]
    first, _, rows, cols, _ = decays(gate, weight, s.sums)
    logits = s.logits[at]
    probs = softmax2(logits)
    low = s.kvs[c]
    fold = lambda x: x[:CH] + x[CH:]
    reads = [fold(nt(exact[h], head(v, h))) for h in range(2)]
    outer = jnp.concatenate([fold(nt(exact[h], state(low, h)[:, DH:])) for h in range(2)], 1)
    dprobs = first * outer + through(reads, rows, cols, s.pairs)
    weighted = probs * dprobs
    sums = [
        jnp.broadcast_to(jnp.sum(slots(weighted, h), axis=-1, keepdims=True), (CH, SLOTS)) for h in range(2)
    ]
    dl = (weighted - probs * jnp.concatenate(sums, 1)) * SCALE
    s.dl[at] = dl
    part = state_grads(dl, probs, first, q, dmix)
    reach = s.fade[...]
    s.dkv[...] += jnp.concatenate([reach] * (s.dkv.shape[1] // reach.shape[1]), 1) * part
    s.fade[...] = reach * fade_of(gate)


def grad_chunk(c, s):
    at = chunk_rows(c)
    q, k, v, dmix = s.q[at], s.k[at], s.v[at], s.dmix[at]
    gate, weight = s.gate[at], s.weight[at]
    dl = s.dl[at]
    first, last, rows, cols, slopes = decays(gate, weight, s.sums)
    probs = softmax2(s.logits[at])
    low, dkv = s.kvs[c], s.enter[...]
    dlow = dkv.astype(BF)
    r0, r1, s0, s1 = back_through([probs, dl], rows, cols, s.pairs)
    turned = [nt(head(a, h), head(b, h)) for h in range(2) for a, b in ((k, q), (v, dmix))]
    dw = last * jnp.concatenate(
        [nt(jnp.concatenate([head(k, h), head(v, h)], 1), state(dlow, h)) for h in range(2)], 1
    )
    parts = [None, weight * dw]
    scores = [nt(head(q, h), head(k, h)) for h in range(2)]
    reads = [nt(head(dmix, h), head(v, h)) for h in range(2)]
    outer = [
        jnp.concatenate([nt(head(x, h), state(low, h)[:, at_state]) for h in range(2)], 1)
        for x, at_state in ((q, slice(0, DH)), (dmix, slice(DH, 2 * DH)))
    ]
    parts[0] = first * (dl * outer[0] + probs * outer[1])
    for i in range(len(rows)):
        keep = s.flipped[i].astype(F32) != 0
        left = jnp.concatenate([jnp.where(keep, x, 0.0).astype(BF) for x in turned], 1)
        a, b = halves((dl * rows[i]).astype(BF)), halves((probs * rows[i]).astype(BF))
        late = slopes[i] * dot(left, jnp.concatenate([a[0], b[0], a[1], b[1]], 0))
        dw = dw + late
        keep = s.pairs[i].astype(F32) != 0
        left = [jnp.concatenate([jnp.where(keep, x, 0.0).astype(BF) for x in both], 1) for both in (scores, reads)]
        early = dot(jnp.concatenate(left, 0), jnp.concatenate(halves(cols[i].astype(BF)), 0))
        early = rows[i] * (dl * early[:CH] + probs * early[CH:])
        parts.append(early + weight * late if i < len(HALVES) else early - weight * late)
    trail = (last * weight).astype(BF)
    spread = (dl * first).astype(BF)
    reading, dscore = [r0.astype(BF), r1.astype(BF)], [s0.astype(BF), s1.astype(BF)]
    dq, dk, dv = [], [], []
    for h in range(2):
        dq.append(dot(dscore[h], head(k, h)) + dot(slots(spread, h), state(low, h)[:, :DH]))
        dk.append(tn(dscore[h], head(q, h)) + dot(slots(trail, h), state(dlow, h)[:, :DH]))
        dv.append(tn(reading[h], head(dmix, h)) + dot(slots(trail, h), state(dlow, h)[:, DH:]))
    dq = (jnp.concatenate(dq, 1) * s.dsq[at].astype(F32)).astype(BF)
    dk = (jnp.concatenate(dk, 1) * s.dsk[at].astype(F32)).astype(BF)
    dv = jnp.concatenate(dv, 1).astype(BF)
    fade = fade_of(gate)
    across = jnp.sum(fade * low.astype(F32) * dkv, axis=1, keepdims=True)
    across = jnp.broadcast_to(across, (across.shape[0], CH)).T[:1]
    flow = dot(s.back[...], split2(jnp.concatenate(parts, 0))) + across
    df = ((flow - jnp.exp(gate) * dw) * s.dzf[at]).astype(BF)
    s.d_all[at] = jnp.concatenate([dq, dk, dv, df], 1)
    s.bias_grad[...] += jnp.sum(df.astype(F32), axis=0, keepdims=True)
    s.enter[...] = fade * dkv + state_grads(dl, probs, first, q, dmix)
    dx = nt(dq, s.wq[...]) + nt(dk, s.wk[...]) + nt(dv, s.wv[...]) + nt(df, s.wf[...])
    s.norm_grad[...] += jnp.sum(dx * s.xn[at].astype(F32), axis=0, keepdims=True)
    s.dx[at] = dx.astype(BF)


class Bag:
    pass


LOADED = (
    "wo", "mixed", "code", "gain", "q", "k", "v", "gate", "weight", "logits", "kvs", "sums", "pairs", "flipped", "back",
    "dsq", "dsk", "dzf", "wq", "wk", "wv", "wf", "normed", "norm_gain", "feed_gain",
)


FF_STEPS = ((0, 1), (2, 3), (4,), (5,))
INSIDE = (True, True, True, True)
ROWS = 128


def back_kernel(sizes, jobs, ticks, pieces, *refs):
    refs = list(refs)
    take = lambda n: [refs.pop(0) for _ in range(n)]
    dh_own, dh_got, act, cot, hn, dgate, dup, down_weight, resid, tokens, xn = take(11)
    sources = take(len(LOADED))
    norm_out, feed_out, bias_out, head_out, block_out, tokens_out, feed_got, dx_got, dresid, *outs = take(13)
    s = Bag()
    for name in LOADED:
        setattr(s, name, refs.pop(0))
    for name in ("hn", "da", "dmix", "dl", "wide_grads", "gain_grad", "bias_grad", "norm_grad", "dkv", "fade", "enter",
                 "reach", "ff_units", "down_units", "mixer_units", "out_units", "feed_part", "sent", "got", "small_held", "small_got",
                 "wide", "narrow", "result"):
        setattr(s, name, refs.pop(0))
    s.dx = s.da
    hidden = dgate.shape[1]
    s.dgate, s.dup = s.wide_grads.at[:, :hidden], s.wide_grads.at[:, hidden:]
    s.d_all = s.wide_grads.at[:, : 3 * s.wq.shape[1] + s.wf.shape[1]]
    load_sem, row_sem, piece_sem, feed_sem = take(4)
    scan_sems, small_sems, swap_sems = take(2), take(2), take(2)
    lines = Lines(sizes)
    half, width = dh_own.shape
    count = 2 * half // CH
    tp_peer = {"tp": 1 - lines.half}

    other_rows = pl.ds(pl.multiple_of((1 - lines.half) * half, half), half)
    early = [
        pltpu.make_async_copy(act, s.wide_grads.at[:, :hidden], row_sem.at[0]),
        pltpu.make_async_copy(cot, s.wide_grads.at[:, hidden : hidden + width], row_sem.at[1]),
    ]
    loads = [pltpu.make_async_copy(x, getattr(s, n), load_sem.at[i]) for i, (n, x) in enumerate(zip(LOADED, sources))]
    late = [
        pltpu.make_async_copy(hn, s.hn, row_sem.at[2]),
        pltpu.make_async_copy(dgate, s.dgate, row_sem.at[3]),
        pltpu.make_async_copy(dup, s.dup, row_sem.at[4]),
    ]
    for copy in early + loads[::-1] + late[:1]:
        copy.start()
    for ref in (s.gain_grad, s.bias_grad, s.norm_grad, s.feed_part, s.dkv):
        ref[...] = jnp.zeros_like(ref)
    s.fade[...] = jnp.ones_like(s.fade)
    lines.greet()
    dx_swap = remote(s.dx.at[other_rows], dx_got, swap_sems, 0, tp_peer)
    work = Jobs(
        lines, jobs, [s.ff_units, s.down_units, s.mixer_units, s.out_units], outs, INSIDE, refs
    )
    pending = [list(t) for t in ticks]

    def tick():
        for j, step in pending.pop(0):
            work.step(j, step)

    def loop(body):
        todo = [pending.pop(0) for _ in range(count)]

        def one(i, carry):
            body(i)
            for k, steps in enumerate(todo):
                if steps:

                    @pl.when(i == k)
                    def _():
                        for j, step in steps:
                            work.step(j, step)

            return carry

        lax.fori_loop(0, count, one, 0)

    feed_gain = loads.pop(LOADED.index("feed_gain"))
    for copy in early + [feed_gain]:
        copy.wait()

    def down_part(n):
        part = tn(s.wide_grads[:, :hidden], s.wide_grads[:, hidden + n * 256 : hidden + (n + 1) * 256]).astype(BF)
        for c in range(2):
            row, done = (2 * n + c) * hidden, 0
            while done < hidden:
                some = min(hidden - done, UNIT - (row + done) % UNIT)
                at = (row + done) % UNIT
                s.down_units[(row + done) // UNIT, at : at + some] = part[done : done + some, c * 128 : (c + 1) * 128]
                done += some

    def row_loads(n):
        at, slot = pl.ds(n * ROWS, ROWS), n % 2
        return [
            pltpu.make_async_copy(src.at[at], dst, piece_sem.at[n, 8 + i])
            for i, (src, dst) in enumerate(
                ((resid, s.wide.at[slot]), (dh_own, s.narrow.at[slot]), (dh_got, s.narrow.at[2 + slot]))
            )
        ]

    def mine(n):
        return pl.ds(pl.multiple_of(lines.half * half + n * ROWS, ROWS), ROWS)

    def dresid_save(n):
        return pltpu.make_async_copy(s.wide.at[n % 2], dresid.at[pl.ds(n * ROWS, ROWS)], piece_sem.at[n, 11])

    def row_grads(n):
        slot = n % 2
        for copy in row_loads(n):
            copy.wait()
        x = s.wide[slot]
        r = lax.rsqrt(jnp.mean(x * x, axis=-1, keepdims=True) + EPS)
        norm = x * r
        dh = s.narrow[slot].astype(F32) + s.narrow[2 + slot].astype(F32)
        s.feed_part[...] += jnp.sum(dh * norm, axis=0, keepdims=True)
        u = dh * s.feed_gain[...]
        full = s.wide_grads[n * ROWS : (n + 1) * ROWS, hidden : hidden + width].astype(F32)
        full = full + r * (u - norm * jnp.mean(u * norm, axis=-1, keepdims=True))
        s.wide[slot] = full
        s.da[mine(n)] = full.astype(BF)
        dresid_save(n).start()

    steps = half // ROWS
    da_swaps = [remote(s.da.at[mine(n)], s.da.at[mine(n)], swap_sems, 1 + n, tp_peer) for n in range(steps)]
    for n in range(2):
        for copy in row_loads(n):
            copy.start()
    for n in range(steps):
        down_part(n)
        row_grads(n)
        da_swaps[n].start()
        dresid_save(n).wait()
        if n + 2 < steps:
            for copy in row_loads(n + 2):
                copy.start()
        tick()
    for copy in late[1:]:
        copy.start()
    for copy in loads:
        copy.wait()
    for copy in da_swaps:
        copy.wait_recv()
    loop(lambda i: score_chunk(i, s))
    for copy in da_swaps:
        copy.wait_send()
    for copy in late:
        copy.wait()

    def out_part(n):
        wide = width // 4
        part = tn(s.normed[...], s.da[:, n * wide : (n + 1) * wide]).astype(BF)
        tall = part.shape[0]
        for c in range(wide // 128):
            row = (n * (wide // 128) + c) * tall
            s.out_units[row // UNIT, row % UNIT : row % UNIT + tall] = part[:, c * 128 : (c + 1) * 128]

    def ff_part(n):
        at = slice(n * 256, min((n + 1) * 256, s.dgate.shape[1]))
        part = tn(s.hn[...], jnp.concatenate([s.dgate[:, at], s.dup[:, at]], 1)).astype(BF)
        for c in range(part.shape[1] // 128):
            s.ff_units[4 * n + c] = part[:, c * 128 : (c + 1) * 128]

    def between(n):
        if n < 4:
            out_part(n)
            for m in FF_STEPS[n]:
                ff_part(m)
            if n == 3:
                xn_load.start()
            tick()

    xn_load = pltpu.make_async_copy(xn, s.hn, row_sem.at[5])

    scans = scan_lines(lines, s.dkv, s.fade, s.enter, s.reach, s.sent, s.got, scan_sems, False, between)
    xn_load.wait()
    s.xn = s.hn
    loop(lambda i: grad_chunk(count - 1 - i, s))
    dx_swap.start()

    lanes = s.bias_grad.shape[1]
    vectors = [s.norm_grad[...] / s.norm_gain[...], s.feed_part[...], s.bias_grad[...], s.gain_grad[...]]
    row = 0
    for v in vectors:
        for c in range(v.shape[1] // lanes):
            s.small_held[0, row : row + 1] = v[:, c * lanes : (c + 1) * lanes]
            row += 1
    s.small_held[0, row:] = jnp.zeros_like(s.small_held[0, row:])

    def small_copies(n):
        if n == 3:
            return [remote(s.small_held.at[3], s.small_got.at[3, 0], small_sems, (3, 0), tp_peer)]
        return [
            remote(s.small_held.at[n], s.small_got.at[n, d - 1], small_sems, (n, d - 1), {"seq": lines.peer(n, d)})
            for d in range(1, sizes[n])
        ]

    def small_step(n):
        if n > 0:
            for copy in small_copies(n - 1):
                copy.wait_recv()
            total = s.small_held[n - 1]
            if n <= 3:
                for d in range(sizes[n - 1] - 1):
                    total = total + s.small_got[n - 1, d]
                s.small_held[n] = total
            else:
                both = total + s.small_got[3, 0]
                wide = width // lanes
                for c in range(2 * wide):
                    (norm_out, feed_out)[c // wide][:, (c % wide) * lanes : (c % wide + 1) * lanes] = both[c : c + 1]
                bias_out[...] = total[2 * wide : 2 * wide + 1]
                for c in range(head_out.shape[1] // lanes):
                    head_out[:, c * lanes : (c + 1) * lanes] = total[2 * wide + 1 + c : 2 * wide + 2 + c]
        if n <= 3:
            for copy in small_copies(n):
                copy.start()

    most = s.wide_grads.shape[0]
    weight_loads = [
        pltpu.make_async_copy(down_weight.at[:most], s.wide_grads.at[:, :width], row_sem.at[6]),
        pltpu.make_async_copy(
            down_weight.at[most:], s.wide_grads.at[: hidden - most, width : 2 * width], row_sem.at[7]
        ),
    ]
    feed_rows = 2 * ROWS
    act_at, feed_at = hidden - most, hidden - most + feed_rows
    feed_ref = s.wide_grads.at[feed_at : feed_at + feed_rows, width : 2 * width]

    def feed_swap(n):
        return remote(feed_ref, feed_got.at[pl.ds(n * feed_rows, feed_rows)], swap_sems, 1 + steps + n, tp_peer)

    def feed_part(n):
        there = n < half // feed_rows
        start = (half if there else 0) + n % (half // feed_rows) * feed_rows
        load = pltpu.make_async_copy(
            act.at[start : start + feed_rows], s.wide_grads.at[act_at : act_at + feed_rows, width : width + hidden],
            feed_sem.at[n],
        )
        load.start()
        if n == 0:
            for copy in weight_loads:
                copy.wait()
        load.wait()
        left = s.wide_grads[act_at : act_at + feed_rows, width : width + hidden]
        part = dot(left[:, :most], s.wide_grads[:, :width])
        part = part + dot(left[:, most:], s.wide_grads[: hidden - most, width : 2 * width])
        if 0 < n <= half // feed_rows:
            feed_swap(n - 1).wait_send()
        s.wide_grads[feed_at : feed_at + feed_rows, width : 2 * width] = part.astype(BF)
        if there:
            feed_swap(n).start()

    def piece(n):
        if n == 0:
            for m in range(half // feed_rows):
                feed_swap(m).wait_recv()
        at = pl.ds(n * ROWS, ROWS)
        copies = [
            pltpu.make_async_copy(src.at[at], dst, piece_sem.at[n, i])
            for i, (src, dst) in enumerate(
                ((resid, s.wide.at[0]), (dresid, s.wide.at[1]), (tokens, s.narrow.at[0]), (feed_got, s.narrow.at[2]),
                 (dx_got, s.narrow.at[3]))
            )
        ]
        for copy in copies:
            copy.start()
        for copy in copies:
            copy.wait()
        lo = feed_at + n % 2 * ROWS
        feed = s.wide_grads[lo : lo + ROWS, width : 2 * width].astype(F32) + s.narrow[2].astype(F32)
        s.result[0] = (s.wide[0] + feed).astype(BF)
        dx = s.dx[mine(n)].astype(F32) + s.narrow[3].astype(F32)
        x = s.narrow[0].astype(F32)
        r = lax.rsqrt(jnp.mean(x * x, axis=-1, keepdims=True) + EPS)
        norm = x * r
        u = dx * s.norm_gain[...]
        s.result[1] = (s.wide[1] + r * (u - norm * jnp.mean(u * norm, axis=-1, keepdims=True))).astype(BF)
        ends = [
            pltpu.make_async_copy(s.result.at[i], out.at[at], piece_sem.at[n, 6 + i])
            for i, out in enumerate((block_out, tokens_out))
        ]
        for copy in ends:
            copy.start()
        for copy in ends:
            copy.wait()

    blocks = s.d_all.shape[1] // 128
    for n in range(-(-blocks // 4)):
        some = min(4, blocks - 4 * n)
        part = tn(s.xn[...], s.d_all[:, n * 512 : n * 512 + some * 128]).astype(BF)
        for c in range(some):
            s.mixer_units[4 * n + c] = part[:, c * 128 : (c + 1) * 128]
        small_step(n)
        tick()
    for copy in weight_loads:
        copy.start()
    dx_swap.wait()
    extras = [lambda n=n: feed_part(n) for n in range(half // feed_rows)]
    for n in range(half // feed_rows):
        extras.append(lambda n=n: feed_part(half // feed_rows + n))
        extras += [lambda m=m: piece(m) for m in (2 * n, 2 * n + 1)]
    step = 0
    while pending:
        tick()
        step += 1
        if step == 1:
            small_step(4)
        if extras and step % pieces == 0:
            extras.pop(0)()
    for extra in extras:
        extra()
    for copy in scans + [c for n in range(4) for c in small_copies(n)]:
        copy.wait_send()
    work.finish()


def back_call(rows, loaded, jobs, ticks, pieces):
    sizes = line_sizes(lax.axis_size("seq"))
    rounds = (sizes[0] * sizes[1] * sizes[2]).bit_length() - 1
    most = max(max(sizes) - 1, 1)
    half, width = rows[0].shape
    span, hidden = 2 * half, rows[2].shape[1]
    lanes, cols = loaded["wf"].shape[1], loaded["wq"].shape[1]
    small = (2 * width + lanes + cols) // lanes
    small = (small + -small % 8, lanes)
    mixer, ff = (3 * cols + lanes) // 128, 2 * hidden // 128
    out, down = (n * width // 128 // UNIT for n in (cols, hidden))
    shapes = [
        ((span, width), BF), ((span, width), BF), ((span, cols), BF), ((span, lanes), F32),
        ((span, 2 * hidden), BF), ((1, cols), F32), ((1, lanes), F32), ((1, width), F32), ((lanes, 2 * DH), F32),
        ((lanes, CH), F32), ((lanes, 2 * DH), F32), ((lanes, CH), F32), ((ff, UNIT, 128), BF),
        ((down, UNIT, 128), BF), ((mixer, UNIT, 128), BF), ((out, UNIT, 128), BF), ((1, width), F32), ((rounds, lanes + TAIL, 2 * DH), BF),
        ((rounds, lanes + TAIL, 2 * DH), BF), ((4, *small), F32), ((4, most, *small), F32), ((2, ROWS, width), F32),
        ((4, ROWS, width), BF), ((2, ROWS, width), BF),
    ]
    dma = pltpu.SemaphoreType.DMA
    scratch = [pltpu.VMEM(loaded[n].shape, loaded[n].dtype) for n in LOADED] + [pltpu.VMEM(*x) for x in shapes]
    scratch += [dma((len(LOADED),)), dma((8,)), dma((half // ROWS, 12)), dma((half // ROWS,))]
    scratch += [dma((rounds,))] * 2 + [dma((4, most))] * 2 + [dma((1 + half // ROWS + half // (2 * ROWS),))] * 2
    scratch += job_scratch(sizes, jobs, INSIDE)
    anywhere, vmem = pl.BlockSpec(memory_space=pl.ANY), pl.BlockSpec(memory_space=pltpu.VMEM)
    units = [(n, UNIT, 128) for n in (ff, down, mixer, out)]
    return pl.pallas_call(
        functools.partial(back_kernel, sizes, jobs, ticks, pieces),
        out_shape=[jax.ShapeDtypeStruct(x, F32) for x in ((1, width), (1, width), (1, lanes), (1, cols))]
        + [jax.ShapeDtypeStruct((half, width), BF)] * 4 + [jax.ShapeDtypeStruct((half, width), F32)]
        + [jax.ShapeDtypeStruct(x, BF) for x in units],
        in_specs=[anywhere] * (len(rows) + len(LOADED)),
        out_specs=[vmem] * 4 + [anywhere] * 9,
        scratch_shapes=scratch,
        compiler_params=pltpu.CompilerParams(collective_id=0, has_side_effects=True, vmem_limit_bytes=63 * 1024 * 1024),
        name="back",
    )(*rows, *[loaded[n] for n in LOADED])


FRONT_LOADED = (
    "wq", "wk", "wv", "wf", "norm_gain", "bias", "sums", "pairs", "gain", "wo", "feed_gain", "wg", "wu", "wd",
)
FRONT_SAVED = ("code", "xn", "q", "k", "v", "dsq", "dsk", "gate", "weight", "dzf", "logits", "kvs", "mixed", "normed", "resid")
WIDE = 256


def silu_pair(raw):
    s = 1.0 / (1.0 + jnp.exp(-raw))
    return (raw * s).astype(BF), (s * (1.0 + raw * (1.0 - s))).astype(BF)


def token_code(lengths, positions):
    start, code = 0, jnp.zeros(positions.shape, F32)
    for i in range(lengths.shape[0]):
        length = lengths[i]
        stop = start + (length + BUCKET - 1) // BUCKET * BUCKET
        mark = jnp.where(positions == start, 2.0, jnp.where(positions < start + length, 1.0, 0.0))
        code = jnp.where((positions >= start) & (positions < stop), mark, code)
        start = stop
    return code


def project_rows(i, s):
    at = pl.ds(pl.multiple_of(i * WIDE, WIDE), WIDE)
    x = s.tokens[at].astype(F32)
    xn = (x * lax.rsqrt(jnp.mean(x * x, axis=-1, keepdims=True) + EPS) * s.norm_gain[...]).astype(BF)
    s.xn[at] = xn
    s.q[at], s.dsq[at] = silu_pair(dot(xn, s.wq[...]))
    s.k[at], s.dsk[at] = silu_pair(dot(xn, s.wk[...]))
    s.v[at] = dot(xn, s.wv[...]).astype(BF)
    z = dot(xn, s.wf[...]) + s.bias[...]
    code = token_code(s.lengths, lax.broadcasted_iota(jnp.int32, z.shape, 0) + s.first_row + i * WIDE)
    s.code[at] = code
    valid, reset = code > 0.5, code > 1.5
    down = jnp.exp(-jnp.abs(z))
    gate = jnp.where(valid, (jnp.minimum(z, 0.0) - jnp.log(1.0 + down)) * (1.0 / NORMALIZER), 0.0)
    s.weight[at] = jnp.where(reset, 1.0, 1.0 - jnp.exp(gate))
    s.gate[at] = jnp.where(reset, RESET_LOG, gate)
    sig_neg = jnp.where(z > 0, down, 1.0) / (1.0 + down)
    s.dzf[at] = jnp.where(valid & (code < 1.5), sig_neg * (1.0 / NORMALIZER), 0.0)
    for n in range(WIDE // CH):
        c = i * (WIDE // CH) + n
        part = chunk_rows(c)
        gate = s.gate[part]
        last = jnp.exp(dot(s.sums[CH : 2 * CH], split3(gate)))
        s.adds[c] = run_part((last * s.weight[part]).astype(BF), s.k[part], s.v[part])
        s.fades[c] = jnp.broadcast_to(fade_of(gate), (gate.shape[1], CH))


def inner_chunk(c, s):
    at = chunk_rows(c)
    first, _, rows, cols, _ = decays(s.gate[at], s.weight[at], s.sums)
    s.first[at] = first
    for i in range(len(rows)):
        s.rows[i, at], s.cols[i, at] = rows[i], cols[i].astype(BF)
    q, k = s.q[at], s.k[at]
    s.logits[at] = through([nt(head(q, h), head(k, h)) for h in range(2)], rows, cols, s.pairs)


def mix_chunk(c, s):
    at = chunk_rows(c)
    q, v = s.q[at], s.v[at]
    first = s.first[at]
    rows, cols = ([ref[i, at] for i in range(len(HALVES) + 1)] for ref in (s.rows, s.cols))
    kv = s.enter[...]
    low = kv.astype(BF)
    s.kvs[c] = low
    outer = jnp.concatenate([nt(head(q, h), state(low, h)[:, :DH]) for h in range(2)], 1)
    logits = first * outer + s.logits[at]
    s.logits[at] = logits
    probs = softmax2(logits)
    reading = back_through([probs], rows, cols, s.pairs)
    spread = (probs * first).astype(BF)
    s.enter[...] = s.fades[c, :, :1] * kv + s.adds[c]
    code = s.code[at, :1]
    for h in range(2):
        mine = slice(h * DH, (h + 1) * DH)
        mixed = dot(slots(spread, h), state(low, h)[:, DH:]) + dot(reading[h].astype(BF), head(v, h))
        s.mixed[at, mine] = mixed
        r = lax.rsqrt(jnp.mean(mixed * mixed, axis=-1, keepdims=True) + EPS)
        s.normed[at, mine] = (mixed * jnp.where(code > 0.5, r, 0.0) * s.gain[:, mine]).astype(BF)


def feed_rows(n, s):
    at = pl.ds(n * WIDE, WIDE)
    hn, cot = s.hidden[at], s.cot[at]
    wide = s.wg.shape[1]
    slot = n % 2
    for c in range(0, wide, 512):
        some = slice(c, min(c + 512, wide))
        gate, up, dact = dot(hn, s.wg[:, some]), dot(hn, s.wu[:, some]), nt(cot, s.wd[some])
        sig = 1.0 / (1.0 + jnp.exp(-gate))
        soft = gate * sig
        s.act[slot, :, some] = (soft * up).astype(BF)
        s.dgate[slot, :, some] = (dact * up * sig * (1.0 + gate * (1.0 - sig))).astype(BF)
        s.dup[slot, :, some] = (dact * soft).astype(BF)
    s.dh[at] = (nt(s.dgate[slot], s.wg[...]) + nt(s.dup[slot], s.wu[...])).astype(BF)


def front_kernel(sizes, *refs):
    refs = list(refs)
    take = lambda n: [refs.pop(0) for _ in range(n)]
    lengths, tokens_own, cot_own = take(3)
    sources, saves = take(len(FRONT_LOADED)), take(len(FRONT_SAVED))
    hidden_out, cot_out, act_out, dgate_out, dup_out, dh_out, dh_got = take(7)
    s = Bag()
    for name in FRONT_LOADED + FRONT_SAVED:
        setattr(s, name, refs.pop(0))
    for name in ("tokens", "total", "fade", "enter", "reach", "sent", "got", "attn", "attn_got", "hidden", "cot", "act",
                 "dgate", "dup", "first", "rows", "cols", "adds", "fades"):
        setattr(s, name, refs.pop(0))
    s.lengths = lengths
    s.dh = s.xn
    load_sem, save_sem, row_sem, part_sem = take(4)
    scan_sems, swap_sems = take(2), take(2)
    lines = Lines(sizes)
    half, width = tokens_own.shape
    count = 2 * half // CH
    tp_peer = {"tp": 1 - lines.half}
    own_rows = pl.ds(pl.multiple_of(lines.half * half, half), half)
    loads = [pltpu.make_async_copy(x, getattr(s, n), load_sem.at[i]) for i, (n, x) in enumerate(zip(FRONT_LOADED, sources))]
    late = loads[FRONT_LOADED.index("wo") :] + [pltpu.make_async_copy(cot_own, s.cot.at[pl.ds(0, half)], row_sem.at[1])]
    loads = loads[: FRONT_LOADED.index("wo")] + [pltpu.make_async_copy(tokens_own, s.tokens.at[own_rows], row_sem.at[0])]
    for copy in loads:
        copy.start()
    s.first_row = lines.index * (2 * half)
    lines.greet()
    tokens_swap = remote(tokens_own, s.tokens.at[own_rows], swap_sems, 0, tp_peer)
    tokens_swap.start()
    cot_swap = remote(cot_own, s.cot.at[pl.ds(half, half)], swap_sems, 1, tp_peer)
    cot_swap.start()
    for copy in late:
        copy.start()
    for copy in loads:
        copy.wait()

    def save(*names):
        for n in names:
            i = FRONT_SAVED.index(n)
            pltpu.make_async_copy(getattr(s, n), saves[i], save_sem.at[i]).start()

    for side in (lines.half, 1 - lines.half):
        lax.fori_loop(0, half // WIDE, lambda i, carry: (project_rows(side * (half // WIDE) + i, s), carry)[1], 0)
        if side is lines.half:
            tokens_swap.wait()
    total, fade = s.adds[0], s.fades[0]
    for c in range(1, count):
        total = s.fades[c, :, :1] * total + s.adds[c]
        fade = fade * s.fades[c]
    s.total[...], s.fade[...] = total, fade
    early = ("code", "xn", "q", "k", "v", "dsq", "dsk", "gate", "weight", "dzf")
    save(*early)

    def between(n):
        if n < 4:
            for c in range(n * count // 4, (n + 1) * count // 4):
                inner_chunk(c, s)

    scans = scan_lines(lines, s.total, s.fade, s.enter, s.reach, s.sent, s.got, scan_sems, True, between)
    lax.fori_loop(0, count, lambda c, carry: (mix_chunk(c, s), carry)[1], 0)
    save("logits", "kvs", "mixed", "normed")

    for copy in late:
        copy.wait()
    steps = half // WIDE
    swaps = [
        remote(s.attn.at[pl.ds(n * WIDE, WIDE)], s.attn_got.at[pl.ds(n * WIDE, WIDE)], swap_sems, 2 + n, tp_peer)
        for n in range(steps)
    ]
    for n in range(2 * steps):
        side = (1 - lines.half) if n < steps else lines.half
        rows = pl.ds(pl.multiple_of(side * half + n % steps * WIDE, WIDE), WIDE)
        s.attn[n * WIDE : (n + 1) * WIDE] = dot(s.normed[rows], s.wo[...]).astype(BF)
        if n < steps:
            swaps[n].start()
    for n in range(steps):
        at = pl.ds(n * WIDE, WIDE)
        swaps[n].wait_recv()
        attn = s.attn[half + n * WIDE : half + (n + 1) * WIDE].astype(F32) + s.attn_got[at].astype(F32)
        x = s.tokens[pl.ds(pl.multiple_of(lines.half * half + n * WIDE, WIDE), WIDE)].astype(F32) + attn
        s.resid[at] = x
        r = lax.rsqrt(jnp.mean(x * x, axis=-1, keepdims=True) + EPS)
        s.hidden[at] = (x * r * s.feed_gain[...]).astype(BF)
        there = s.hidden.at[pl.ds(half + n * WIDE, WIDE)]
        swaps.append(remote(s.hidden.at[at], there, swap_sems, 2 + steps + n, tp_peer))
        swaps[-1].start()
    save("resid")
    cot_swap.wait()
    cot_save = pltpu.make_async_copy(s.cot, cot_out, row_sem.at[2])
    cot_save.start()

    outs = ((s.act, act_out), (s.dgate, dgate_out), (s.dup, dup_out))
    part = lambda n: [
        pltpu.make_async_copy(src.at[n % 2], dst.at[pl.ds(n * WIDE, WIDE)], part_sem.at[n, i])
        for i, (src, dst) in enumerate(outs)
    ]
    back = [
        remote(s.dh.at[pl.ds(half + n * WIDE, WIDE)], dh_got.at[pl.ds(n * WIDE, WIDE)], swap_sems, 2 + 2 * steps + n, tp_peer)
        for n in range(steps)
    ]
    busy = {}
    at_xn = FRONT_SAVED.index("xn")
    pltpu.make_async_copy(s.xn, saves[at_xn], save_sem.at[at_xn]).wait()
    for n in [0] + list(range(steps, 2 * steps)) + list(range(1, steps)):
        if n % 2 in busy:
            for copy in busy[n % 2]:
                copy.wait()
        if n >= steps:
            swaps[n].wait_recv()
        feed_rows(n, s)
        busy[n % 2] = part(n)
        for copy in busy[n % 2]:
            copy.start()
        if n >= steps:
            back[n - steps].start()
    ends = [
        pltpu.make_async_copy(s.hidden, hidden_out, row_sem.at[3]),
        pltpu.make_async_copy(s.dh.at[pl.ds(0, half)], dh_out, row_sem.at[4]),
    ]
    for copy in ends:
        copy.start()
    for copy in ends + busy[0] + busy[1] + [cot_save]:
        copy.wait()
    for i, n in enumerate(FRONT_SAVED):
        if i != at_xn:
            pltpu.make_async_copy(getattr(s, n), saves[i], save_sem.at[i]).wait()
    for copy in back:
        copy.wait()
    for copy in scans + swaps:
        copy.wait_send()


def front_call(lengths, tokens, cot, loaded):
    sizes = line_sizes(lax.axis_size("seq"))
    rounds = (sizes[0] * sizes[1] * sizes[2]).bit_length() - 1
    half, width = tokens.shape
    span = 2 * half
    lanes, cols, hidden = (loaded[n].shape[1] for n in ("wf", "wq", "wg"))
    levels = len(HALVES) + 1
    shapes = dict(
        code=((span, lanes), F32),
        xn=((span, width), BF), q=((span, cols), BF), k=((span, cols), BF), v=((span, cols), BF), dsq=((span, cols), BF),
        dsk=((span, cols), BF), gate=((span, lanes), F32), weight=((span, lanes), F32), dzf=((span, lanes), F32),
        logits=((span, lanes), F32), kvs=((span // CH, lanes, 2 * DH), BF), mixed=((span, cols), F32),
        normed=((span, cols), BF), resid=((half, width), F32),
    )
    others = [
        ((span, width), BF), ((lanes, 2 * DH), F32), ((lanes, CH), F32), ((lanes, 2 * DH), F32), ((lanes, CH), F32),
        ((rounds, lanes + TAIL, 2 * DH), BF), ((rounds, lanes + TAIL, 2 * DH), BF), ((span, width), BF), ((half, width), BF),
        ((span, width), BF), ((span, width), BF), ((2, WIDE, hidden), BF), ((2, WIDE, hidden), BF), ((2, WIDE, hidden), BF),
        ((span, lanes), F32), ((levels, span, lanes), F32), ((levels, span, lanes), BF),
        ((span // CH, lanes, 2 * DH), F32), ((span // CH, lanes, CH), F32),
    ]
    more = [((span, width), BF)] * 2 + [((span, hidden), BF)] * 3 + [((half, width), BF)] * 2
    dma = pltpu.SemaphoreType.DMA
    scratch = [pltpu.VMEM(loaded[n].shape, loaded[n].dtype) for n in FRONT_LOADED]
    scratch += [pltpu.VMEM(*shapes[n]) for n in FRONT_SAVED] + [pltpu.VMEM(*x) for x in others]
    scratch += [dma((len(FRONT_LOADED),)), dma((len(FRONT_SAVED),)), dma((5,)), dma((span // WIDE, 3))]
    scratch += [dma((rounds,))] * 2 + [dma((2 + 3 * (half // WIDE),))] * 2
    anywhere = pl.BlockSpec(memory_space=pl.ANY)
    outs = pl.pallas_call(
        functools.partial(front_kernel, sizes),
        out_shape=[jax.ShapeDtypeStruct(*x) for x in [shapes[n] for n in FRONT_SAVED] + more],
        in_specs=[pl.BlockSpec(memory_space=pltpu.SMEM)] + [anywhere] * (2 + len(FRONT_LOADED)),
        out_specs=[anywhere] * (len(FRONT_SAVED) + len(more)),
        scratch_shapes=scratch,
        compiler_params=pltpu.CompilerParams(collective_id=1, has_side_effects=True, vmem_limit_bytes=63 * 1024 * 1024),
        name="front",
    )(lengths, tokens, cot, *[loaded[n] for n in FRONT_LOADED])
    return dict(zip(FRONT_SAVED, outs)), outs[len(FRONT_SAVED) :]


def widen_kernel(parts, *refs):
    for (which, blocks), out_ref in zip(parts, refs[-len(parts) :]):
        for c, block in enumerate(blocks):
            out_ref[:, c * 128 : (c + 1) * 128] = refs[which][block].astype(F32)


def widen(arrays, parts, steps):
    return pl.pallas_call(
        functools.partial(widen_kernel, parts),
        grid=(steps,),
        in_specs=[pl.BlockSpec((a.shape[0], a.shape[1] // steps, 128), lambda i: (0, i, 0)) for a in arrays],
        out_specs=[pl.BlockSpec((arrays[w].shape[1] // steps, len(b) * 128), lambda i: (i, 0)) for w, b in parts],
        out_shape=[jax.ShapeDtypeStruct((arrays[w].shape[1], len(b) * 128), F32) for w, b in parts],
        compiler_params=pltpu.CompilerParams(dimension_semantics=("arbitrary",), vmem_limit_bytes=VMEM_LIMIT),
        name="widen",
    )(*arrays)


X, Y, Z = 0, 1, 2
PIECES = 4
JOBS = (
    (2, 0, 5, (X, Y, Z)),
    (1, 0, 4, (Y, X, Z)),
    (2, 5, 2, (X, Y, Z)),
    (1, 4, 1, (X, Y, Z)),
    (3, 0, 1, (Z, Y, X)),
    (3, 1, 3, (Y, Z, X)),
    (0, 0, 6, (X, Y, Z)),
    (0, 6, 5, (Y, X, Z)),
    (1, 5, 2, (Y, Z, X)),
    (0, 11, 8, (X, Y, Z)),
    (2, 7, 3, (Y, Z, X)),
    (0, 19, 3, (Y, X, Z)),
    (2, 10, 3, (X, Y, Z)),
    (1, 7, 4, (X, Y, Z)),
)
TICKS = (
    (), ((1, 0), (3, 0),), ((8, 0),), ((13, 0),), ((3, 1),), (), (), (), ((1, 1),), (), (), ((13, 1), (8, 1),),
    ((3, 2), (1, 2), (6, 0),), ((13, 2), (8, 2), (3, 3), (7, 0),), ((1, 3), (9, 0),),
    ((13, 3), (3, 4), (6, 1), (8, 3), (11, 0),), ((7, 1), (1, 4), (3, 5), (6, 2),), ((13, 4),), (),
    ((9, 1), (8, 4), (11, 1),), ((6, 3),), ((13, 5), (7, 2),), ((8, 5),), ((1, 5),), ((3, 6),), ((9, 2),),
    ((6, 4), (11, 2), (2, 0),), ((10, 0),), ((12, 0),), ((8, 6),), ((7, 3),), ((0, 0),), ((13, 6),), ((1, 6),),
    ((2, 1),), ((9, 3),), ((11, 3),), ((6, 5),), ((12, 1),), ((7, 4),), ((10, 1),), ((5, 0),), ((2, 2),), ((12, 2),),
    ((0, 1),), ((9, 4),), ((11, 4),), ((5, 1),), ((4, 0),), ((10, 2),), ((0, 2),), ((2, 3),), ((6, 6),), ((12, 3),),
    ((7, 5),), ((9, 5),), ((11, 5),), ((5, 2),), ((10, 3),), ((4, 1),), ((7, 6),), ((0, 3),), ((2, 4),), ((12, 4),),
    ((11, 6),), ((4, 2),), ((9, 6),), ((2, 5),), ((5, 3),), ((10, 4),), ((4, 3),), ((0, 4),), ((12, 5),), ((2, 6),),
    ((5, 4),), ((4, 4),), ((10, 5),), ((0, 5),), ((4, 5),), ((12, 6),), ((5, 5),), ((10, 6),), ((4, 6),), ((5, 6),),
    ((0, 6),),
)


def token_code(lengths, positions):
    start, code = 0, jnp.zeros(positions.shape, F32)
    for i in range(lengths.shape[0]):
        length = lengths[i]
        stop = start + (length + BUCKET - 1) // BUCKET * BUCKET
        mark = jnp.where(positions == start, 2.0, jnp.where(positions < start + length, 1.0, 0.0))
        code = jnp.where((positions >= start) & (positions < stop), mark, code)
        start = stop
    return code


def project_rows(i, s):
    at = pl.ds(pl.multiple_of(i * WIDE, WIDE), WIDE)
    x = s.tokens[at].astype(F32)
    xn = (x * lax.rsqrt(jnp.mean(x * x, axis=-1, keepdims=True) + EPS) * s.norm_gain[...]).astype(BF)
    s.xn[at] = xn
    s.q[at], s.dsq[at] = silu_pair(dot(xn, s.wq[...]))
    s.k[at], s.dsk[at] = silu_pair(dot(xn, s.wk[...]))
    s.v[at] = dot(xn, s.wv[...]).astype(BF)
    z = dot(xn, s.wf[...]) + s.bias[...]
    code = token_code(s.lengths, lax.broadcasted_iota(jnp.int32, z.shape, 0) + s.first_row + i * WIDE)
    s.code[at] = code
    valid, reset = code > 0.5, code > 1.5
    down = jnp.exp(-jnp.abs(z))
    gate = jnp.where(valid, (jnp.minimum(z, 0.0) - jnp.log(1.0 + down)) * (1.0 / NORMALIZER), 0.0)
    s.weight[at] = jnp.where(reset, 1.0, 1.0 - jnp.exp(gate))
    s.gate[at] = jnp.where(reset, RESET_LOG, gate)
    sig_neg = jnp.where(z > 0, down, 1.0) / (1.0 + down)
    s.dzf[at] = jnp.where(valid & (code < 1.5), sig_neg * (1.0 / NORMALIZER), 0.0)
    for n in range(WIDE // CH):
        c = i * (WIDE // CH) + n
        part = chunk_rows(c)
        gate = s.gate[part]
        last = jnp.exp(dot(s.sums[CH : 2 * CH], split3(gate)))
        s.adds[c] = run_part((last * s.weight[part]).astype(BF), s.k[part], s.v[part])
        s.fades[c] = jnp.broadcast_to(fade_of(gate), (gate.shape[1], CH))


def inner_chunk(c, s):
    at = chunk_rows(c)
    first, _, rows, cols, _ = decays(s.gate[at], s.weight[at], s.sums)
    s.first[at] = first
    for i in range(len(rows)):
        s.rows[i, at], s.cols[i, at] = rows[i], cols[i].astype(BF)
    q, k = s.q[at], s.k[at]
    s.logits[at] = through([nt(head(q, h), head(k, h)) for h in range(2)], rows, cols, s.pairs)


def mix_chunk(c, s):
    at = chunk_rows(c)
    q, v = s.q[at], s.v[at]
    first = s.first[at]
    rows, cols = ([ref[i, at] for i in range(len(HALVES) + 1)] for ref in (s.rows, s.cols))
    kv = s.enter[...]
    low = kv.astype(BF)
    s.kvs[c] = low
    outer = jnp.concatenate([nt(head(q, h), state(low, h)[:, :DH]) for h in range(2)], 1)
    logits = first * outer + s.logits[at]
    s.logits[at] = logits
    probs = softmax2(logits)
    reading = back_through([probs], rows, cols, s.pairs)
    spread = (probs * first).astype(BF)
    s.enter[...] = s.fades[c, :, :1] * kv + s.adds[c]
    code = s.code[at, :1]
    for h in range(2):
        mine = slice(h * DH, (h + 1) * DH)
        mixed = dot(slots(spread, h), state(low, h)[:, DH:]) + dot(reading[h].astype(BF), head(v, h))
        s.mixed[at, mine] = mixed
        r = lax.rsqrt(jnp.mean(mixed * mixed, axis=-1, keepdims=True) + EPS)
        s.normed[at, mine] = (mixed * jnp.where(code > 0.5, r, 0.0) * s.gain[:, mine]).astype(BF)


def feed_rows(n, s):
    at = pl.ds(n * WIDE, WIDE)
    hn, cot = s.hidden[at], s.cot[at]
    wide = s.wg.shape[1]
    slot = n % 2
    for c in range(0, wide, 512):
        some = slice(c, min(c + 512, wide))
        gate, up, dact = dot(hn, s.wg[:, some]), dot(hn, s.wu[:, some]), nt(cot, s.wd[some])
        sig = 1.0 / (1.0 + jnp.exp(-gate))
        soft = gate * sig
        s.act[slot, :, some] = (soft * up).astype(BF)
        s.dgate[slot, :, some] = (dact * up * sig * (1.0 + gate * (1.0 - sig))).astype(BF)
        s.dup[slot, :, some] = (dact * soft).astype(BF)
    s.dh[at] = (nt(s.dgate[slot], s.wg[...]) + nt(s.dup[slot], s.wu[...])).astype(BF)


def front_kernel(sizes, *refs):
    refs = list(refs)
    take = lambda n: [refs.pop(0) for _ in range(n)]
    lengths, tokens_own, cot_own = take(3)
    sources, saves = take(len(FRONT_LOADED)), take(len(FRONT_SAVED))
    hidden_out, cot_out, act_out, dgate_out, dup_out, dh_out, dh_got = take(7)
    s = Bag()
    for name in FRONT_LOADED + FRONT_SAVED:
        setattr(s, name, refs.pop(0))
    for name in ("tokens", "total", "fade", "enter", "reach", "sent", "got", "attn", "attn_got", "hidden", "cot", "act",
                 "dgate", "dup", "first", "rows", "cols", "adds", "fades"):
        setattr(s, name, refs.pop(0))
    s.lengths = lengths
    s.dh = s.xn
    load_sem, save_sem, row_sem, part_sem = take(4)
    scan_sems, swap_sems = take(2), take(2)
    lines = Lines(sizes)
    half, width = tokens_own.shape
    count = 2 * half // CH
    tp_peer = {"tp": 1 - lines.half}
    own_rows = pl.ds(pl.multiple_of(lines.half * half, half), half)
    loads = [pltpu.make_async_copy(x, getattr(s, n), load_sem.at[i]) for i, (n, x) in enumerate(zip(FRONT_LOADED, sources))]
    late = loads[FRONT_LOADED.index("wo") :] + [pltpu.make_async_copy(cot_own, s.cot.at[pl.ds(0, half)], row_sem.at[1])]
    loads = loads[: FRONT_LOADED.index("wo")] + [pltpu.make_async_copy(tokens_own, s.tokens.at[own_rows], row_sem.at[0])]
    for copy in loads:
        copy.start()
    s.first_row = lines.index * (2 * half)
    lines.greet()
    tokens_swap = remote(tokens_own, s.tokens.at[own_rows], swap_sems, 0, tp_peer)
    tokens_swap.start()
    cot_swap = remote(cot_own, s.cot.at[pl.ds(half, half)], swap_sems, 1, tp_peer)
    cot_swap.start()
    for copy in late:
        copy.start()
    for copy in loads:
        copy.wait()

    def save(*names):
        for n in names:
            i = FRONT_SAVED.index(n)
            pltpu.make_async_copy(getattr(s, n), saves[i], save_sem.at[i]).start()

    for side in (lines.half, 1 - lines.half):
        lax.fori_loop(0, half // WIDE, lambda i, carry: (project_rows(side * (half // WIDE) + i, s), carry)[1], 0)
        if side is lines.half:
            tokens_swap.wait()
    total, fade = s.adds[0], s.fades[0]
    for c in range(1, count):
        total = s.fades[c, :, :1] * total + s.adds[c]
        fade = fade * s.fades[c]
    s.total[...], s.fade[...] = total, fade
    early = ("code", "xn", "q", "k", "v", "dsq", "dsk", "gate", "weight", "dzf")
    save(*early)

    def between(n):
        if n < 4:
            for c in range(n * count // 4, (n + 1) * count // 4):
                inner_chunk(c, s)

    scans = scan_lines(lines, s.total, s.fade, s.enter, s.reach, s.sent, s.got, scan_sems, True, between)
    lax.fori_loop(0, count, lambda c, carry: (mix_chunk(c, s), carry)[1], 0)
    save("logits", "kvs", "mixed", "normed")

    for copy in late:
        copy.wait()
    steps = half // WIDE
    swaps = [
        remote(s.attn.at[pl.ds(n * WIDE, WIDE)], s.attn_got.at[pl.ds(n * WIDE, WIDE)], swap_sems, 2 + n, tp_peer)
        for n in range(steps)
    ]
    for n in range(2 * steps):
        side = (1 - lines.half) if n < steps else lines.half
        rows = pl.ds(pl.multiple_of(side * half + n % steps * WIDE, WIDE), WIDE)
        s.attn[n * WIDE : (n + 1) * WIDE] = dot(s.normed[rows], s.wo[...]).astype(BF)
        if n < steps:
            swaps[n].start()
    for n in range(steps):
        at = pl.ds(n * WIDE, WIDE)
        swaps[n].wait_recv()
        attn = s.attn[half + n * WIDE : half + (n + 1) * WIDE].astype(F32) + s.attn_got[at].astype(F32)
        x = s.tokens[pl.ds(pl.multiple_of(lines.half * half + n * WIDE, WIDE), WIDE)].astype(F32) + attn
        s.resid[at] = x
        r = lax.rsqrt(jnp.mean(x * x, axis=-1, keepdims=True) + EPS)
        s.hidden[at] = (x * r * s.feed_gain[...]).astype(BF)
        there = s.hidden.at[pl.ds(half + n * WIDE, WIDE)]
        swaps.append(remote(s.hidden.at[at], there, swap_sems, 2 + steps + n, tp_peer))
        swaps[-1].start()
    save("resid")
    cot_swap.wait()
    cot_save = pltpu.make_async_copy(s.cot, cot_out, row_sem.at[2])
    cot_save.start()

    outs = ((s.act, act_out), (s.dgate, dgate_out), (s.dup, dup_out))
    part = lambda n: [
        pltpu.make_async_copy(src.at[n % 2], dst.at[pl.ds(n * WIDE, WIDE)], part_sem.at[n, i])
        for i, (src, dst) in enumerate(outs)
    ]
    back = [
        remote(s.dh.at[pl.ds(half + n * WIDE, WIDE)], dh_got.at[pl.ds(n * WIDE, WIDE)], swap_sems, 2 + 2 * steps + n, tp_peer)
        for n in range(steps)
    ]
    busy = {}
    at_xn = FRONT_SAVED.index("xn")
    pltpu.make_async_copy(s.xn, saves[at_xn], save_sem.at[at_xn]).wait()
    for n in [0] + list(range(steps, 2 * steps)) + list(range(1, steps)):
        if n % 2 in busy:
            for copy in busy[n % 2]:
                copy.wait()
        if n >= steps:
            swaps[n].wait_recv()
        feed_rows(n, s)
        busy[n % 2] = part(n)
        for copy in busy[n % 2]:
            copy.start()
        if n >= steps:
            back[n - steps].start()
    ends = [
        pltpu.make_async_copy(s.hidden, hidden_out, row_sem.at[3]),
        pltpu.make_async_copy(s.dh.at[pl.ds(0, half)], dh_out, row_sem.at[4]),
    ]
    for copy in ends:
        copy.start()
    for copy in ends + busy[0] + busy[1] + [cot_save]:
        copy.wait()
    for i, n in enumerate(FRONT_SAVED):
        if i != at_xn:
            pltpu.make_async_copy(getattr(s, n), saves[i], save_sem.at[i]).wait()
    for copy in back:
        copy.wait()
    for copy in scans + swaps:
        copy.wait_send()


def front_call(lengths, tokens, cot, loaded):
    sizes = line_sizes(lax.axis_size("seq"))
    rounds = (sizes[0] * sizes[1] * sizes[2]).bit_length() - 1
    half, width = tokens.shape
    span = 2 * half
    lanes, cols, hidden = (loaded[n].shape[1] for n in ("wf", "wq", "wg"))
    levels = len(HALVES) + 1
    shapes = dict(
        code=((span, lanes), F32),
        xn=((span, width), BF), q=((span, cols), BF), k=((span, cols), BF), v=((span, cols), BF), dsq=((span, cols), BF),
        dsk=((span, cols), BF), gate=((span, lanes), F32), weight=((span, lanes), F32), dzf=((span, lanes), F32),
        logits=((span, lanes), F32), kvs=((span // CH, lanes, 2 * DH), BF), mixed=((span, cols), F32),
        normed=((span, cols), BF), resid=((half, width), F32),
    )
    others = [
        ((span, width), BF), ((lanes, 2 * DH), F32), ((lanes, CH), F32), ((lanes, 2 * DH), F32), ((lanes, CH), F32),
        ((rounds, lanes + TAIL, 2 * DH), BF), ((rounds, lanes + TAIL, 2 * DH), BF), ((span, width), BF), ((half, width), BF),
        ((span, width), BF), ((span, width), BF), ((2, WIDE, hidden), BF), ((2, WIDE, hidden), BF), ((2, WIDE, hidden), BF),
        ((span, lanes), F32), ((levels, span, lanes), F32), ((levels, span, lanes), BF),
        ((span // CH, lanes, 2 * DH), F32), ((span // CH, lanes, CH), F32),
    ]
    more = [((span, width), BF)] * 2 + [((span, hidden), BF)] * 3 + [((half, width), BF)] * 2
    dma = pltpu.SemaphoreType.DMA
    scratch = [pltpu.VMEM(loaded[n].shape, loaded[n].dtype) for n in FRONT_LOADED]
    scratch += [pltpu.VMEM(*shapes[n]) for n in FRONT_SAVED] + [pltpu.VMEM(*x) for x in others]
    scratch += [dma((len(FRONT_LOADED),)), dma((len(FRONT_SAVED),)), dma((5,)), dma((span // WIDE, 3))]
    scratch += [dma((rounds,))] * 2 + [dma((2 + 3 * (half // WIDE),))] * 2
    anywhere = pl.BlockSpec(memory_space=pl.ANY)
    outs = pl.pallas_call(
        functools.partial(front_kernel, sizes),
        out_shape=[jax.ShapeDtypeStruct(*x) for x in [shapes[n] for n in FRONT_SAVED] + more],
        in_specs=[pl.BlockSpec(memory_space=pltpu.SMEM)] + [anywhere] * (2 + len(FRONT_LOADED)),
        out_specs=[anywhere] * (len(FRONT_SAVED) + len(more)),
        scratch_shapes=scratch,
        compiler_params=pltpu.CompilerParams(collective_id=1, has_side_effects=True, vmem_limit_bytes=63 * 1024 * 1024),
        name="front",
    )(lengths, tokens, cot, *[loaded[n] for n in FRONT_LOADED])
    return dict(zip(FRONT_SAVED, outs)), outs[len(FRONT_SAVED) :]


def widen_kernel(parts, *refs):
    for (which, blocks), out_ref in zip(parts, refs[-len(parts) :]):
        for c, block in enumerate(blocks):
            out_ref[:, c * 128 : (c + 1) * 128] = refs[which][block].astype(F32)


def widen(arrays, parts, steps):
    return pl.pallas_call(
        functools.partial(widen_kernel, parts),
        grid=(steps,),
        in_specs=[pl.BlockSpec((a.shape[0], a.shape[1] // steps, 128), lambda i: (0, i, 0)) for a in arrays],
        out_specs=[pl.BlockSpec((arrays[w].shape[1] // steps, len(b) * 128), lambda i: (i, 0)) for w, b in parts],
        out_shape=[jax.ShapeDtypeStruct((arrays[w].shape[1], len(b) * 128), F32) for w, b in parts],
        compiler_params=pltpu.CompilerParams(dimension_semantics=("arbitrary",), vmem_limit_bytes=VMEM_LIMIT),
        name="widen",
    )(*arrays)


X, Y, Z = 0, 1, 2
PIECES = 4
JOBS = (
    (2, 0, 1, (Y, X, Z)),
    (2, 1, 4, (Y, X, Z)),
    (3, 0, 4, (Y, X, Z)),
    (1, 0, 3, (Y, Z, X)),
    (0, 0, 4, (X, Y, Z)),
    (2, 5, 3, (X, Z, Y)),
    (1, 3, 4, (X, Y, Z)),
    (0, 4, 8, (Y, X, Z)),
    (2, 8, 3, (X, Y, Z)),
    (0, 12, 6, (X, Y, Z)),
    (2, 11, 2, (Z, Y, X)),
    (0, 18, 3, (X, Y, Z)),
    (1, 7, 4, (Y, X, Z)),
    (0, 21, 1, (Y, X, Z)),
)
TICKS = (
    (), ((3, 0),), ((6, 0),), ((12, 0),), (), (), (), ((3, 1),), (), (), ((6, 1),), (), ((12, 1), (3, 2), (4, 0),),
    ((6, 2), (7, 0),), ((12, 2), (3, 3), (9, 0),), ((6, 3), (4, 1), (3, 4),), ((12, 3), (7, 1), (2, 0), (11, 0),),
    ((4, 2), (9, 1), (6, 4),), (), (), ((3, 5),), ((2, 1), (7, 2),), ((12, 4),), (), ((4, 3), (9, 2), (11, 1),), (),
    ((1, 0),), ((2, 2), (6, 5),), ((7, 3),), ((12, 5),), ((5, 0),), ((3, 6),), ((4, 4),), ((8, 0),), ((11, 2),),
    ((6, 6),), ((9, 3),), ((0, 0),), ((10, 0),), ((1, 1),), ((2, 3),), ((5, 1),), ((8, 1),), ((12, 6),), ((7, 4),),
    ((1, 2),), ((11, 3),), ((4, 5),), ((0, 1),), ((13, 0),), ((8, 2),), ((9, 4),), ((7, 5),), ((13, 1),), ((10, 1),),
    ((9, 5),), ((4, 6),), ((0, 2),), ((13, 2),), ((2, 4),), ((5, 2),), ((1, 3),), ((9, 6),), ((7, 6),), ((11, 4),),
    ((10, 2),), ((5, 3),), ((2, 5),), ((8, 3),), ((10, 3),), ((0, 3),), ((11, 5),), ((13, 3),), ((5, 4),), ((10, 4),),
    ((1, 4),), ((11, 6),), ((8, 4),), ((0, 4),), ((2, 6),), ((13, 4),), ((10, 5),), ((1, 5),), ((0, 5),), ((8, 5),),
    ((13, 5),), ((5, 5),), ((8, 6),), ((1, 6),), ((0, 6),), ((10, 6),), ((13, 6),), ((5, 6),),
)


def per_device(
    tokens, norm_gain, query_weight, key_weight, value_weight, forget_weight, forget_bias, head_gain,
    out_weight, feed_gain, gate_weight, up_weight, down_weight, lengths, cotangent,
):
    half, width = tokens.shape
    span = 2 * half
    cols = query_weight.shape[1]
    lanes = forget_weight.shape[1]
    sums, pairs, flipped, back = tables()
    sums, back = jnp.asarray(sums, BF), jnp.asarray(back, BF)
    pairs, flipped = jnp.asarray(pairs, BF), jnp.asarray(flipped, BF)

    weights = dict(wq=query_weight, wk=key_weight, wv=value_weight, wf=forget_weight, wo=out_weight)
    shared = dict(sums=sums, pairs=pairs, gain=head_gain[None], norm_gain=norm_gain[None])
    wide = dict(wg=gate_weight, wu=up_weight, wd=down_weight, bias=forget_bias[None], feed_gain=feed_gain[None])
    saved, (hidden, cot, act, dgate, dup, dh_own, dh_got) = front_call(lengths, tokens, cotangent, dict(weights, **shared, **wide))
    resid = saved["resid"]
    loaded = dict(weights, **shared, flipped=flipped, back=back, feed_gain=feed_gain[None])
    for name in ("code", "q", "k", "v", "dsq", "dsk", "gate", "weight", "dzf", "logits", "kvs", "mixed", "normed"):
        loaded[name] = saved[name]
    rows = (dh_own, dh_got, act, cot, hidden, dgate, dup, down_weight, resid, tokens, saved["xn"])
    norm_sum, feed_sum, bias_sum, head_sum, block_out, tokens_grad, _, _, _, *sums = back_call(rows, loaded, JOBS, TICKS, PIECES)
    ff_sum, down_sum, mixer_sum, out_sum = sums
    blocks, ff_blocks, wide = cols // 128, gate_weight.shape[1] // 128, tuple(range(width // 128))
    which = lambda up: tuple(4 * (c // 2) + 2 * up + c % 2 - (up if c == ff_blocks - 1 else 0) for c in range(ff_blocks))
    parts = [(0, tuple(range(i * blocks, (i + 1) * blocks))) for i in range(3)] + [(0, (3 * blocks,)), (1, wide)]
    parts += [(2, which(0)), (2, which(1)), (3, wide)]
    arrays = [mixer_sum, out_sum.reshape(-1, cols, 128), ff_sum, down_sum.reshape(-1, down_weight.shape[0], 128)]
    query_sum, key_sum, value_sum, forget_sum, out_grad, gate_grad, up_grad, down_grad = widen(arrays, parts, 8)
    return (
        block_out, tokens_grad, norm_sum[0], query_sum, key_sum, value_sum, forget_sum, bias_sum[0], head_sum[0], out_grad,
        feed_sum[0], gate_grad, up_grad, down_grad,
    )


def solution(mesh):
    rows, by_col, by_row = P(("seq", "tp"), None), P(None, "tp"), P("tp", None)
    return jax.shard_map(
        per_device,
        mesh=mesh,
        in_specs=(
            rows, P(), by_col, by_col, by_col, by_col, P("tp"), P("tp"), by_row, P(), by_col, by_col, by_row, P(), rows,
        ),
        out_specs=(
            rows, rows, P(), by_col, by_col, by_col, by_col, P("tp"), P("tp"), by_row, P(), by_col, by_col, by_row,
        ),
        check_vma=False,
    )
```
